256 devices in a mesh: tm: 16 (over z, core), row: 16 (over y, x).
Axes of the slice: x: 4, y: 4, z: 8, core: 2. Of those that a mesh axis runs over, the one named last changes fastest.
Arguments:
- element_trans: float32 [16, 512, 512], P('tm', 'row'), may hold values from -1.5 to 1.5
- element_mean: float32 [16, 512], P('tm', 'row'), may hold values from -4 to 4
- element_cov: float32 [16, 512, 512], P('tm', 'row'), may hold values from -2 to 6, as said below
- element_info: float32 [16, 512, 512], P('tm', 'row'), may hold values from -2 to 4, as said below
- element_pull: float32 [16, 512], P('tm', 'row'), may hold values from -4 to 4
- dynamics: float32 [16, 512, 512], P('tm'), may hold values from -0.25 to 0.25
- process_noise: float32 [16, 512, 512], P('tm'), may hold values from -2 to 4, as said below
Outputs:
- smoothed_mean: float32 [16, 512], P('tm', 'row')
- filtered_mean: float32 [16, 512], P('tm', 'row')
- filtered_covariance: float32 [16, 512, 512], P('tm', 'row')
The draws below stay inside these ranges and needn't reach their ends.
Inputs may be any that keep to these rules, and one draw needn't show every extreme that they name: `element_cov`: every step's matrix is symmetric positive definite. `element_info`: every step's matrix is symmetric positive semidefinite. `process_noise`: every step's matrix is symmetric positive definite.
All inputs are finite; a program needn't handle non-finite values.
Results may differ from the reference program's by a relative error of at most 0.0003.
Values sent between devices are 32-bit elements; how exact they have to be, the bound alone decides.
A program may use at most 128 MiB of HBM per device.

```python
import math
import jax
import jax.numpy as jnp
from jax import lax

OCEAN_VARIABLES = 512
EPOCH_COUNT = 16


def rough_normal(key, shape):
    return jax.random.normal(key, shape, jnp.float32)


def spd_stack(key, floor_value, spread_value):
    sampler_seeds = jax.random.split(key, 2)
    factor_rows = rough_normal(sampler_seeds[0], (EPOCH_COUNT, OCEAN_VARIABLES, OCEAN_VARIABLES))
    scales = jnp.exp(jax.random.uniform(sampler_seeds[1], (EPOCH_COUNT, OCEAN_VARIABLES), jnp.float32, math.log(0.7), math.log(1.4)))
    gram = jnp.einsum('tik,tjk->tij', factor_rows, factor_rows) * (spread_value / OCEAN_VARIABLES)
    based = gram + floor_value * jnp.eye(OCEAN_VARIABLES, dtype=jnp.float32)
    return based * scales[:, :, None] * scales[:, None, :]


def draw_element_cov(key, part):
    return spd_stack(jax.random.fold_in(key, 21), 0.3, 0.5)


def draw_element_info(key, part):
    return spd_stack(jax.random.fold_in(key, 22), 0.0, 0.3)


def draw_process_noise(key, part):
    return spd_stack(jax.random.fold_in(key, 23), 0.2, 0.25)


def draw_element_trans(key, part):
    sampler_seeds = jax.random.split(jax.random.fold_in(key, 31), 4)
    modes_basis = jax.random.orthogonal(sampler_seeds[0], OCEAN_VARIABLES)
    decay_coefficient = jnp.exp(jax.random.uniform(sampler_seeds[1], (EPOCH_COUNT, OCEAN_VARIABLES), jnp.float32, math.log(0.01), math.log(0.6)))
    shock_amplitude = jax.random.uniform(sampler_seeds[2], (EPOCH_COUNT, OCEAN_VARIABLES), jnp.float32) < 0.05
    persistence_coefficient = jnp.where(shock_amplitude, 0.6, 1.0 - decay_coefficient)
    noise_part = rough_normal(sampler_seeds[3], (EPOCH_COUNT, OCEAN_VARIABLES, OCEAN_VARIABLES)) * (0.03 / math.sqrt(OCEAN_VARIABLES))
    return jnp.einsum('ik,tk,jk->tij', modes_basis, persistence_coefficient, modes_basis) + noise_part


def level_of(own_key, shape, pieces, smallest, top_value):
    def one(dim, shards_of):
        steps = jax.random.uniform(jax.random.fold_in(jax.random.fold_in(own_key, 6), dim), (shards_of,), jnp.float32, smallest / len(pieces), top_value / len(pieces))
        return jnp.repeat(jnp.exp(steps), shape[dim] // shards_of).reshape((-1,) + (1,) * (len(shape) - dim - 1))

    loudness = one(*pieces[0])
    for cut in pieces[1:]:
        loudness = loudness * one(*cut)
    return loudness


def noise(key, shape, spread, reach, shards=(), held_as=jnp.bfloat16):
    loudness = level_of(key, shape, shards, -0.22, 0.18) if shards else 1.0
    array = jax.random.normal(key, shape, jnp.float32) * spread * loudness
    return jnp.minimum(jnp.maximum(array, -reach), reach).astype(held_as)


def setup_inputs(seed: int = 0) -> dict:
    keys = jax.random.split(jax.random.key(seed), 8)
    element_trans = draw_element_trans(jax.random.fold_in(keys[7], 71), 0)
    element_mean = noise(keys[1], (EPOCH_COUNT, OCEAN_VARIABLES), 0.5, 4.0, ((0, 16), (1, 16)), jnp.float32)
    element_cov = draw_element_cov(jax.random.fold_in(keys[7], 71), 0)
    element_info = draw_element_info(jax.random.fold_in(keys[7], 71), 0)
    element_pull = noise(keys[4], (EPOCH_COUNT, OCEAN_VARIABLES), 0.5, 4.0, ((0, 16), (1, 16)), jnp.float32)
    dynamics = noise(keys[5], (EPOCH_COUNT, OCEAN_VARIABLES, OCEAN_VARIABLES), OCEAN_VARIABLES ** -0.5, 0.25, ((0, 16),), jnp.float32)
    process_noise = draw_process_noise(jax.random.fold_in(keys[7], 71), 0)
    return {"element_trans": element_trans, "element_mean": element_mean, "element_cov": element_cov, "element_info": element_info, "element_pull": element_pull, "dynamics": dynamics, "process_noise": process_noise}


HIGHEST = lax.Precision.HIGHEST

def multiply_arrays(lhs_mat, rhs_mat):
    return jnp.dot(lhs_mat.astype(jnp.float32), rhs_mat.astype(jnp.float32), precision=HIGHEST, preferred_element_type=jnp.float32)

def spd_solve(lower_factor, rhs_mat):
    middle = lax.linalg.triangular_solve(lower_factor, rhs_mat, left_side=True, lower=True)
    return lax.linalg.triangular_solve(lower_factor, middle, left_side=True, lower=True, transpose_a=True)

def reference(element_trans, element_mean, element_cov, element_info, element_pull, dynamics, process_noise):

    def forward(carried, inputs):
        mean_now, cov_now = carried
        trans_next, mean_next, cov_next, info_next, pull_next = inputs
        stacked = cov_now + multiply_arrays(multiply_arrays(cov_now, info_next), cov_now)
        factor = jnp.linalg.cholesky(stacked)
        leading = multiply_arrays(trans_next, cov_now)
        weighted = multiply_arrays(spd_solve(factor, leading.T).T, cov_now)
        passed = trans_next - multiply_arrays(weighted, info_next)
        mean_new = multiply_arrays(passed, mean_now) + multiply_arrays(weighted, pull_next) + mean_next
        cov_new = multiply_arrays(weighted, trans_next.T) + cov_next
        return ((mean_new, cov_new), (mean_new, cov_new))
    initial = (element_mean[0], element_cov[0])
    _, (means_rest, covs_rest) = lax.scan(forward, initial, (element_trans[1:], element_mean[1:], element_cov[1:], element_info[1:], element_pull[1:]))
    filtered_mean = jnp.concatenate([element_mean[:1], means_rest], axis=0)
    filtered_covariance = jnp.concatenate([element_cov[:1], covs_rest], axis=0)

    def gain_step(inputs):
        propagate_dynamics_once, noise_step, cov_now, mean_now = inputs
        projected = multiply_arrays(propagate_dynamics_once, cov_now)
        innovation = multiply_arrays(projected, propagate_dynamics_once.T) + noise_step
        factor = jnp.linalg.cholesky(innovation)
        gain_mat = spd_solve(factor, projected).T
        offset = mean_now - multiply_arrays(gain_mat, multiply_arrays(propagate_dynamics_once, mean_now))
        return (gain_mat, offset)
    gain_all, offset_all = lax.map(gain_step, (dynamics, process_noise, filtered_covariance, filtered_mean))
    last_index = gain_all.shape[0] - 1

    def backward(carried, inputs):
        gain_mat, offset = inputs
        smoothed_now = multiply_arrays(gain_mat, carried) + offset
        return (smoothed_now, smoothed_now)
    _, smoothed_rest = lax.scan(backward, filtered_mean[last_index], (gain_all[:last_index], offset_all[:last_index]), reverse=True)
    smoothed_mean = jnp.concatenate([smoothed_rest, filtered_mean[last_index:]], axis=0)
    return (smoothed_mean, filtered_mean, filtered_covariance)
```

```python
import functools

import jax
import jax.numpy as jnp
from jax import lax
from jax.experimental import pallas as pl
from jax.experimental.pallas import tpu as pltpu
from jax.sharding import PartitionSpec as P

MESH = pl.DeviceIdType.MESH
F32, BF16 = jnp.float32, jnp.bfloat16
NN = (((1,), (0,)), ((), ()))
NT = (((1,), (1,)), ((), ()))
TN = (((0,), (0,)), ((), ()))
VROWS = 16
VMEM_LIMIT = 56 * 1024 * 1024


def places():
    time_pos, row_pos = lax.axis_index("tm"), lax.axis_index("row")
    return time_pos // 2, time_pos % 2, row_pos // 4, row_pos % 4


def dot(lhs, rhs, dims=NN):
    return lax.dot_general(lhs, rhs, dims, preferred_element_type=F32)


def put(pair, value, start=0):
    high = value.astype(BF16)
    rows = pl.ds(start, value.shape[0])
    pair[0][rows, :] = high
    pair[1][rows, :] = (value - high.astype(F32)).astype(BF16)


def times(lhs, rhs, dims=NN, rows=None):
    lhs_high, lhs_low = (p[...] if rows is None else p[:rows, :] for p in lhs)
    rhs_high, rhs_low = (p[: p.shape[1], :] for p in rhs)
    return dot(lhs_high, rhs_high, dims) + dot(lhs_high, rhs_low, dims) + dot(lhs_low, rhs_high, dims)


def eye(size):
    rows = lax.broadcasted_iota(jnp.int32, (size, size), 0)
    return (rows == lax.broadcasted_iota(jnp.int32, (size, size), 1)).astype(F32)


def invert(matrix, upper, lower, out, mat, work, value, coarse):
    size = matrix.shape[0]
    put(mat, matrix)
    first = 2.0 / (upper + lower)
    bound = (upper - lower) / (upper + lower)
    scale = 2.0 / (2.0 - bound * bound)
    start = (scale * first) * (2.0 * eye(size) - first * matrix)
    value[...] = start
    put(out, start)
    bound = bound * bound / (2.0 - bound * bound)

    def scaled(bound):
        scale = 2.0 / (2.0 - bound * bound)
        if coarse:
            residual = eye(size) - dot(mat[0][...], out[0][...])
            work[0][:size, :] = residual.astype(BF16)
            new = scale * (value[...] + dot(out[0][...], work[0][:size, :]))
        else:
            residual = eye(size) - times(mat, out)
            put(work, residual)
            new = scale * (value[...] + times(out, work))
        value[...] = new
        put(out, new)
        return bound * bound / (2.0 - bound * bound)

    lax.while_loop(lambda b: b > 0.008, scaled, bound)

    def plain(carry):
        count, _ = carry
        residual = eye(size) - times(mat, out)
        put(work, residual)
        error = jnp.sum(residual * residual)
        new = value[...] + times(out, work)
        value[...] = new
        put(out, new)
        return count + 1, error

    lax.while_loop(lambda c: (c[0] < 48) & (c[1] > 1e-4), plain, (jnp.int32(0), jnp.float32(1.0)))


def one_norm(matrix):
    return jnp.max(jnp.sum(jnp.abs(matrix), axis=0, keepdims=True))


def spread(row):
    return jnp.broadcast_to(row, (VROWS, row.shape[1]))


def combine(own, own_vec, prior, prior_vec, new, new_vec, pairs, value, closing):
    size = value.shape[0]
    one, two, three, four, five, six = pairs
    put(one, own[2])
    put(one, own_vec[...], size)
    put(two, prior[0])
    product = times(one, two)
    coupling = product[:size]
    shifted = prior_vec[0:1, :] + product[size + 1 : size + 2]
    upper = 2.0 + one_norm(coupling)
    invert(eye(size) + coupling, upper, 1.0, three, four, five, value, True)
    put(four, own[1])
    put(five, times(two, three), 0)
    put(six, times(five, four, rows=size))
    if closing:
        put(five, spread(shifted), 0)
        put(one, times(five, three, rows=VROWS), 0)
        mean = times(one, four, rows=VROWS)
        new_vec[0:1, :] = mean[0:1] + own_vec[0:1, :]
        new[0] = times(four, six, TN) + own[0]
        return
    new[0] = times(four, six, TN) + own[0]
    put(five, prior[1])
    put(five, spread(shifted), size)
    gained = times(five, three)
    put(two, gained[:size])
    put(six, gained[:size])
    put(six, gained[size:], size)
    moved = times(six, four)
    new[1] = moved[:size]
    put(three, own[2])
    put(five, prior_vec[...], size)
    pulled = times(five, three)
    put(six, pulled[:size])
    put(six, spread(own_vec[1:2, :] - pulled[size : size + 1]), size)
    informed = times(six, two, NT)
    new[2] = informed[:size] + prior[2]
    new_vec[0:1, :] = moved[size : size + 1] + own_vec[0:1, :]
    new_vec[1:2, :] = informed[size : size + 1] + prior_vec[1:2, :]


def scratch_pairs(size, count, tall):
    shapes = []
    for index in range(count):
        rows = size + VROWS if index in tall else size
        shapes += [pltpu.VMEM((rows, size), BF16)] * 2
    return shapes


def paired(refs):
    return [(refs[i], refs[i + 1]) for i in range(0, len(refs), 2)]


TALL = (0, 4, 5)


def unpack(slabs, mats, vecs):
    size = mats.shape[1]
    count = slabs.shape[0]
    piece = size // count
    total = slabs[0, 3 * piece :, :]
    for index in range(count):
        rows = pl.ds(index * piece, piece)
        mats[1, rows, :] = slabs[index, :piece, :]
        mats[0, rows, :] = slabs[index, piece : 2 * piece, :]
        mats[2, rows, :] = slabs[index, 2 * piece : 3 * piece, :]
        if index:
            total = total + slabs[index, 3 * piece :, :]
    mats[1] = mats[1].T
    vecs[...] = jnp.zeros_like(vecs)
    vecs[0:8, :] = total


def first_kernel(own_slabs, prior_slabs, new, new_vec, own, own_vec, prior, prior_vec, value, *pairs):
    odd = lax.axis_index("tm") % 2 == 1

    @pl.when(odd)
    def _():
        unpack(own_slabs, own, own_vec)
        unpack(prior_slabs, prior, prior_vec)
        new_vec[...] = jnp.zeros_like(new_vec)
        combine(own, own_vec, prior, prior_vec, new, new_vec, paired(pairs), value, False)

    @pl.when(jnp.logical_not(odd))
    def _():
        unpack(own_slabs, new, new_vec)


def level_kernel(own, own_vec, prior, prior_vec, new, new_vec, value, *pairs, distance):
    present = (lax.axis_index("tm") // distance) % 2 == 1

    @pl.when(present)
    def _():
        new_vec[...] = jnp.zeros_like(new_vec)
        combine(own, own_vec, prior, prior_vec, new, new_vec, paired(pairs), value, False)

    @pl.when(jnp.logical_not(present))
    def _():
        new[...] = own[...]
        new_vec[...] = own_vec[...]


def gain_kernel(
    own, own_vec, prior, prior_vec, dynamics, noise, gain, offset, cov_out, mean_out, new, value, *pairs, distance
):
    size = value.shape[0]
    time_pos, row_pos = lax.axis_index("tm"), lax.axis_index("row")
    present = (time_pos // distance) % 2 == 1
    pairs = paired(pairs)
    one, two, three, four, five, six = pairs

    @pl.when(present)
    def _():
        combine(own, own_vec, prior, prior_vec, new, mean_out, pairs, value, True)

    @pl.when(jnp.logical_not(present))
    def _():
        new[0] = own[0]
        mean_out[0:1, :] = own_vec[0:1, :]

    piece = cov_out.shape[0]
    cov_out[...] = new[0, pl.ds(pl.multiple_of(row_pos * piece, piece), piece), :]
    mean = mean_out[0:1, :]

    @pl.when(time_pos == 15)
    def _():
        gain[...] = jnp.zeros_like(gain)
        offset[...] = spread(mean)

    @pl.when(time_pos < 15)
    def _():
        put(two, dynamics[...])
        put(three, new[0])
        put(one, times(two, three))
        put(one, spread(mean), size)
        product = times(one, two, NT)
        innovation = product[:size] + noise[...]
        predicted = product[size:]
        upper = one_norm(innovation)
        invert(innovation, upper, upper * 0.001, three, four, two, value, False)
        put(five, predicted, size)
        weights = times(three, one)
        gain[...] = weights
        put(six, weights)
        high, low = five[0][size:, :], five[1][size:, :]
        moved = (
            dot(high, six[0][0:size, :]) + dot(low, six[0][0:size, :]) + dot(high, six[1][0:size, :])
        )
        offset[...] = spread(mean) - moved


def remote(src, dst, send, recv, tm, row):
    return pltpu.make_async_remote_copy(
        src_ref=src, dst_ref=dst, send_sem=send, recv_sem=recv, device_id=(tm, row), device_id_type=MESH
    )


def greet(barrier, tm, row):
    pl.semaphore_signal(barrier, inc=1, device_id=(tm, row), device_id_type=MESH)


def gather_kernel(trans, cov, info, vecs, own, prior, send, recv, far_send, far_recv):
    z, core, y, x = places()
    time_pos, row_pos = lax.axis_index("tm"), lax.axis_index("row")
    piece = trans.shape[0]
    keep = (time_pos > 0).astype(F32)
    barrier = pltpu.get_barrier_semaphore()
    across = [(y * 4 + (x + k) % 4) for k in (1, 2, 3)]
    along = [((y + k) % 4) * 4 + x for k in (1, 2, 3)]
    for peer in across + along:
        greet(barrier, time_pos, peer)

    @pl.when(core == 1)
    def _():
        greet(barrier, time_pos - 1, row_pos)

    own[y, x, :piece, :] = trans[...] * keep
    own[y, x, piece : 2 * piece, :] = cov[...]
    own[y, x, 2 * piece : 3 * piece, :] = info[...] * keep
    kept_rows = jnp.where(lax.broadcasted_iota(jnp.int32, vecs.shape, 0) == 0, 1.0, keep)
    own[y, x, 3 * piece :, :] = vecs[...] * kept_rows

    def gather(near, other, line):
        copies = []
        for k in range(3):
            copy = remote(own.at[y, x], own.at[y, x], send.at[k], recv.at[k], time_pos, near[k])
            copy.start()
            copies.append(copy)
        for copy in copies:
            copy.wait()
        later = []
        for k in range(3):
            copy = remote(line(0), line(0), send.at[3 + k], recv.at[3 + k], time_pos, other[k])
            copy.start()
            later.append(copy)
        return later

    @pl.when(core == 0)
    def _():
        pl.semaphore_wait(barrier, 7)
        later = gather(across, along, lambda k: own.at[y])
        passed = []
        for k in range(4):
            if k:
                later[k - 1].wait_recv()
            line = (y + 4 - k) % 4
            copy = remote(own.at[line], prior.at[line], far_send.at[k], far_recv.at[k], time_pos + 1, row_pos)
            copy.start()
            passed.append(copy)
        for copy in later + passed:
            copy.wait_send()

    @pl.when(core == 1)
    def _():
        pl.semaphore_wait(barrier, 6)
        later = gather(along, across, lambda k: own.at[:, x])
        for copy in later:
            copy.wait()
        for k in range(4):
            line = (y + 4 - k) % 4
            remote(own.at[line], prior.at[line], far_send.at[k], far_recv.at[k], time_pos, row_pos).wait_recv()


def pass_kernel(mats, vecs, got, got_vec, send, recv, vec_send, vec_recv, *, distance):
    z, core, y, x = places()
    time_pos, row_pos = lax.axis_index("tm"), lax.axis_index("row")
    reach = distance // 2
    rows = got.shape[0] // 32
    barrier = pltpu.get_barrier_semaphore()
    target = (z // reach) % 2 == 1
    source = ((z // reach) % 2 == 0) & (z % reach == reach - 1) & (core == 1)
    source_pos = ((z // reach) * reach) * 2 - 1
    inner = (1 - core) * x + core * y
    outer = (1 - core) * y + core * x

    def row_of(a, b):
        return (1 - core) * (b * 4 + a) + core * (a * 4 + b)

    def piece(index, count=1):
        return pl.ds(pl.multiple_of(index * rows, rows), count * rows)

    near = [row_of((inner + k) % 4, outer) for k in (1, 2, 3)]
    other = [row_of(inner, (outer + k) % 4) for k in (1, 2, 3)]

    @pl.when(source)
    def _():
        pl.semaphore_wait(barrier, 2 * reach)
        copies = []
        for step in range(reach):
            for side in range(2):
                there = time_pos + 1 + 2 * step + side
                slot = 2 * step + side
                index = side * 16 + (y * 4 + x if side == 0 else x * 4 + y)
                copy = remote(mats.at[piece(index)], got.at[piece(index)], send.at[slot], recv.at[0], there, row_pos)
                copy.start()
                small = remote(vecs, got_vec, vec_send.at[slot], vec_recv, there, row_pos)
                small.start()
                copies += [copy, small]
        for copy in copies:
            copy.wait_send()

    @pl.when(target)
    def _():
        twin = 2 * z + 1 - core
        greet(barrier, source_pos, row_pos)
        for peer in near + other:
            greet(barrier, time_pos, peer)
        greet(barrier, twin, row_pos)
        pl.semaphore_wait(barrier, 7)
        mine = core * 16 + outer * 4 + inner
        remote(got.at[piece(mine)], got.at[piece(mine)], send.at[0], recv.at[0], time_pos, row_pos).wait_recv()
        copies = []
        for k in range(3):
            copy = remote(got.at[piece(mine)], got.at[piece(mine)], send.at[k], recv.at[1 + k], time_pos, near[k])
            copy.start()
            copies.append(copy)
        for copy in copies:
            copy.wait_recv()
        later = []
        line = piece(core * 16 + outer * 4, 4)
        for k in range(3):
            copy = remote(got.at[line], got.at[line], send.at[3 + k], recv.at[4 + k], time_pos, other[k])
            copy.start()
            later.append(copy)
        passed = []
        for k in range(4):
            if k:
                later[k - 1].wait_recv()
            line = piece(core * 16 + ((outer + 4 - k) % 4) * 4, 4)
            copy = remote(got.at[line], got.at[line], send.at[6 + k], recv.at[7 + k], twin, row_pos)
            copy.start()
            passed.append(copy)
        for copy in passed:
            copy.wait_recv()
        remote(got_vec, got_vec, vec_send.at[0], vec_recv, time_pos, row_pos).wait_recv()
        for copy in copies + later + passed:
            copy.wait_send()


def chain_kernel(gain, offset, smooth, near_gain, near_offset, held, sent, state, *rest):
    pairs, (send, recv) = paired(rest[:-2]), rest[-2:]
    one, two = pairs
    z, core, _, _ = places()
    time_pos, row_pos = lax.axis_index("tm"), lax.axis_index("row")
    size = gain.shape[0]
    barrier = pltpu.get_barrier_semaphore()
    first, last = core == 0, z == 7

    @pl.when(first)
    def _():
        greet(barrier, time_pos + 1, row_pos)

    @pl.when(jnp.logical_not(last))
    def _():
        greet(barrier, 2 * z + 2, row_pos)

    put(two, gain[...])
    link = remote(gain, near_gain, send.at[0], recv.at[0], 2 * z, row_pos)
    small = remote(offset, near_offset, send.at[1], recv.at[1], 2 * z, row_pos)

    @pl.when(core == 1)
    def _():
        pl.semaphore_wait(barrier, 1)
        link.start()
        small.start()
        state[...] = offset[0:8, :]

    @pl.when(first & (z > 0))
    def _():
        pl.semaphore_wait(barrier, 2)

    @pl.when(first)
    def _():
        link.wait_recv()
        small.wait_recv()
        put(one, near_gain[...])
        put(one, near_offset[...], size)
        product = times(one, two)
        put(two, product[:size])
        state[...] = product[size : size + 8] + offset[0:8, :]

    @pl.when(jnp.logical_not(last))
    def _():
        remote(held, held, send.at[2], recv.at[2], time_pos, row_pos).wait_recv()
        value = held[...]
        high = value.astype(BF16).astype(F32)
        both = jnp.concatenate([high, value - high], axis=0).astype(BF16)
        result = dot(both, two[0][...])
        result = result[:8] + result[8:] + dot(both, two[1][...])[:8]
        state[...] = state[...] + result

    @pl.when(first & (z > 0))
    def _():
        sent[...] = state[...]
        copies = [remote(sent, held, send.at[2 + k], recv.at[2], 2 * z - 2 + k, row_pos) for k in range(2)]
        for copy in copies:
            copy.start()
        for copy in copies:
            copy.wait_send()

    smooth[...] = state[...]

    @pl.when(core == 1)
    def _():
        link.wait_send()
        small.wait_send()


def body(trans, mean, cov, info, pull, dynamics, noise):
    row_pos = lax.axis_index("row")
    piece, size = trans.shape[1:]
    row_start = row_pos * piece
    shape = jax.ShapeDtypeStruct
    vmem = pl.BlockSpec(memory_space=pltpu.VMEM)
    dma = pltpu.SemaphoreType.DMA

    def params(**more):
        return pltpu.CompilerParams(vmem_limit_bytes=VMEM_LIMIT, **more)

    lines = jnp.concatenate([mean, pull, jnp.zeros((6, piece), F32)], axis=0)
    placed = lax.dynamic_update_slice(jnp.zeros((8, size), F32), lines, (0, row_start))
    slab = shape((4, 4, 3 * piece + 8, size), F32)
    own_slabs, prior_slabs = pl.pallas_call(
        gather_kernel,
        out_shape=(slab, slab),
        in_specs=[vmem] * 4,
        out_specs=(vmem, vmem),
        scratch_shapes=[dma((6,)), dma((6,)), dma((4,)), dma((4,))],
        compiler_params=params(collective_id=0, has_side_effects=True),
    )(trans[0], cov[0], info[0], placed)

    mats_shape, vecs_shape = shape((3, size, size), F32), shape((VROWS, size), F32)
    held = [pltpu.VMEM((3, size, size), F32), pltpu.VMEM((VROWS, size), F32)]
    flat = (16, 3 * piece + 8, size)
    mats, vecs = pl.pallas_call(
        first_kernel,
        out_shape=(mats_shape, vecs_shape),
        in_specs=[vmem] * 2,
        out_specs=(vmem, vmem),
        scratch_shapes=held * 2 + [pltpu.VMEM((size, size), F32)] + scratch_pairs(size, 6, TALL),
        compiler_params=params(),
    )(own_slabs.reshape(flat), prior_slabs.reshape(flat))

    def passed(mats, vecs, distance, count):
        return pl.pallas_call(
            functools.partial(pass_kernel, distance=distance),
            out_shape=(shape((count * size, size), F32), vecs_shape),
            in_specs=[pl.BlockSpec(memory_space=pl.ANY)] * 2,
            out_specs=(vmem, vmem),
            scratch_shapes=[dma((10,)), dma((11,)), dma((8,)), dma],
            compiler_params=params(collective_id=distance, has_side_effects=True),
        )(mats.reshape(3 * size, size), vecs)

    for distance in (2, 4):
        got, got_vec = passed(mats, vecs, distance, 3)
        mats, vecs = pl.pallas_call(
            functools.partial(level_kernel, distance=distance),
            out_shape=(mats_shape, vecs_shape),
            in_specs=[vmem] * 4,
            out_specs=(vmem, vmem),
            scratch_shapes=[pltpu.VMEM((size, size), F32)] + scratch_pairs(size, 6, TALL),
            compiler_params=params(),
        )(mats, vecs, got.reshape(3, size, size), got_vec)

    got, got_vec = passed(mats, vecs, 8, 1)
    gain, offset, cov_out, mean_out = pl.pallas_call(
        functools.partial(gain_kernel, distance=8),
        out_shape=(
            shape((size, size), F32),
            vecs_shape,
            shape((piece, size), F32),
            shape((8, size), F32),
        ),
        in_specs=[vmem] * 6,
        out_specs=(vmem,) * 4,
        scratch_shapes=[pltpu.VMEM((1, size, size), F32), pltpu.VMEM((size, size), F32)]
        + scratch_pairs(size, 6, TALL),
        compiler_params=params(),
    )(mats, vecs, got.reshape(1, size, size), got_vec, dynamics[0], noise[0])

    smooth = pl.pallas_call(
        chain_kernel,
        out_shape=shape((8, size), F32),
        in_specs=[vmem] * 2,
        out_specs=vmem,
        scratch_shapes=[
            pltpu.VMEM((size, size), F32),
            pltpu.VMEM((VROWS, size), F32),
            pltpu.VMEM((8, size), F32),
            pltpu.VMEM((8, size), F32),
            pltpu.VMEM((8, size), F32),
        ]
        + scratch_pairs(size, 2, (0,))
        + [dma((4,)), dma((3,))],
        compiler_params=params(collective_id=1, has_side_effects=True),
    )(gain, offset)

    return (
        lax.dynamic_slice(smooth, (0, row_start), (1, piece)),
        lax.dynamic_slice(mean_out, (0, row_start), (1, piece)),
        cov_out[None],
    )


def solution(mesh):
    in_specs = (
        P("tm", "row", None),
        P("tm", "row"),
        P("tm", "row", None),
        P("tm", "row", None),
        P("tm", "row"),
        P("tm", None, None),
        P("tm", None, None),
    )
    out_specs = (P("tm", "row"), P("tm", "row"), P("tm", "row", None))
    return jax.shard_map(body, mesh=mesh, in_specs=in_specs, out_specs=out_specs, check_vma=False)
```

```python
import functools

import jax
import jax.numpy as jnp
from jax import lax
from jax.experimental import pallas as pl
from jax.experimental.pallas import tpu as pltpu
from jax.sharding import PartitionSpec as P

MESH = pl.DeviceIdType.MESH
F32, BF16 = jnp.float32, jnp.bfloat16
NN = (((1,), (0,)), ((), ()))
NT = (((1,), (1,)), ((), ()))
TN = (((0,), (0,)), ((), ()))
VROWS = 16
REACH = 0.008
VMEM_LIMIT = 56 * 1024 * 1024


def places():
    time_pos, row_pos = lax.axis_index("tm"), lax.axis_index("row")
    return time_pos // 2, time_pos % 2, row_pos // 4, row_pos % 4


def dot(lhs, rhs, dims=NN):
    return lax.dot_general(lhs, rhs, dims, preferred_element_type=F32)


def put(pair, value, start=0):
    high = value.astype(BF16)
    rows = pl.ds(start, value.shape[0])
    pair[0][rows, :] = high
    pair[1][rows, :] = (value - high.astype(F32)).astype(BF16)


def put_high(pair, value):
    pair[0][: value.shape[0], :] = value.astype(BF16)


def times(lhs, rhs, dims=NN, rows=None):
    lhs_high, lhs_low = (p[...] if rows is None else p[:rows, :] for p in lhs)
    rhs_high, rhs_low = (p[: p.shape[1], :] for p in rhs)
    return dot(lhs_high, rhs_high, dims) + dot(lhs_high, rhs_low, dims) + dot(lhs_low, rhs_high, dims)


def eye(size):
    rows = lax.broadcasted_iota(jnp.int32, (size, size), 0)
    return (rows == lax.broadcasted_iota(jnp.int32, (size, size), 1)).astype(F32)


def invert(matrix, upper, lower, out, mat, work, value):
    size = matrix.shape[0]
    put(mat, matrix)
    first = 2.0 / (upper + lower)
    bound = (upper - lower) / (upper + lower)

    def scale_of(bound):
        return 2.0 / (2.0 - bound * bound)

    def approach(coarse):
        def scaled(bound):
            if coarse:
                put_high(work, eye(size) - dot(mat[0][...], out[0][...]))
                new = scale_of(bound) * (value[...] + dot(out[0][...], work[0][:size, :]))
            else:
                put(work, eye(size) - times(mat, out))
                new = scale_of(bound) * (value[...] + times(out, work))
            value[...] = new
            put(out, new)
            return bound * bound * 0.5 * scale_of(bound)

        start = (scale_of(bound) * first) * (2.0 * eye(size) - first * matrix_of())
        value[...] = start
        put(out, start)
        lax.while_loop(lambda b: b > REACH, scaled, bound * bound * 0.5 * scale_of(bound))

    def matrix_of():
        return mat[0][...].astype(F32) + mat[1][...].astype(F32)

    def check():
        residual = eye(size) - times(mat, out)
        put_high(work, residual)
        return jnp.sum(residual * residual)

    def step():
        new = value[...] + dot(out[0][...], work[0][:size, :])
        value[...] = new
        put(out, new)

    def again(carry):
        count, error = carry
        step()
        return count + 1, check()

    def whole(error):
        approach(False)
        return check()

    approach(True)
    error = check()
    error = lax.cond(error < 1.0, lambda e: e, whole, error)
    lax.while_loop(lambda c: (c[0] < 48) & (c[1] > 1e-4), again, (jnp.int32(0), error))
    step()


def one_norm(matrix):
    return jnp.max(jnp.sum(jnp.abs(matrix), axis=0, keepdims=True))


def spread(row):
    return jnp.broadcast_to(row, (VROWS, row.shape[1]))


def combine(own, own_vec, prior, prior_vec, new, new_vec, pairs, value, closing):
    size = value.shape[0]
    one, two, three, four, five, six = pairs
    put(one, own[2])
    put(one, own_vec[...], size)
    put(two, prior[0])
    product = times(one, two)
    coupling = product[:size]
    shifted = prior_vec[0:1, :] + product[size + 1 : size + 2]
    upper = 2.0 + one_norm(coupling)
    invert(eye(size) + coupling, upper, 1.0, three, four, five, value)
    put(four, own[1])
    put(five, times(two, three), 0)
    put(six, times(five, four, rows=size))
    if closing:
        put(five, spread(shifted), 0)
        put(one, times(five, three, rows=VROWS), 0)
        mean = times(one, four, rows=VROWS)
        new_vec[0:1, :] = mean[0:1] + own_vec[0:1, :]
        new[0] = times(four, six, TN) + own[0]
        return
    new[0] = times(four, six, TN) + own[0]
    put(five, prior[1])
    put(five, spread(shifted), size)
    gained = times(five, three)
    put(two, gained[:size])
    put(six, gained[:size])
    put(six, gained[size:], size)
    moved = times(six, four)
    new[1] = moved[:size]
    put(three, own[2])
    put(five, spread(prior_vec[0:1, :]), size)
    pulled = times(five, three)
    put(six, pulled[:size])
    put(six, spread(own_vec[1:2, :] - pulled[size : size + 1]), size)
    informed = times(six, two, NT)
    new[2] = informed[:size] + prior[2]
    new_vec[0:1, :] = moved[size : size + 1] + own_vec[0:1, :]
    new_vec[1:2, :] = informed[size : size + 1] + prior_vec[1:2, :]


def scratch_pairs(size, count, tall):
    shapes = []
    for index in range(count):
        rows = size + VROWS if index in tall else size
        shapes += [pltpu.VMEM((rows, size), BF16)] * 2
    return shapes


def paired(refs):
    return [(refs[i], refs[i + 1]) for i in range(0, len(refs), 2)]


TALL = (0, 4, 5)


def unpack(slabs, mats, vecs):
    size = mats.shape[1]
    count = slabs.shape[0]
    piece = size // count
    total = slabs[0, 3 * piece :, :]
    for index in range(count):
        rows = pl.ds(index * piece, piece)
        mats[1, rows, :] = slabs[index, :piece, :]
        mats[0, rows, :] = slabs[index, piece : 2 * piece, :]
        mats[2, rows, :] = slabs[index, 2 * piece : 3 * piece, :]
        if index:
            total = total + slabs[index, 3 * piece :, :]
    mats[1] = mats[1].T
    vecs[...] = jnp.zeros_like(vecs)
    vecs[0:8, :] = total


def first_kernel(own_slabs, prior_slabs, new, new_vec, own, own_vec, prior, prior_vec, value, *pairs):
    odd = lax.axis_index("tm") % 2 == 1

    @pl.when(odd)
    def _():
        unpack(own_slabs, own, own_vec)
        unpack(prior_slabs, prior, prior_vec)
        new_vec[...] = jnp.zeros_like(new_vec)
        combine(own, own_vec, prior, prior_vec, new, new_vec, paired(pairs), value, False)

    @pl.when(jnp.logical_not(odd))
    def _():
        unpack(own_slabs, new, new_vec)


def level_kernel(own, own_vec, prior, prior_vec, new, new_vec, value, *pairs, distance):
    present = (lax.axis_index("tm") // distance) % 2 == 1

    @pl.when(present)
    def _():
        new_vec[...] = jnp.zeros_like(new_vec)
        combine(own, own_vec, prior, prior_vec, new, new_vec, paired(pairs), value, False)

    @pl.when(jnp.logical_not(present))
    def _():
        new[...] = own[...]
        new_vec[...] = own_vec[...]


def gain_kernel(
    own, own_vec, prior, prior_vec, dynamics, noise, gain, offset, cov_out, mean_out, new, value, *pairs, distance
):
    size = value.shape[0]
    time_pos, row_pos = lax.axis_index("tm"), lax.axis_index("row")
    present = (time_pos // distance) % 2 == 1
    pairs = paired(pairs)
    one, two, three, four, five, six = pairs

    @pl.when(present)
    def _():
        combine(own, own_vec, prior, prior_vec, new, mean_out, pairs, value, True)

    @pl.when(jnp.logical_not(present))
    def _():
        new[0] = own[0]
        mean_out[0:1, :] = own_vec[0:1, :]

    piece = cov_out.shape[0]
    cov_out[...] = new[0, pl.ds(pl.multiple_of(row_pos * piece, piece), piece), :]
    mean = mean_out[0:1, :]

    @pl.when(time_pos == 15)
    def _():
        gain[...] = jnp.zeros_like(gain)
        offset[...] = spread(mean)

    @pl.when(time_pos < 15)
    def _():
        put(two, dynamics[...])
        put(three, new[0])
        put(one, times(two, three))
        put(one, spread(mean), size)
        product = times(one, two, NT)
        innovation = product[:size] + noise[...]
        predicted = product[size:]
        upper = one_norm(innovation)
        invert(innovation, upper, upper * 0.004, three, four, two, value)
        put(five, predicted, size)
        weights = times(three, one)
        gain[...] = weights
        put(six, weights)
        high, low = five[0][size:, :], five[1][size:, :]
        moved = (
            dot(high, six[0][0:size, :]) + dot(low, six[0][0:size, :]) + dot(high, six[1][0:size, :])
        )
        offset[...] = spread(mean) - moved


def remote(src, dst, send, recv, tm, row):
    return pltpu.make_async_remote_copy(
        src_ref=src, dst_ref=dst, send_sem=send, recv_sem=recv, device_id=(tm, row), device_id_type=MESH
    )


def greet(barrier, tm, row):
    pl.semaphore_signal(barrier, inc=1, device_id=(tm, row), device_id_type=MESH)


class Ring:
    def __init__(self, block, peer, send, recv, base):
        self.block, self.peer, self.send, self.recv, self.base = block, peer, send, recv, base
        self.copies = []

    def copy(self, view, slot, step):
        slot += self.base
        copy = remote(view, view, self.send.at[slot], self.recv.at[slot], *self.peer(step))
        copy.start()
        self.copies.append(copy)

    def start(self):
        self.copy(self.block(0, None), 0, 1)
        self.copy(self.block(0, None), 1, 3)

    def forward_up(self):
        self.copies[0].wait_recv()
        self.copy(self.block(3, 0), 2, 1)

    def forward_down(self):
        self.copies[1].wait_recv()
        self.copy(self.block(1, 1), 3, 3)

    def finish(self):
        self.copies[2].wait_recv()
        self.copies[3].wait_recv()

    def drain(self):
        for copy in self.copies:
            copy.wait_send()


def gather_kernel(trans, cov, info, vecs, own, prior, send, recv, far_send, far_recv):
    z, core, y, x = places()
    time_pos, row_pos = lax.axis_index("tm"), lax.axis_index("row")
    piece = trans.shape[0]
    half = (3 * piece + 8) // 16 * 8
    keep = (time_pos > 0).astype(F32)
    barrier = pltpu.get_barrier_semaphore()

    def across(k):
        return time_pos, y * 4 + (x + k) % 4

    def along(k):
        return time_pos, ((y + k) % 4) * 4 + x

    for peer in (across(1), across(3), along(1), along(3)):
        greet(barrier, *peer)

    @pl.when(core == 1)
    def _():
        greet(barrier, time_pos - 1, row_pos)

    own[y, x, :piece, :] = trans[...] * keep
    own[y, x, piece : 2 * piece, :] = cov[...]
    own[y, x, 2 * piece : 3 * piece, :] = info[...] * keep
    kept_rows = jnp.where(lax.broadcasted_iota(jnp.int32, vecs.shape, 0) == 0, 1.0, keep)
    own[y, x, 3 * piece :, :] = vecs[...] * kept_rows

    def part(ref, which):
        if which is None:
            return ref
        return ref.at[pl.ds(half, 3 * piece + 8 - half)] if which else ref.at[pl.ds(0, half)]

    @pl.when(core == 0)
    def _():
        pl.semaphore_wait(barrier, 5)
        inner = Ring(lambda k, h: part(own.at[y, (x + k) % 4], h), across, send, recv, 0)
        outer = Ring(
            lambda k, h: own.at[(y + k) % 4] if h is None else own.at[(y + k) % 4, pl.ds(2 * h, 2)],
            along,
            send,
            recv,
            4,
        )
        passed = []

        def over(k):
            line = (y + k) % 4
            copy = remote(own.at[line], prior.at[line], far_send.at[k], far_recv.at[k], time_pos + 1, row_pos)
            copy.start()
            passed.append(copy)

        inner.start()
        inner.forward_up()
        inner.forward_down()
        inner.finish()
        outer.start()
        over(0)
        outer.forward_up()
        over(3)
        outer.forward_down()
        over(1)
        outer.finish()
        over(2)
        inner.drain()
        outer.drain()
        for copy in passed:
            copy.wait_send()

    @pl.when(core == 1)
    def _():
        pl.semaphore_wait(barrier, 4)
        inner = Ring(lambda k, h: part(own.at[(y + k) % 4, x], h), along, send, recv, 0)
        outer = Ring(
            lambda k, h: own.at[:, (x + k) % 4] if h is None else own.at[pl.ds(2 * h, 2), (x + k) % 4],
            across,
            send,
            recv,
            4,
        )
        for ring in (inner, outer):
            ring.start()
            ring.forward_up()
            ring.forward_down()
            ring.finish()
        inner.drain()
        outer.drain()
        for k in range(4):
            line = (y + k) % 4
            remote(own.at[line], prior.at[line], far_send.at[k], far_recv.at[k], time_pos, row_pos).wait_recv()


def pass_kernel(mats, vecs, got, got_vec, send, recv, far_send, far_recv, vec_send, vec_recv, *, distance):
    z, core, y, x = places()
    time_pos, row_pos = lax.axis_index("tm"), lax.axis_index("row")
    reach = distance // 2
    rows = got.shape[0] // 32
    barrier = pltpu.get_barrier_semaphore()
    target = (z // reach) % 2 == 1
    source = ((z // reach) % 2 == 0) & (z % reach == reach - 1) & (core == 1)
    source_pos = ((z // reach) * reach) * 2 - 1
    inner_pos = (1 - core) * x + core * y
    outer_pos = (1 - core) * y + core * x

    def row_of(a, b):
        return (1 - core) * (b * 4 + a) + core * (a * 4 + b)

    def view(start, count):
        return got.at[pl.ds(pl.multiple_of(start, 8), count)]

    def inner_peer(k):
        return time_pos, row_of((inner_pos + k) % 4, outer_pos)

    def outer_peer(k):
        return time_pos, row_of(inner_pos, (outer_pos + k) % 4)

    def inner_block(k, half):
        start = (core * 16 + outer_pos * 4 + (inner_pos + k) % 4) * rows
        return view(start, rows) if half is None else view(start + half * (rows // 2), rows // 2)

    def outer_block(k, half):
        start = (core * 16 + ((outer_pos + k) % 4) * 4) * rows
        return view(start, 4 * rows) if half is None else view(start + half * 2 * rows, 2 * rows)

    @pl.when(source)
    def _():
        pl.semaphore_wait(barrier, 2 * reach)
        copies = []
        for step in range(reach):
            for side in range(2):
                there = time_pos + 1 + 2 * step + side
                slot = 2 * step + side
                index = side * 16 + (y * 4 + x if side == 0 else x * 4 + y)
                slab = pl.ds(pl.multiple_of(index * rows, 8), rows)
                copy = remote(mats.at[slab], got.at[slab], far_send.at[slot], far_recv.at[4], there, row_pos)
                copy.start()
                small = remote(
                    vecs.at[pl.ds(0, 8)], got_vec, vec_send.at[slot], vec_recv, there, row_pos
                )
                small.start()
                copies += [copy, small]
        for copy in copies:
            copy.wait_send()

    @pl.when(target)
    def _():
        twin = 2 * z + 1 - core
        greet(barrier, source_pos, row_pos)
        for k in (1, 3):
            greet(barrier, *inner_peer(k))
            greet(barrier, *outer_peer(k))
        greet(barrier, twin, row_pos)
        pl.semaphore_wait(barrier, 5)
        mine = inner_block(0, None)
        remote(mine, mine, far_send.at[4], far_recv.at[4], time_pos, row_pos).wait_recv()
        inner = Ring(inner_block, inner_peer, send, recv, 0)
        outer = Ring(outer_block, outer_peer, send, recv, 4)
        passed = []

        def over(k):
            line = outer_block(k, None)
            copy = remote(line, line, far_send.at[k], far_recv.at[k], twin, row_pos)
            copy.start()
            passed.append(copy)

        inner.start()
        inner.forward_up()
        inner.forward_down()
        inner.finish()
        outer.start()
        over(0)
        outer.forward_up()
        over(3)
        outer.forward_down()
        over(1)
        outer.finish()
        over(2)
        for copy in passed:
            copy.wait_recv()
        remote(got_vec, got_vec, vec_send.at[0], vec_recv, time_pos, row_pos).wait_recv()
        inner.drain()
        outer.drain()
        for copy in passed:
            copy.wait_send()


def chain_kernel(gain, offset, smooth, near_gain, near_offset, held, sent, state, *rest):
    pairs, (send, recv) = paired(rest[:-2]), rest[-2:]
    one, two = pairs
    z, core, _, _ = places()
    time_pos, row_pos = lax.axis_index("tm"), lax.axis_index("row")
    size = gain.shape[0]
    barrier = pltpu.get_barrier_semaphore()
    first, last = core == 0, z == 7

    @pl.when(first)
    def _():
        greet(barrier, time_pos + 1, row_pos)

    @pl.when(jnp.logical_not(last))
    def _():
        greet(barrier, 2 * z + 2, row_pos)

    put(two, gain[...])
    link = remote(gain, near_gain, send.at[0], recv.at[0], 2 * z, row_pos)
    small = remote(offset, near_offset, send.at[1], recv.at[1], 2 * z, row_pos)

    @pl.when(core == 1)
    def _():
        pl.semaphore_wait(barrier, 1)
        link.start()
        small.start()
        state[...] = offset[0:8, :]

    @pl.when(first & (z > 0))
    def _():
        pl.semaphore_wait(barrier, 2)

    @pl.when(first)
    def _():
        link.wait_recv()
        small.wait_recv()
        put(one, near_gain[...])
        put(one, near_offset[...], size)
        product = times(one, two)
        put(two, product[:size])
        state[...] = product[size : size + 8] + offset[0:8, :]

    @pl.when(jnp.logical_not(last))
    def _():
        remote(held, held, send.at[2], recv.at[2], time_pos, row_pos).wait_recv()
        value = held[...]
        high = value.astype(BF16).astype(F32)
        both = jnp.concatenate([high, value - high], axis=0).astype(BF16)
        result = dot(both, two[0][...])
        result = result[:8] + result[8:] + dot(both, two[1][...])[:8]
        state[...] = state[...] + result

    @pl.when(first & (z > 0))
    def _():
        sent[...] = state[...]
        copies = [remote(sent, held, send.at[2 + k], recv.at[2], 2 * z - 2 + k, row_pos) for k in range(2)]
        for copy in copies:
            copy.start()
        for copy in copies:
            copy.wait_send()

    smooth[...] = state[...]

    @pl.when(core == 1)
    def _():
        link.wait_send()
        small.wait_send()


def body(trans, mean, cov, info, pull, dynamics, noise):
    row_pos = lax.axis_index("row")
    piece, size = trans.shape[1:]
    row_start = row_pos * piece
    shape = jax.ShapeDtypeStruct
    vmem = pl.BlockSpec(memory_space=pltpu.VMEM)
    dma = pltpu.SemaphoreType.DMA

    def params(**more):
        return pltpu.CompilerParams(vmem_limit_bytes=VMEM_LIMIT, **more)

    lines = jnp.concatenate([mean, pull, jnp.zeros((6, piece), F32)], axis=0)
    placed = lax.dynamic_update_slice(jnp.zeros((8, size), F32), lines, (0, row_start))
    slab = shape((4, 4, 3 * piece + 8, size), F32)
    own_slabs, prior_slabs = pl.pallas_call(
        gather_kernel,
        out_shape=(slab, slab),
        in_specs=[vmem] * 4,
        out_specs=(vmem, vmem),
        scratch_shapes=[dma((8,)), dma((8,)), dma((4,)), dma((4,))],
        compiler_params=params(collective_id=0, has_side_effects=True),
    )(trans[0], cov[0], info[0], placed)

    mats_shape, vecs_shape = shape((3, size, size), F32), shape((VROWS, size), F32)
    held = [pltpu.VMEM((3, size, size), F32), pltpu.VMEM((VROWS, size), F32)]
    flat = (16, 3 * piece + 8, size)
    mats, vecs = pl.pallas_call(
        first_kernel,
        out_shape=(mats_shape, vecs_shape),
        in_specs=[vmem] * 2,
        out_specs=(vmem, vmem),
        scratch_shapes=held * 2 + [pltpu.VMEM((size, size), F32)] + scratch_pairs(size, 6, TALL),
        compiler_params=params(),
    )(own_slabs.reshape(flat), prior_slabs.reshape(flat))

    def passed(mats, vecs, distance, count):
        return pl.pallas_call(
            functools.partial(pass_kernel, distance=distance),
            out_shape=(shape((count * size, size), F32), shape((8, size), F32)),
            in_specs=[pl.BlockSpec(memory_space=pl.ANY)] * 2,
            out_specs=(vmem, vmem),
            scratch_shapes=[dma((8,)), dma((8,)), dma((8,)), dma((5,)), dma((8,)), dma],
            compiler_params=params(collective_id=distance, has_side_effects=True),
        )(mats.reshape(3 * size, size), vecs)

    for distance in (2, 4):
        got, got_vec = passed(mats, vecs, distance, 3)
        mats, vecs = pl.pallas_call(
            functools.partial(level_kernel, distance=distance),
            out_shape=(mats_shape, vecs_shape),
            in_specs=[vmem] * 4,
            out_specs=(vmem, vmem),
            scratch_shapes=[pltpu.VMEM((size, size), F32)] + scratch_pairs(size, 6, TALL),
            compiler_params=params(),
        )(mats, vecs, got.reshape(3, size, size), got_vec)

    got, got_vec = passed(mats, vecs, 8, 1)
    gain, offset, cov_out, mean_out = pl.pallas_call(
        functools.partial(gain_kernel, distance=8),
        out_shape=(
            shape((size, size), F32),
            vecs_shape,
            shape((piece, size), F32),
            shape((8, size), F32),
        ),
        in_specs=[vmem] * 6,
        out_specs=(vmem,) * 4,
        scratch_shapes=[pltpu.VMEM((1, size, size), F32), pltpu.VMEM((size, size), F32)]
        + scratch_pairs(size, 6, TALL),
        compiler_params=params(),
    )(mats, vecs, got.reshape(1, size, size), got_vec, dynamics[0], noise[0])

    smooth = pl.pallas_call(
        chain_kernel,
        out_shape=shape((8, size), F32),
        in_specs=[vmem] * 2,
        out_specs=vmem,
        scratch_shapes=[
            pltpu.VMEM((size, size), F32),
            pltpu.VMEM((VROWS, size), F32),
            pltpu.VMEM((8, size), F32),
            pltpu.VMEM((8, size), F32),
            pltpu.VMEM((8, size), F32),
        ]
        + scratch_pairs(size, 2, (0,))
        + [dma((4,)), dma((3,))],
        compiler_params=params(collective_id=1, has_side_effects=True),
    )(gain, offset)

    return (
        lax.dynamic_slice(smooth, (0, row_start), (1, piece)),
        lax.dynamic_slice(mean_out, (0, row_start), (1, piece)),
        cov_out[None],
    )


def solution(mesh):
    in_specs = (
        P("tm", "row", None),
        P("tm", "row"),
        P("tm", "row", None),
        P("tm", "row", None),
        P("tm", "row"),
        P("tm", None, None),
        P("tm", None, None),
    )
    out_specs = (P("tm", "row"), P("tm", "row"), P("tm", "row", None))
    return jax.shard_map(body, mesh=mesh, in_specs=in_specs, out_specs=out_specs, check_vma=False)
```

```python
import functools

import jax
import jax.numpy as jnp
from jax import lax
from jax.experimental import pallas as pl
from jax.experimental.pallas import tpu as pltpu
from jax.sharding import PartitionSpec as P

MESH = pl.DeviceIdType.MESH
F32, BF16 = jnp.float32, jnp.bfloat16
NN = (((1,), (0,)), ((), ()))
NT = (((1,), (1,)), ((), ()))
TN = (((0,), (0,)), ((), ()))
VROWS = 16
LANES = 128
REACH = 0.008
SMALL = 4e-3
MIB = 1024 * 1024


def places():
    time_pos, row_pos = lax.axis_index("tm"), lax.axis_index("row")
    return time_pos // 2, time_pos % 2, row_pos // 4, row_pos % 4


def dot(lhs, rhs, dims=NN):
    return lax.dot_general(lhs, rhs, dims, preferred_element_type=F32)


def put(pair, value, start=0, column=0):
    high = value.astype(BF16)
    rows, columns = pl.ds(start, value.shape[0]), pl.ds(column, value.shape[1])
    pair[0, rows, columns] = high
    pair[1, rows, columns] = (value - high.astype(F32)).astype(BF16)


def put_high(pair, value):
    pair[0, : value.shape[0], :] = value.astype(BF16)


class Tools:
    def __init__(self, refs):
        self.product, self.value, *self.pairs = refs
        self.size = self.value.shape[0]

    def times(self, lhs, rhs, dims=NN, rows=None):
        size = self.size
        rows = lhs.shape[1] if rows is None else rows
        high, low = rhs[0, :size, :], rhs[1, :size, :]
        left = lhs[0, :rows, :]
        return dot(left, high, dims) + dot(left, low, dims) + dot(lhs[1, :rows, :], high, dims)

    def thin(self, lhs, rhs):
        size = self.size
        high = lhs.astype(BF16)
        low = (lhs - high.astype(F32)).astype(BF16)
        return dot(high, rhs[0, :size, :]) + dot(high, rhs[1, :size, :]) + dot(low, rhs[0, :size, :])


def scratch_tools(size):
    tall = size + VROWS
    return [pltpu.VMEM((tall, size), F32), pltpu.VMEM((size, size), F32)] + [
        pltpu.VMEM((2, tall if index in (0, 4, 5) else size, size), BF16) for index in range(6)
    ]


def eye(size):
    rows = lax.broadcasted_iota(jnp.int32, (size, size), 0)
    return (rows == lax.broadcasted_iota(jnp.int32, (size, size), 1)).astype(F32)


def invert(tools, upper, lower, out, mat, work):
    size, value, product = tools.size, tools.value, tools.product
    first = 2.0 / (upper + lower)
    opening = (upper - lower) / (upper + lower)

    def scale_of(bound):
        return 2.0 / (2.0 - bound * bound)

    def start():
        whole = mat[0].astype(F32) + mat[1].astype(F32)
        new = (scale_of(opening) * first) * (2.0 * eye(size) - first * whole)
        value[...] = new
        put(out, new)

    def add(lhs, rhs, count, sign):
        def one(index, carry):
            left = lhs[index // 2, :size, :]
            right = rhs[index % 2, :size, :]
            product[:size, :] = product[:size, :] + sign * dot(left, right)
            return carry

        lax.fori_loop(0, count, one, 0)

    def settle(new):
        value[...] = new
        put(out, new)

    def next_bound(bound):
        return bound * bound * 0.5 * scale_of(bound)

    def coarse(bound):
        put_high(work, eye(size) - dot(mat[0], out[0]))
        settle(scale_of(bound) * (value[...] + dot(out[0], work[0, :size, :])))
        return next_bound(bound)

    def careful(bound):
        product[:size, :] = eye(size)
        add(mat, out, 3, -1.0)
        put(work, product[:size, :])
        product[:size, :] = value[...]
        add(out, work, 3, 1.0)
        settle(scale_of(bound) * product[:size, :])
        return next_bound(bound)

    def check():
        residual = eye(size) - tools.times(mat, out)
        product[:size, :] = residual
        put_high(work, residual)
        return jnp.sum(residual * residual)

    def step():
        settle(value[...] + dot(out[0], work[0, :size, :]))

    def recheck(error):
        start()
        lax.while_loop(lambda bound: bound > REACH, careful, next_bound(opening))
        product[:size, :] = eye(size)
        add(mat, out, 3, -1.0)
        residual = product[:size, :]
        put_high(work, residual)
        return jnp.sum(residual * residual)

    def again(carry):
        step()
        return carry[0] + 1, check()

    start()
    lax.while_loop(lambda bound: bound > REACH, coarse, next_bound(opening))
    error = check()
    error = lax.cond(error < 1.0, lambda e: e, recheck, error)
    lax.while_loop(lambda c: (c[0] < 60) & (c[1] > SMALL), again, (jnp.int32(0), error))
    put_high(work, product[:size, :] + dot(work[0, :size, :], work[0, :size, :]))
    step()


def one_norm(matrix):
    return jnp.max(jnp.sum(jnp.abs(matrix), axis=0, keepdims=True))


def spread(row):
    return jnp.broadcast_to(row, (VROWS, row.shape[1]))


def row_of(tile, start):
    return jnp.concatenate([tile[start + i : start + i + 1, :] for i in range(4)], axis=1)


def set_row(tile, start, row):
    for i in range(4):
        tile[start + i : start + i + 1, :] = row[0:1, i * LANES : (i + 1) * LANES]


UPPER = [(i, j) for i in range(4) for j in range(i, 4)]
FULL = [(i, j) for i in range(4) for j in range(4)]
BLOCKS = {0: (0, UPPER), 2: (10, UPPER), 1: (20, FULL)}


def each_block(packed, which):
    base, places_of = BLOCKS[which]
    for index, (i, j) in enumerate(places_of):
        value = packed[pl.ds((base + index) * LANES, LANES), :]
        yield i * LANES, j * LANES, value
        if places_of is UPPER and i != j:
            yield j * LANES, i * LANES, value.T


def pack(mats, packed, which):
    base, places_of = BLOCKS[which]
    for index, (i, j) in enumerate(places_of):
        packed[pl.ds((base + index) * LANES, LANES), :] = mats[
            which, pl.ds(i * LANES, LANES), pl.ds(j * LANES, LANES)
        ]


def fill(prior, which, pair):
    if len(prior.shape) == 3:
        put(pair, prior[which])
    else:
        for i, j, value in each_block(prior, which):
            put(pair, value, i, j)


def increase(mats, which, prior):
    if len(prior.shape) == 3:
        mats[which] = mats[which] + prior[which]
    else:
        for i, j, value in each_block(prior, which):
            rows, columns = pl.ds(i, LANES), pl.ds(j, LANES)
            mats[which, rows, columns] = mats[which, rows, columns] + value


def combine(own, own_vec, prior, prior_vec, new, new_vec, tools, closing):
    size = tools.size
    times, thin = tools.times, tools.thin
    one, two, three, four, five, six = tools.pairs
    prior_mean, prior_pull = row_of(prior_vec, 0), row_of(prior_vec, 4)
    mean, pull = row_of(own_vec, 0), row_of(own_vec, 4)
    put(one, own[2])
    put(one, spread(pull), size)
    fill(prior, 0, two)
    coupling = times(one, two)
    shifted = prior_mean + coupling[size : size + 1]
    coupling = coupling[:size]
    upper = 2.0 + one_norm(coupling)
    put(four, eye(size) + coupling)
    invert(tools, upper, 1.0, three, four, five)
    put(four, own[1])
    put(five, times(two, three))
    put(six, times(five, four, rows=size))
    new[0] = times(four, six, TN) + own[0]
    if closing:
        moved = thin(thin(spread(shifted), three), four)
        set_row(new_vec, 0, moved[0:1] + mean)
        return
    fill(prior, 1, five)
    put(five, spread(shifted), size)
    gained = times(five, three)
    put(two, gained[:size])
    put(six, gained)
    moved = times(six, four)
    new[1] = moved[:size]
    set_row(new_vec, 0, moved[size : size + 1] + mean)
    put(three, own[2])
    put(five, spread(prior_mean), size)
    pulled = times(five, three)
    put(six, pulled[:size])
    put(six, spread(pull - pulled[size : size + 1]), size)
    informed = times(six, two, NT)
    new[2] = informed[:size]
    increase(new, 2, prior)
    set_row(new_vec, 4, informed[size : size + 1] + prior_pull)


def unpack(slabs, mats, vecs):
    piece = mats.shape[1] // 16
    for y in range(4):
        total = None
        for x in range(4):
            rows = pl.ds((4 * y + x) * piece, piece)
            for index in range(10):
                which = 1 if index < 4 else 0 if index < 7 else 2
                group = index if index < 4 else (y + (index - 4) % 3) % 4
                mats[which, rows, pl.ds(group * LANES, LANES)] = slabs[y, x, pl.ds(index * piece, piece), :]
            tile = slabs[y, x, pl.ds(10 * piece, 8), :]
            total = tile if total is None else total + tile
        vecs[y : y + 1, :] = total[0:1, :]
        vecs[4 + y : 5 + y, :] = total[1:2, :]
    mats[1] = mats[1].T
    for which in (0, 2):
        for y in range(4):
            left, right = pl.ds(y * LANES, LANES), pl.ds((y + 3) % 4 * LANES, LANES)
            mats[which, left, right] = mats[which, right, left].T


def first_kernel(own_slabs, prior_slabs, new, new_vec, packed, own, own_vec, prior, prior_vec, *refs):
    time_pos = lax.axis_index("tm")
    odd = time_pos % 2 == 1

    @pl.when(odd)
    def _():
        unpack(own_slabs, own, own_vec)
        unpack(prior_slabs, prior, prior_vec)
        combine(own, own_vec, prior, prior_vec, new, new_vec, Tools(refs), False)

    @pl.when(time_pos % 4 == 1)
    def _():
        for which in range(3):
            pack(new, packed, which)

    @pl.when(jnp.logical_not(odd))
    def _():
        unpack(own_slabs, new, new_vec)


def level_kernel(own, own_vec, prior, prior_vec, new, new_vec, packed, *refs, distance):
    time_pos = lax.axis_index("tm")
    present = (time_pos // distance) % 2 == 1

    @pl.when(present)
    def _():
        combine(own, own_vec, prior, prior_vec, new, new_vec, Tools(refs), False)

    @pl.when(time_pos % (4 * distance) == 2 * distance - 1)
    def _():
        for which in range(3) if distance < 4 else (0,):
            pack(new, packed, which)

    @pl.when(jnp.logical_not(present))
    def _():
        new[...] = own[...]
        new_vec[...] = own_vec[...]


def gain_kernel(
    own, own_vec, prior, prior_vec, dynamics, noise, gain, offset, cov_out, mean_out, new, mean_tile, *refs, distance
):
    tools = Tools(refs)
    size, times, thin = tools.size, tools.times, tools.thin
    time_pos, row_pos = lax.axis_index("tm"), lax.axis_index("row")
    present = (time_pos // distance) % 2 == 1
    one, two, three, four, five, six = tools.pairs

    @pl.when(present)
    def _():
        combine(own, own_vec, prior, prior_vec, new, mean_tile, tools, True)

    @pl.when(jnp.logical_not(present))
    def _():
        new[0] = own[0]
        mean_tile[...] = own_vec[...]

    piece = cov_out.shape[0]
    cov_out[...] = new[0, pl.ds(pl.multiple_of(row_pos * piece, piece), piece), :]
    mean = row_of(mean_tile, 0)
    share(mean_out, mean, row_pos)

    @pl.when(time_pos == 15)
    def _():
        gain[...] = jnp.zeros_like(gain)
        offset[...] = jnp.broadcast_to(mean, offset.shape)

    @pl.when(time_pos < 15)
    def _():
        put(two, dynamics[...])
        put(three, new[0])
        put(one, times(two, three))
        put(one, spread(mean), size)
        projected = times(one, two, NT)
        predicted = projected[size:]
        innovation = projected[:size] + noise[...]
        upper = one_norm(innovation)
        put(four, innovation)
        invert(tools, upper, upper * 0.004, three, four, two)
        weights = times(three, one)
        gain[...] = weights
        put(six, weights)
        offset[...] = mean - thin(predicted, six)[:8]


def share(out, row, row_pos):
    piece = out.shape[1]
    for index in range(16):

        @pl.when(row_pos == index)
        def _():
            out[...] = row[0:1, index * piece : (index + 1) * piece]


def remote(src, dst, send, recv, tm, row):
    return pltpu.make_async_remote_copy(
        src_ref=src, dst_ref=dst, send_sem=send, recv_sem=recv, device_id=(tm, row), device_id_type=MESH
    )


def greet(barrier, tm, row):
    pl.semaphore_signal(barrier, inc=1, device_id=(tm, row), device_id_type=MESH)


def gather_kernel(trans, mean, cov, info, pull, own, prior, send, recv, far_send, far_recv):
    z, core, y, x = places()
    time_pos, row_pos = lax.axis_index("tm"), lax.axis_index("row")
    piece = trans.shape[0]
    keep = (time_pos > 0).astype(F32)
    barrier = pltpu.get_barrier_semaphore()
    across = [y * 4 + (x + k) % 4 for k in (1, 2, 3)]
    along = [((y + k) % 4) * 4 + x for k in (1, 2, 3)]
    for peer in across + along:
        greet(barrier, time_pos, peer)

    @pl.when(core == 1)
    def _():
        greet(barrier, time_pos - 1, row_pos)

    for index in range(4):
        own[y, x, pl.ds(index * piece, piece), :] = trans[:, index * LANES : (index + 1) * LANES] * keep
    for index in range(3):
        columns = pl.ds(pl.multiple_of((y + index) % 4 * LANES, LANES), LANES)
        own[y, x, pl.ds((4 + index) * piece, piece), :] = cov[:, columns]
        own[y, x, pl.ds((7 + index) * piece, piece), :] = info[:, columns] * keep
    own[y, x, pl.ds(10 * piece, 8), :] = jnp.zeros((8, LANES), F32)
    for index in range(4):

        @pl.when(x == index)
        def _():
            lanes = pl.ds(index * piece, piece)
            own[y, x, pl.ds(10 * piece, 1), lanes] = mean[...]
            own[y, x, pl.ds(10 * piece + 1, 1), lanes] = pull[...] * keep

    def gather(near, other, line):
        copies = []
        for k in range(3):
            copy = remote(own.at[y, x], own.at[y, x], send.at[k], recv.at[k], time_pos, near[k])
            copy.start()
            copies.append(copy)
        for copy in copies:
            copy.wait_recv()
        later = []
        for k in range(3):
            copy = remote(line, line, send.at[3 + k], recv.at[3 + k], time_pos, other[k])
            copy.start()
            later.append(copy)
        return copies, later

    @pl.when(core == 0)
    def _():
        pl.semaphore_wait(barrier, 7)
        copies, later = gather(across, along, own.at[y])
        passed = []
        for k in range(4):
            if k:
                later[k - 1].wait_recv()
            line = (y + 4 - k) % 4
            copy = remote(own.at[line], prior.at[line], far_send.at[k], far_recv.at[k], time_pos + 1, row_pos)
            copy.start()
            passed.append(copy)
        for copy in copies + later + passed:
            copy.wait_send()

    @pl.when(core == 1)
    def _():
        pl.semaphore_wait(barrier, 6)
        copies, later = gather(along, across, own.at[:, x])
        for copy in later:
            copy.wait_recv()
        for copy in copies + later:
            copy.wait_send()
        for k in range(4):
            line = (y + 4 - k) % 4
            remote(own.at[line], prior.at[line], far_send.at[k], far_recv.at[k], time_pos, row_pos).wait_recv()


CHUNKS = 2


def pass_kernel(packed, vecs, got, got_vec, far_send, far_recv, send, recv, twin_send, twin_recv, vec_send, vec_recv, *, distance, relay):
    z, core, y, x = places()
    time_pos, row_pos = lax.axis_index("tm"), lax.axis_index("row")
    reach = distance // 2
    rows = got.shape[0] // (8 * CHUNKS)
    barrier = pltpu.get_barrier_semaphore()
    target = (z // reach) % 2 == 1
    source = ((z // reach) % 2 == 0) & (z % reach == reach - 1) & (core == 1)
    source_pos = ((z // reach) * reach) * 2 - 1
    outer_pos = (1 - core) * y + core * x
    hops = 1 if relay else reach

    def view(ref, side, line, chunk):
        start = ((side * 4 + line) * CHUNKS + chunk) * rows
        return ref.at[pl.ds(pl.multiple_of(start, 8), rows)]

    def outer_row(k):
        place = (outer_pos + k) % 4
        return (1 - core) * (place * 4 + x) + core * (y * 4 + place)

    @pl.when(source)
    def _():
        pl.semaphore_wait(barrier, 2 * hops)
        copies = []
        for step in reversed(range(hops)):
            for side in range(2):
                slot = 2 * step + side
                there = time_pos + 1 + slot
                small = remote(vecs, got_vec, vec_send.at[slot], vec_recv, there, row_pos)
                small.start()
                copies.append(small)
        for chunk in range(CHUNKS):
            for step in reversed(range(hops)):
                for side in range(2):
                    slot = 2 * step + side
                    there = time_pos + 1 + slot
                    line = y if side == 0 else x
                    copy = remote(
                        view(packed, side, line, chunk),
                        view(got, side, line, chunk),
                        far_send.at[slot * CHUNKS + chunk],
                        far_recv.at[chunk],
                        there,
                        row_pos,
                    )
                    copy.start()
                    copies.append(copy)
        for copy in copies:
            copy.wait_send()

    @pl.when(target)
    def _():
        twin = 2 * z + 1 - core
        onward = (z % reach) < reach - 1
        first = (z % reach) == 0
        if relay:

            @pl.when(first)
            def _():
                greet(barrier, source_pos, row_pos)

            @pl.when(jnp.logical_not(first))
            def _():
                greet(barrier, time_pos - 2, row_pos)

        else:
            greet(barrier, source_pos, row_pos)
        for k in (1, 2, 3):
            greet(barrier, time_pos, outer_row(k))
        greet(barrier, twin, row_pos)
        if relay:

            @pl.when(onward)
            def _():
                pl.semaphore_wait(barrier, 5)

            @pl.when(jnp.logical_not(onward))
            def _():
                pl.semaphore_wait(barrier, 4)

        else:
            pl.semaphore_wait(barrier, 4)
        copies = []
        relayed = []
        arrived = remote(got_vec, got_vec, vec_send.at[0], vec_recv, time_pos + 2, row_pos)
        if relay:
            arrived.wait_recv()

            @pl.when(onward)
            def _():
                arrived.start()

        def over(k, chunk):
            mine = view(got, core, (outer_pos + 4 - k) % 4, chunk)
            slot = k * CHUNKS + chunk
            copy = remote(mine, mine, twin_send.at[slot], twin_recv.at[slot], twin, row_pos)
            copy.start()
            copies.append(copy)

        for chunk in range(CHUNKS):
            mine = view(got, core, outer_pos, chunk)
            onto = remote(mine, mine, far_send.at[chunk], far_recv.at[chunk], time_pos + 2, row_pos)
            onto.wait_recv()
            if relay:

                @pl.when(onward)
                def _():
                    onto.start()

                relayed.append(onto)
            for k in range(1, 4):
                slot = (k - 1) * CHUNKS + chunk
                copy = remote(mine, mine, send.at[slot], recv.at[slot], time_pos, outer_row(k))
                copy.start()
                copies.append(copy)
            over(0, chunk)
        for chunk in range(CHUNKS):
            for k in (1, 3, 2):
                line = view(got, core, (outer_pos + 4 - k) % 4, chunk)
                slot = (k - 1) * CHUNKS + chunk
                remote(line, line, send.at[slot], recv.at[slot], time_pos, outer_row(k)).wait_recv()
                over(k, chunk)
        for k in range(4):
            for chunk in range(CHUNKS):
                theirs = view(got, 1 - core, 0, chunk)
                slot = k * CHUNKS + chunk
                remote(theirs, theirs, twin_send.at[slot], twin_recv.at[slot], twin, row_pos).wait_recv()
        if not relay:
            arrived.wait_recv()
        for copy in copies:
            copy.wait_send()
        if relay:

            @pl.when(onward)
            def _():
                arrived.wait_send()
                for copy in relayed:
                    copy.wait_send()


def chain_kernel(gain, offset, smooth, near_gain, near_offset, held, sent, state, *rest):
    refs, (send, recv) = rest[:-2], rest[-2:]
    product, one, two = refs
    z, core, _, _ = places()
    time_pos, row_pos = lax.axis_index("tm"), lax.axis_index("row")
    size = gain.shape[0]
    barrier = pltpu.get_barrier_semaphore()
    first, last = core == 0, z == 7

    @pl.when(first)
    def _():
        greet(barrier, time_pos + 1, row_pos)

    @pl.when(jnp.logical_not(last))
    def _():
        greet(barrier, 2 * z + 2, row_pos)

    put(two, gain[...])
    link = remote(gain, near_gain, send.at[0], recv.at[0], 2 * z, row_pos)
    small = remote(offset, near_offset, send.at[1], recv.at[1], 2 * z, row_pos)

    def apply(row8):
        high = row8.astype(BF16).astype(F32)
        both = jnp.concatenate([high, row8 - high], axis=0).astype(BF16)
        result = dot(both, two[0])
        return result[:8] + result[8:] + dot(both, two[1])[:8]

    @pl.when(core == 1)
    def _():
        pl.semaphore_wait(barrier, 1)
        small.start()

        @pl.when(jnp.logical_not(last))
        def _():
            link.start()

        state[...] = offset[...]

    @pl.when(first & (z > 0))
    def _():
        pl.semaphore_wait(barrier, 2)

    @pl.when(first & last)
    def _():
        small.wait_recv()
        state[...] = apply(near_offset[...]) + offset[...]

    @pl.when(first & jnp.logical_not(last))
    def _():
        small.wait_recv()
        state[...] = apply(near_offset[...]) + offset[...]
        link.wait_recv()
        put(one, near_gain[...])

        def part(index, carry):
            columns = pl.ds(pl.multiple_of(index * 256, 256), 256)
            high, low = two[0, :, columns], two[1, :, columns]
            product[:, columns] = dot(one[0], high) + dot(one[0], low) + dot(one[1], high)
            return carry

        lax.fori_loop(0, size // 256, part, 0)
        put(two, product[...])

    @pl.when(jnp.logical_not(last))
    def _():
        remote(held, held, send.at[2], recv.at[2], time_pos, row_pos).wait_recv()
        state[...] = state[...] + apply(held[...])

    @pl.when(first & (z > 0))
    def _():
        sent[...] = state[...]
        copies = [remote(sent, held, send.at[2 + k], recv.at[2], 2 * z - 2 + k, row_pos) for k in range(2)]
        for copy in copies:
            copy.start()
        for copy in copies:
            copy.wait_send()

    share(smooth, state[0:1, :], row_pos)

    @pl.when(core == 1)
    def _():
        small.wait_send()

        @pl.when(jnp.logical_not(last))
        def _():
            link.wait_send()


def body(trans, mean, cov, info, pull, dynamics, noise):
    piece, size = trans.shape[1:]
    shape = jax.ShapeDtypeStruct
    vmem = pl.BlockSpec(memory_space=pltpu.VMEM)
    dma = pltpu.SemaphoreType.DMA

    def params(mib, **more):
        return pltpu.CompilerParams(vmem_limit_bytes=mib * MIB, **more)

    slab = shape((4, 4, 10 * piece + 8, LANES), F32)
    own_slabs, prior_slabs = pl.pallas_call(
        gather_kernel,
        out_shape=(slab, slab),
        in_specs=[vmem] * 5,
        out_specs=(vmem, vmem),
        scratch_shapes=[dma((6,)), dma((6,)), dma((4,)), dma((4,))],
        compiler_params=params(12, collective_id=0, has_side_effects=True),
    )(trans[0], mean, cov[0], info[0], pull)

    mats_shape, vecs_shape = shape((3, size, size), F32), shape((8, LANES), F32)
    packed_shape = shape((36 * LANES, LANES), F32)
    held = [pltpu.VMEM((3, size, size), F32), pltpu.VMEM((8, LANES), F32)]
    mats, vecs, packed = pl.pallas_call(
        first_kernel,
        out_shape=(mats_shape, vecs_shape, packed_shape),
        in_specs=[vmem] * 2,
        out_specs=(vmem,) * 3,
        scratch_shapes=held * 2 + scratch_tools(size),
        compiler_params=params(32),
    )(own_slabs, prior_slabs)

    def passed(packed, vecs, distance, blocks):
        return pl.pallas_call(
            functools.partial(pass_kernel, distance=distance, relay=distance == 4),
            out_shape=(shape((blocks * LANES, LANES), F32), vecs_shape),
            in_specs=[vmem] * 2,
            out_specs=(vmem, vmem),
            scratch_shapes=[
                dma((8 * CHUNKS,)),
                dma((CHUNKS,)),
                dma((3 * CHUNKS,)),
                dma((3 * CHUNKS,)),
                dma((4 * CHUNKS,)),
                dma((4 * CHUNKS,)),
                dma((8,)),
                dma,
            ],
            compiler_params=params(12, collective_id=distance, has_side_effects=True),
        )(packed, vecs)

    for distance in (2, 4):
        got, got_vec = passed(packed, vecs, distance, 36)
        mats, vecs, packed = pl.pallas_call(
            functools.partial(level_kernel, distance=distance),
            out_shape=(mats_shape, vecs_shape, packed_shape),
            in_specs=[vmem] * 4,
            out_specs=(vmem,) * 3,
            scratch_shapes=scratch_tools(size),
            compiler_params=params(28),
        )(mats, vecs, got, got_vec)

    got, got_vec = passed(packed, vecs, 8, 10)
    gain, offset, cov_out, mean_out = pl.pallas_call(
        functools.partial(gain_kernel, distance=8),
        out_shape=(
            shape((size, size), F32),
            shape((8, size), F32),
            shape((piece, size), F32),
            shape((1, piece), F32),
        ),
        in_specs=[vmem] * 6,
        out_specs=(vmem,) * 4,
        scratch_shapes=[pltpu.VMEM((1, size, size), F32), pltpu.VMEM((8, LANES), F32)] + scratch_tools(size),
        compiler_params=params(28),
    )(mats, vecs, got, got_vec, dynamics[0], noise[0])

    smooth = pl.pallas_call(
        chain_kernel,
        out_shape=shape((1, piece), F32),
        in_specs=[vmem] * 2,
        out_specs=vmem,
        scratch_shapes=[
            pltpu.VMEM((size, size), F32),
            pltpu.VMEM((8, size), F32),
            pltpu.VMEM((8, size), F32),
            pltpu.VMEM((8, size), F32),
            pltpu.VMEM((8, size), F32),
            pltpu.VMEM((size, size), F32),
            pltpu.VMEM((2, size, size), BF16),
            pltpu.VMEM((2, size, size), BF16),
            dma((4,)),
            dma((3,)),
        ],
        compiler_params=params(12, collective_id=1, has_side_effects=True),
    )(gain, offset)

    return smooth, mean_out, cov_out[None]


def solution(mesh):
    in_specs = (
        P("tm", "row", None),
        P("tm", "row"),
        P("tm", "row", None),
        P("tm", "row", None),
        P("tm", "row"),
        P("tm", None, None),
        P("tm", None, None),
    )
    out_specs = (P("tm", "row"), P("tm", "row"), P("tm", "row", None))
    return jax.shard_map(body, mesh=mesh, in_specs=in_specs, out_specs=out_specs, check_vma=False)
```

```python
import functools

import jax
import jax.numpy as jnp
from jax import lax
from jax.experimental import pallas as pl
from jax.experimental.pallas import tpu as pltpu
from jax.sharding import PartitionSpec as P

MESH = pl.DeviceIdType.MESH
F32, BF16 = jnp.float32, jnp.bfloat16
NN = (((1,), (0,)), ((), ()))
NT = (((1,), (1,)), ((), ()))
TN = (((0,), (0,)), ((), ()))
VROWS = 16
LANES = 128
REACH = 0.008
SMALL = 4e-3
MIB = 1024 * 1024


def places():
    time_pos, row_pos = lax.axis_index("tm"), lax.axis_index("row")
    return time_pos // 2, time_pos % 2, row_pos // 4, row_pos % 4


def dot(lhs, rhs, dims=NN):
    return lax.dot_general(lhs, rhs, dims, preferred_element_type=F32)


def put(pair, value, start=0, column=0):
    high = value.astype(BF16)
    rows, columns = pl.ds(start, value.shape[0]), pl.ds(column, value.shape[1])
    pair[0, rows, columns] = high
    pair[1, rows, columns] = (value - high.astype(F32)).astype(BF16)


def put_high(pair, value):
    pair[0, : value.shape[0], :] = value.astype(BF16)


class Tools:
    def __init__(self, refs):
        self.product, self.value, *self.pairs = refs
        self.size = self.value.shape[0]

    def times(self, lhs, rhs, dims=NN, rows=None):
        size = self.size
        rows = lhs.shape[1] if rows is None else rows
        high, low = rhs[0, :size, :], rhs[1, :size, :]
        left = lhs[0, :rows, :]
        return dot(left, high, dims) + dot(left, low, dims) + dot(lhs[1, :rows, :], high, dims)

    def thin(self, lhs, rhs):
        size = self.size
        high = lhs.astype(BF16)
        low = (lhs - high.astype(F32)).astype(BF16)
        return dot(high, rhs[0, :size, :]) + dot(high, rhs[1, :size, :]) + dot(low, rhs[0, :size, :])


def scratch_tools(size):
    tall = size + VROWS
    return [pltpu.VMEM((tall, size), F32), pltpu.VMEM((size, size), F32)] + [
        pltpu.VMEM((2, tall if index in (0, 4, 5) else size, size), BF16) for index in range(6)
    ]


def eye(size):
    rows = lax.broadcasted_iota(jnp.int32, (size, size), 0)
    return (rows == lax.broadcasted_iota(jnp.int32, (size, size), 1)).astype(F32)


def invert(tools, upper, lower, out, mat, work):
    size, value, product = tools.size, tools.value, tools.product
    first = 2.0 / (upper + lower)
    opening = (upper - lower) / (upper + lower)

    def scale_of(bound):
        return 2.0 / (2.0 - bound * bound)

    def start():
        whole = mat[0].astype(F32) + mat[1].astype(F32)
        new = (scale_of(opening) * first) * (2.0 * eye(size) - first * whole)
        value[...] = new
        put(out, new)

    def add(lhs, rhs, count, sign):
        def one(index, carry):
            left = lhs[index // 2, :size, :]
            right = rhs[index % 2, :size, :]
            product[:size, :] = product[:size, :] + sign * dot(left, right)
            return carry

        lax.fori_loop(0, count, one, 0)

    def settle(new):
        value[...] = new
        put(out, new)

    def next_bound(bound):
        return bound * bound * 0.5 * scale_of(bound)

    def coarse(bound):
        put_high(work, eye(size) - dot(mat[0], out[0]))
        settle(scale_of(bound) * (value[...] + dot(out[0], work[0, :size, :])))
        return next_bound(bound)

    def careful(bound):
        product[:size, :] = eye(size)
        add(mat, out, 3, -1.0)
        put(work, product[:size, :])
        product[:size, :] = value[...]
        add(out, work, 3, 1.0)
        settle(scale_of(bound) * product[:size, :])
        return next_bound(bound)

    def check():
        residual = eye(size) - tools.times(mat, out)
        product[:size, :] = residual
        put_high(work, residual)
        return jnp.sum(residual * residual)

    def step():
        settle(value[...] + dot(out[0], work[0, :size, :]))

    def recheck(error):
        start()
        lax.while_loop(lambda bound: bound > REACH, careful, next_bound(opening))
        product[:size, :] = eye(size)
        add(mat, out, 3, -1.0)
        residual = product[:size, :]
        put_high(work, residual)
        return jnp.sum(residual * residual)

    def again(carry):
        step()
        return carry[0] + 1, check()

    start()
    lax.while_loop(lambda bound: bound > REACH, coarse, next_bound(opening))
    error = check()
    error = lax.cond(error < 1.0, lambda e: e, recheck, error)
    lax.while_loop(lambda c: (c[0] < 60) & (c[1] > SMALL), again, (jnp.int32(0), error))
    put_high(work, product[:size, :] + dot(work[0, :size, :], work[0, :size, :]))
    step()


def one_norm(matrix):
    return jnp.max(jnp.sum(jnp.abs(matrix), axis=0, keepdims=True))


def spread(row):
    return jnp.broadcast_to(row, (VROWS, row.shape[1]))


def row_of(tile, start):
    return jnp.concatenate([tile[start + i : start + i + 1, :] for i in range(4)], axis=1)


def set_row(tile, start, row):
    for i in range(4):
        tile[start + i : start + i + 1, :] = row[0:1, i * LANES : (i + 1) * LANES]


UPPER = [(i, j) for i in range(4) for j in range(i, 4)]
FULL = [(i, j) for i in range(4) for j in range(4)]
BLOCKS = {0: (0, 0, UPPER), 2: (1, 0, UPPER), 1: (1, 10, FULL)}


def each_block(packed, which):
    part, base, places_of = BLOCKS[which]
    for index, (i, j) in enumerate(places_of):
        value = packed[part][pl.ds((base + index) * LANES, LANES), :]
        yield i * LANES, j * LANES, value
        if places_of is UPPER and i != j:
            yield j * LANES, i * LANES, value.T


def pack(mats, packed, which):
    part, base, places_of = BLOCKS[which]
    for index, (i, j) in enumerate(places_of):
        packed[part][pl.ds((base + index) * LANES, LANES), :] = mats[
            which, pl.ds(i * LANES, LANES), pl.ds(j * LANES, LANES)
        ]


def fill(prior, which, pair):
    if isinstance(prior, tuple):
        for i, j, value in each_block(prior, which):
            put(pair, value, i, j)
    else:
        put(pair, prior[which])


def increase(mats, which, prior):
    if isinstance(prior, tuple):
        for i, j, value in each_block(prior, which):
            rows, columns = pl.ds(i, LANES), pl.ds(j, LANES)
            mats[which, rows, columns] = mats[which, rows, columns] + value
    else:
        mats[which] = mats[which] + prior[which]


def solve(own, own_vec, prior, prior_vec, inverse, tools):
    size = tools.size
    one, two, three, four, five, six = tools.pairs
    put(one, own[2])
    put(one, spread(row_of(own_vec, 4)), size)
    fill(prior, 0, two)
    coupling = tools.times(one, two)
    shifted = row_of(prior_vec, 0) + coupling[size : size + 1]
    coupling = coupling[:size]
    upper = 2.0 + one_norm(coupling)
    put(four, eye(size) + coupling)
    invert(tools, upper, 1.0, inverse, four, five)
    return shifted


def combine_cov(own, prior, inverse, new, tools):
    times = tools.times
    one, two, three, four, five, six = tools.pairs
    fill(prior, 0, two)
    put(four, own[1])
    put(five, times(two, inverse))
    put(six, times(five, four, rows=tools.size))
    new[0] = times(four, six, TN) + own[0]


def combine_rest(own, own_vec, prior, prior_vec, inverse, shifted, new, new_vec, tools):
    size, times = tools.size, tools.times
    one, two, three, four, five, six = tools.pairs
    prior_mean, prior_pull = row_of(prior_vec, 0), row_of(prior_vec, 4)
    mean, pull = row_of(own_vec, 0), row_of(own_vec, 4)
    fill(prior, 1, five)
    put(five, spread(shifted), size)
    gained = times(five, inverse)
    put(two, gained[:size])
    put(six, gained)
    moved = times(six, four)
    new[1] = moved[:size]
    set_row(new_vec, 0, moved[size : size + 1] + mean)
    put(three, own[2])
    put(five, spread(prior_mean), size)
    pulled = times(five, three)
    put(six, pulled[:size])
    put(six, spread(pull - pulled[size : size + 1]), size)
    informed = times(six, two, NT)
    new[2] = informed[:size]
    increase(new, 2, prior)
    set_row(new_vec, 4, informed[size : size + 1] + prior_pull)


def unpack(slabs, mats, vecs):
    piece = mats.shape[1] // 16
    for y in range(4):
        total = None
        for x in range(4):
            rows = pl.ds((4 * y + x) * piece, piece)
            for index in range(10):
                which = 1 if index < 4 else 0 if index < 7 else 2
                group = index if index < 4 else (y + (index - 4) % 3) % 4
                mats[which, rows, pl.ds(group * LANES, LANES)] = slabs[y, x, pl.ds(index * piece, piece), :]
            tile = slabs[y, x, pl.ds(10 * piece, 8), :]
            total = tile if total is None else total + tile
        vecs[y : y + 1, :] = total[0:1, :]
        vecs[4 + y : 5 + y, :] = total[1:2, :]
    mats[1] = mats[1].T
    for which in (0, 2):
        for y in range(4):
            left, right = pl.ds(y * LANES, LANES), pl.ds((y + 3) % 4 * LANES, LANES)
            mats[which, left, right] = mats[which, right, left].T


def first_kernel(own_slabs, prior_slabs, own, own_vec, prior, prior_vec, inverse, shifted, *refs):
    odd = lax.axis_index("tm") % 2 == 1
    unpack(own_slabs, own, own_vec)

    @pl.when(odd)
    def _():
        unpack(prior_slabs, prior, prior_vec)
        shifted[...] = spread(solve(own, own_vec, prior, prior_vec, inverse, Tools(refs)))[:8]


def level_kernel(own, own_vec, prior_cov, prior_rest, prior_vec, inverse, shifted, *refs, distance):
    @pl.when((lax.axis_index("tm") // distance) % 2 == 1)
    def _():
        prior = (prior_cov, prior_rest)
        shifted[...] = spread(solve(own, own_vec, prior, prior_vec, inverse, Tools(refs)))[:8]


def gain_kernel(
    own, own_vec, prior_cov, prior_vec, dynamics, noise, gain, offset, cov_out, mean_out, new, mean_tile, *refs, distance
):
    tools = Tools(refs)
    size, times, thin = tools.size, tools.times, tools.thin
    time_pos, row_pos = lax.axis_index("tm"), lax.axis_index("row")
    present = (time_pos // distance) % 2 == 1
    one, two, three, four, five, six = tools.pairs

    @pl.when(present)
    def _():
        prior = (prior_cov,)
        shifted = solve(own, own_vec, prior, prior_vec, three, tools)
        combine_cov(own, prior, three, new, tools)
        moved = thin(thin(spread(shifted), three), four)
        set_row(mean_tile, 0, moved[0:1] + row_of(own_vec, 0))

    @pl.when(jnp.logical_not(present))
    def _():
        new[0] = own[0]
        mean_tile[...] = own_vec[...]

    piece = cov_out.shape[0]
    cov_out[...] = new[0, pl.ds(pl.multiple_of(row_pos * piece, piece), piece), :]
    mean = row_of(mean_tile, 0)
    share(mean_out, mean, row_pos)

    @pl.when(time_pos == 15)
    def _():
        gain[...] = jnp.zeros_like(gain)
        offset[...] = jnp.broadcast_to(mean, offset.shape)

    @pl.when(time_pos < 15)
    def _():
        put(two, dynamics[...])
        put(three, new[0])
        put(one, times(two, three))
        put(one, spread(mean), size)
        projected = times(one, two, NT)
        predicted = projected[size:]
        innovation = projected[:size] + noise[...]
        upper = one_norm(innovation)
        put(four, innovation)
        invert(tools, upper, upper * 0.004, three, four, two)
        weights = times(three, one)
        gain[...] = weights
        put(six, weights)
        offset[...] = mean - thin(predicted, six)[:8]


def share(out, row, row_pos):
    piece = out.shape[1]
    for index in range(16):

        @pl.when(row_pos == index)
        def _():
            out[...] = row[0:1, index * piece : (index + 1) * piece]


def remote(src, dst, send, recv, tm, row):
    return pltpu.make_async_remote_copy(
        src_ref=src, dst_ref=dst, send_sem=send, recv_sem=recv, device_id=(tm, row), device_id_type=MESH
    )


def greet(barrier, tm, row):
    pl.semaphore_signal(barrier, inc=1, device_id=(tm, row), device_id_type=MESH)


def gather_kernel(trans_in, mean_in, cov_in, info_in, pull_in, own, prior, *refs):
    trans, mean, cov, info, pull, load, send, recv, far_send, far_recv = refs
    loads = []
    for index, pair in enumerate(zip((trans_in, mean_in, cov_in, info_in, pull_in), (trans, mean, cov, info, pull))):
        loads.append(pltpu.make_async_copy(*pair, load.at[index]))
        loads[-1].start()
    z, core, y, x = places()
    time_pos, row_pos = lax.axis_index("tm"), lax.axis_index("row")
    piece = trans.shape[0]
    keep = (time_pos > 0).astype(F32)
    barrier = pltpu.get_barrier_semaphore()
    across = [y * 4 + (x + k) % 4 for k in (1, 2, 3)]
    along = [((y + k) % 4) * 4 + x for k in (1, 2, 3)]
    for peer in across + along:
        greet(barrier, time_pos, peer)

    @pl.when(core == 1)
    def _():
        greet(barrier, time_pos - 1, row_pos)

    for copy in loads:
        copy.wait()
    for index in range(4):
        own[y, x, pl.ds(index * piece, piece), :] = trans[:, index * LANES : (index + 1) * LANES] * keep
    for index in range(3):
        columns = pl.ds(pl.multiple_of((y + index) % 4 * LANES, LANES), LANES)
        own[y, x, pl.ds((4 + index) * piece, piece), :] = cov[:, columns]
        own[y, x, pl.ds((7 + index) * piece, piece), :] = info[:, columns] * keep
    own[y, x, pl.ds(10 * piece, 8), :] = jnp.zeros((8, LANES), F32)
    for index in range(4):

        @pl.when(x == index)
        def _():
            lanes = pl.ds(index * piece, piece)
            own[y, x, pl.ds(10 * piece, 1), lanes] = mean[...]
            own[y, x, pl.ds(10 * piece + 1, 1), lanes] = pull[...] * keep

    def gather(near, other, line):
        copies = []
        for k in range(3):
            copy = remote(own.at[y, x], own.at[y, x], send.at[k], recv.at[k], time_pos, near[k])
            copy.start()
            copies.append(copy)
        for copy in copies:
            copy.wait_recv()
        later = []
        for k in range(3):
            copy = remote(line, line, send.at[3 + k], recv.at[3 + k], time_pos, other[k])
            copy.start()
            later.append(copy)
        return copies, later

    @pl.when(core == 0)
    def _():
        pl.semaphore_wait(barrier, 7)
        copies, later = gather(across, along, own.at[y])
        passed = []
        for k in range(4):
            if k:
                later[k - 1].wait_recv()
            line = (y + 4 - k) % 4
            copy = remote(own.at[line], prior.at[line], far_send.at[k], far_recv.at[k], time_pos + 1, row_pos)
            copy.start()
            passed.append(copy)
        for copy in copies + later + passed:
            copy.wait_send()

    @pl.when(core == 1)
    def _():
        pl.semaphore_wait(barrier, 6)
        copies, later = gather(along, across, own.at[:, x])
        for copy in later:
            copy.wait_recv()
        for copy in copies + later:
            copy.wait_send()
        for k in range(4):
            line = (y + 4 - k) % 4
            remote(own.at[line], prior.at[line], far_send.at[k], far_recv.at[k], time_pos, row_pos).wait_recv()


def step_kernel(own, own_vec, *refs, count, distance, parts):
    prior_refs, refs = refs[:count], refs[count:]
    prior_vec, inverse, shifted, new, new_vec = refs[:5]
    got, got_vec = refs[5 : 5 + parts], refs[5 + parts]
    packed, refs = refs[6 + parts : 8 + parts], refs[8 + parts :]
    far_send, far_recv, send, recv, twin_send, twin_recv, vec_send, vec_recv = refs[:8]
    tools = Tools(refs[8:])
    prior = prior_refs[0] if count == 1 else prior_refs
    z, core, y, x = places()
    time_pos, row_pos = lax.axis_index("tm"), lax.axis_index("row")
    reach, relay = distance, distance == 2
    barrier = pltpu.get_barrier_semaphore()
    target = (z // reach) % 2 == 1
    source = ((z // reach) % 2 == 0) & (z % reach == reach - 1) & (core == 1)
    source_pos = ((z // reach) * reach) * 2 - 1
    outer_pos = (1 - core) * y + core * x
    hops = 1 if relay else reach
    onward = target & ((z % reach) < reach - 1) if relay else None
    present = (time_pos // distance) % 2 == 1
    twin = 2 * z + 1 - core

    def view(ref, side, line):
        rows = ref.shape[0] // 8
        return ref.at[pl.ds(pl.multiple_of((side * 4 + line) * rows, 8), rows)]

    def outer_row(k):
        place = (outer_pos + k) % 4
        return (1 - core) * (place * 4 + x) + core * (y * 4 + place)

    @pl.when(target)
    def _():
        if relay:
            greet(barrier, (z % reach == 0) * source_pos + (z % reach != 0) * (time_pos - 2), row_pos)
        else:
            greet(barrier, source_pos, row_pos)
        for k in (1, 2, 3):
            greet(barrier, time_pos, outer_row(k))
        greet(barrier, twin, row_pos)

    @pl.when(present)
    def _():
        combine_cov(own, prior, inverse, new, tools)

    def deliver(part):
        for step in reversed(range(hops)):
            for side in range(2):
                slot = 2 * step + side
                line = y if side == 0 else x
                yield remote(
                    view(packed[part], side, line),
                    view(got[part], side, line),
                    far_send.at[part * 8 + slot],
                    far_recv.at[part],
                    time_pos + 1 + slot,
                    row_pos,
                )

    def deliver_vec():
        for slot in reversed(range(2 * hops)):
            yield remote(new_vec, got_vec, vec_send.at[slot], vec_recv, time_pos + 1 + slot, row_pos)

    @pl.when(source)
    def _():
        pack(new, packed, 0)
        pl.semaphore_wait(barrier, 2 * hops)
        for copy in deliver(0):
            copy.start()

    @pl.when(present)
    def _():
        combine_rest(own, own_vec, prior, prior_vec, inverse, shifted[0:1, :], new, new_vec, tools)

    @pl.when(jnp.logical_not(present))
    def _():
        new[...] = own[...]
        new_vec[...] = own_vec[...]

    @pl.when(source)
    def _():
        for copy in deliver_vec():
            copy.start()
        if parts > 1:
            pack(new, packed, 2)
            pack(new, packed, 1)
            for copy in deliver(1):
                copy.start()
        for part in range(parts):
            for copy in deliver(part):
                copy.wait_send()
        for copy in deliver_vec():
            copy.wait_send()

    def onto(part):
        mine = view(got[part], core, outer_pos)
        return remote(mine, mine, far_send.at[part * 8], far_recv.at[part], time_pos + 2, row_pos)

    @pl.when(target)
    def _():
        if relay:

            @pl.when(onward)
            def _():
                pl.semaphore_wait(barrier, 5)

            @pl.when(jnp.logical_not(onward))
            def _():
                pl.semaphore_wait(barrier, 4)

        else:
            pl.semaphore_wait(barrier, 4)
        copies = []

        def over(k, part):
            mine = view(got[part], core, (outer_pos + 4 - k) % 4)
            slot = k * parts + part
            copy = remote(mine, mine, twin_send.at[slot], twin_recv.at[slot], twin, row_pos)
            copy.start()
            copies.append(copy)

        def pass_vec():
            arrived = remote(got_vec, got_vec, vec_send.at[0], vec_recv, time_pos + 2, row_pos)
            arrived.wait_recv()
            if relay:

                @pl.when(onward)
                def _():
                    arrived.start()

        for part in range(parts):
            onto(part).wait_recv()
            if relay:

                @pl.when(onward)
                def _():
                    onto(part).start()

            mine = view(got[part], core, outer_pos)
            for k in range(1, 4):
                slot = (k - 1) * parts + part
                copy = remote(mine, mine, send.at[slot], recv.at[slot], time_pos, outer_row(k))
                copy.start()
                copies.append(copy)
            over(0, part)
        pass_vec()
        for part in range(parts):
            for k in (1, 3, 2):
                line = view(got[part], core, (outer_pos + 4 - k) % 4)
                slot = (k - 1) * parts + part
                remote(line, line, send.at[slot], recv.at[slot], time_pos, outer_row(k)).wait_recv()
                over(k, part)
        for k in range(4):
            for part in range(parts):
                theirs = view(got[part], 1 - core, 0)
                slot = k * parts + part
                remote(theirs, theirs, twin_send.at[slot], twin_recv.at[slot], twin, row_pos).wait_recv()
        for copy in copies:
            copy.wait_send()
        if relay:

            @pl.when(onward)
            def _():
                remote(got_vec, got_vec, vec_send.at[0], vec_recv, time_pos + 2, row_pos).wait_send()
                for part in range(parts):
                    onto(part).wait_send()


def chain_kernel(gain, offset, smooth, near_gain, near_offset, held, sent, state, *rest):
    refs, (send, recv) = rest[:-2], rest[-2:]
    product, one, two = refs
    z, core, _, _ = places()
    time_pos, row_pos = lax.axis_index("tm"), lax.axis_index("row")
    size = gain.shape[0]
    barrier = pltpu.get_barrier_semaphore()
    first, last = core == 0, z == 7

    @pl.when(first)
    def _():
        greet(barrier, time_pos + 1, row_pos)

    @pl.when(jnp.logical_not(last))
    def _():
        greet(barrier, 2 * z + 2, row_pos)

    put(two, gain[...])
    link = remote(gain, near_gain, send.at[0], recv.at[0], 2 * z, row_pos)
    small = remote(offset, near_offset, send.at[1], recv.at[1], 2 * z, row_pos)

    def apply(row8):
        high = row8.astype(BF16).astype(F32)
        both = jnp.concatenate([high, row8 - high], axis=0).astype(BF16)
        result = dot(both, two[0])
        return result[:8] + result[8:] + dot(both, two[1])[:8]

    @pl.when(core == 1)
    def _():
        pl.semaphore_wait(barrier, 1)
        small.start()

        @pl.when(jnp.logical_not(last))
        def _():
            link.start()

        state[...] = offset[...]

    @pl.when(first & (z > 0))
    def _():
        pl.semaphore_wait(barrier, 2)

    @pl.when(first & last)
    def _():
        small.wait_recv()
        state[...] = apply(near_offset[...]) + offset[...]

    @pl.when(first & jnp.logical_not(last))
    def _():
        small.wait_recv()
        state[...] = apply(near_offset[...]) + offset[...]
        link.wait_recv()
        put(one, near_gain[...])

        def part(index, carry):
            columns = pl.ds(pl.multiple_of(index * 256, 256), 256)
            high, low = two[0, :, columns], two[1, :, columns]
            product[:, columns] = dot(one[0], high) + dot(one[0], low) + dot(one[1], high)
            return carry

        lax.fori_loop(0, size // 256, part, 0)
        put(two, product[...])

    @pl.when(jnp.logical_not(last))
    def _():
        remote(held, held, send.at[2], recv.at[2], time_pos, row_pos).wait_recv()
        state[...] = state[...] + apply(held[...])

    @pl.when(first & (z > 0))
    def _():
        sent[...] = state[...]
        copies = [remote(sent, held, send.at[2 + k], recv.at[2], 2 * z - 2 + k, row_pos) for k in range(2)]
        for copy in copies:
            copy.start()
        for copy in copies:
            copy.wait_send()

    share(smooth, state[0:1, :], row_pos)

    @pl.when(core == 1)
    def _():
        small.wait_send()

        @pl.when(jnp.logical_not(last))
        def _():
            link.wait_send()


def body(trans, mean, cov, info, pull, dynamics, noise):
    piece, size = trans.shape[1:]
    shape = jax.ShapeDtypeStruct
    vmem = pl.BlockSpec(memory_space=pltpu.VMEM)
    dma = pltpu.SemaphoreType.DMA

    def params(mib, **more):
        return pltpu.CompilerParams(vmem_limit_bytes=mib * MIB, **more)

    hbm = pl.BlockSpec(memory_space=pltpu.HBM)
    slab = shape((4, 4, 10 * piece + 8, LANES), F32)
    mats_shape, vecs_shape = shape((3, size, size), F32), shape((8, LANES), F32)
    pair_shape, row_shape = shape((2, size, size), BF16), shape((8, size), F32)
    part_shapes = shape((10 * LANES, LANES), F32), shape((26 * LANES, LANES), F32)
    own_slabs, prior_slabs = pl.pallas_call(
        gather_kernel,
        out_shape=(slab, slab),
        in_specs=[hbm] * 5,
        out_specs=(vmem, vmem),
        scratch_shapes=[pltpu.VMEM(array.shape, F32) for array in (trans[0], mean, cov[0], info[0], pull)]
        + [dma((5,)), dma((6,)), dma((6,)), dma((4,)), dma((4,))],
        compiler_params=params(12, collective_id=0, has_side_effects=True),
    )(trans[0], mean, cov[0], info[0], pull)

    mats, vecs, got, got_vec, inverse, shifted = pl.pallas_call(
        first_kernel,
        out_shape=(mats_shape, vecs_shape, mats_shape, vecs_shape, pair_shape, row_shape),
        in_specs=[vmem] * 2,
        out_specs=(vmem,) * 6,
        scratch_shapes=scratch_tools(size),
        compiler_params=params(28),
    )(own_slabs, prior_slabs)
    got = [got]

    for distance in (1, 2, 4):
        parts = 2 if distance < 4 else 1
        hops = 1 if distance < 4 else 4
        mats, vecs, *got_parts, new_vec = pl.pallas_call(
            functools.partial(step_kernel, count=len(got), distance=distance, parts=parts),
            out_shape=(mats_shape, vecs_shape, *part_shapes[:parts], vecs_shape),
            in_specs=[vmem] * (5 + len(got)),
            out_specs=(vmem,) * (3 + parts),
            scratch_shapes=[pltpu.VMEM(part.shape, F32) for part in part_shapes]
            + [dma((8 * parts,)), dma((parts,))]
            + [dma((3 * parts,))] * 2
            + [dma((4 * parts,))] * 2
            + [dma((2 * hops,)), dma]
            + scratch_tools(size),
            compiler_params=params(28, collective_id=1 + distance, has_side_effects=True),
        )(mats, vecs, *got, got_vec, inverse, shifted)
        got, got_vec = got_parts, new_vec
        if distance < 4:
            inverse, shifted = pl.pallas_call(
                functools.partial(level_kernel, distance=2 * distance),
                out_shape=(pair_shape, row_shape),
                in_specs=[vmem] * 5,
                out_specs=(vmem,) * 2,
                scratch_shapes=scratch_tools(size),
                compiler_params=params(28),
            )(mats, vecs, *got, got_vec)

    gain, offset, cov_out, mean_out = pl.pallas_call(
        functools.partial(gain_kernel, distance=8),
        out_shape=(
            shape((size, size), F32),
            shape((8, size), F32),
            shape((piece, size), F32),
            shape((1, piece), F32),
        ),
        in_specs=[vmem] * 6,
        out_specs=(vmem,) * 4,
        scratch_shapes=[pltpu.VMEM((1, size, size), F32), pltpu.VMEM((8, LANES), F32)] + scratch_tools(size),
        compiler_params=params(28),
    )(mats, vecs, *got, got_vec, dynamics[0], noise[0])

    smooth = pl.pallas_call(
        chain_kernel,
        out_shape=shape((1, piece), F32),
        in_specs=[vmem] * 2,
        out_specs=vmem,
        scratch_shapes=[
            pltpu.VMEM((size, size), F32),
            pltpu.VMEM((8, size), F32),
            pltpu.VMEM((8, size), F32),
            pltpu.VMEM((8, size), F32),
            pltpu.VMEM((8, size), F32),
            pltpu.VMEM((size, size), F32),
            pltpu.VMEM((2, size, size), BF16),
            pltpu.VMEM((2, size, size), BF16),
            dma((4,)),
            dma((3,)),
        ],
        compiler_params=params(12, collective_id=1, has_side_effects=True),
    )(gain, offset)

    return smooth, mean_out, cov_out[None]


def solution(mesh):
    in_specs = (
        P("tm", "row", None),
        P("tm", "row"),
        P("tm", "row", None),
        P("tm", "row", None),
        P("tm", "row"),
        P("tm", None, None),
        P("tm", None, None),
    )
    out_specs = (P("tm", "row"), P("tm", "row"), P("tm", "row", None))
    return jax.shard_map(body, mesh=mesh, in_specs=in_specs, out_specs=out_specs, check_vma=False)
```

```python
import functools

import jax
import jax.numpy as jnp
from jax import lax
from jax.experimental import pallas as pl
from jax.experimental.pallas import tpu as pltpu
from jax.sharding import PartitionSpec as P

MESH = pl.DeviceIdType.MESH
F32, BF16 = jnp.float32, jnp.bfloat16
NN = (((1,), (0,)), ((), ()))
NT = (((1,), (1,)), ((), ()))
TN = (((0,), (0,)), ((), ()))
VROWS = 16
LANES = 128
REACH = 0.008
SMALL = 4e-3
STEPS = 4
MIB = 1024 * 1024


def places():
    time_pos, row_pos = lax.axis_index("tm"), lax.axis_index("row")
    return time_pos // 2, time_pos % 2, row_pos // 4, row_pos % 4


def dot(lhs, rhs, dims=NN):
    return lax.dot_general(lhs, rhs, dims, preferred_element_type=F32)


def put(pair, value, start=0, column=0):
    high = value.astype(BF16)
    rows, columns = pl.ds(start, value.shape[0]), pl.ds(column, value.shape[1])
    pair[0, rows, columns] = high
    pair[1, rows, columns] = (value - high.astype(F32)).astype(BF16)


def put_high(pair, value):
    pair[0, : value.shape[0], :] = value.astype(BF16)


class Tools:
    def __init__(self, refs):
        self.product, self.value, *self.pairs = refs
        self.size = self.value.shape[0]

    def times(self, lhs, rhs, dims=NN, rows=None):
        size = self.size
        rows = lhs.shape[1] if rows is None else rows
        high, low = rhs[0, :size, :], rhs[1, :size, :]
        left = lhs[0, :rows, :]
        return dot(left, high, dims) + dot(left, low, dims) + dot(lhs[1, :rows, :], high, dims)

    def thin(self, lhs, rhs):
        size = self.size
        high = lhs.astype(BF16)
        low = (lhs - high.astype(F32)).astype(BF16)
        return dot(high, rhs[0, :size, :]) + dot(high, rhs[1, :size, :]) + dot(low, rhs[0, :size, :])


def scratch_tools(size):
    tall = size + VROWS
    return [pltpu.VMEM((tall, size), F32), pltpu.VMEM((size, size), F32)] + [
        pltpu.VMEM((2, tall if index in (0, 4, 5) else size, size), BF16) for index in range(6)
    ]


def eye(size):
    rows = lax.broadcasted_iota(jnp.int32, (size, size), 0)
    return (rows == lax.broadcasted_iota(jnp.int32, (size, size), 1)).astype(F32)


class Newton:
    def __init__(self, tools, upper, lower, out, mat, work):
        self.tools, self.size, self.value, self.product = tools, tools.size, tools.value, tools.product
        self.out, self.mat, self.work = out, mat, work
        self.first = 2.0 / (upper + lower)
        self.opening = (upper - lower) / (upper + lower)

    @staticmethod
    def scale_of(bound):
        return 2.0 / (2.0 - bound * bound)

    def after(self, bound):
        return bound * bound * 0.5 * self.scale_of(bound)

    def start(self):
        whole = self.mat[0].astype(F32) + self.mat[1].astype(F32)
        new = (self.scale_of(self.opening) * self.first) * (2.0 * eye(self.size) - self.first * whole)
        self.value[...] = new
        put(self.out, new)
        return self.after(self.opening)

    def coarse(self, bound):
        size, out, work = self.size, self.out, self.work
        put_high(work, eye(size) - dot(self.mat[0], out[0]))
        new = self.scale_of(bound) * (self.value[...] + dot(out[0], work[0, :size, :]))
        self.value[...] = new
        put_high(out, new)
        return self.after(bound)

    def add(self, lhs, rhs, sign):
        size, product = self.size, self.product

        def one(index, carry):
            product[:size, :] += sign * dot(lhs[index // 2, :size, :], rhs[index % 2, :size, :])
            return carry

        lax.fori_loop(0, 3, one, 0)

    def careful(self, bound):
        size, product = self.size, self.product
        product[:size, :] = eye(size)
        self.add(self.mat, self.out, -1.0)
        put(self.work, product[:size, :])
        product[:size, :] = self.value[...]
        self.add(self.out, self.work, 1.0)
        self.settle(self.scale_of(bound) * product[:size, :])
        return self.after(bound)

    def settle(self, new):
        self.value[...] = new
        put(self.out, new)

    def check(self):
        residual = eye(self.size) - self.tools.times(self.mat, self.out)
        self.product[: self.size, :] = residual
        put_high(self.work, residual)
        return jnp.sum(residual * residual)

    def step(self):
        self.settle(self.value[...] + dot(self.out[0], self.work[0, : self.size, :]))

    def last_step(self):
        small = self.work[0, : self.size, :]
        put_high(self.work, self.product[: self.size, :] + dot(small, small))
        put(self.out, self.value[...] + dot(self.out[0], self.work[0, : self.size, :]))

    def whole(self):
        def from_start(error):
            lax.while_loop(lambda bound: bound > REACH, self.careful, self.start())
            return self.check()

        def again(carry):
            self.step()
            return carry[0] + 1, self.check()

        lax.while_loop(lambda bound: bound > REACH, self.coarse, self.start())
        put(self.out, self.value[...])
        error = self.check()
        error = lax.cond(error < 1.0, lambda e: e, from_start, error)
        lax.while_loop(lambda c: (c[0] < 60) & (c[1] > SMALL), again, (jnp.int32(0), error))
        self.last_step()

    def fixed(self):
        lax.fori_loop(0, STEPS, lambda _, bound: self.coarse(bound), self.start())
        put(self.out, self.value[...])
        error = self.check()
        self.last_step()
        return error


def one_norm(matrix):
    return jnp.max(jnp.sum(jnp.abs(matrix), axis=0, keepdims=True))


def spread(row):
    return jnp.broadcast_to(row, (VROWS, row.shape[1]))


def row_of(tile, start):
    return jnp.concatenate([tile[start + i : start + i + 1, :] for i in range(4)], axis=1)


def set_row(tile, start, row):
    for i in range(4):
        tile[start + i : start + i + 1, :] = row[0:1, i * LANES : (i + 1) * LANES]


UPPER = [(i, j) for i in range(4) for j in range(i, 4)]
FULL = [(i, j) for i in range(4) for j in range(4)]
BLOCKS = {0: (0, 0, UPPER), 2: (1, 0, UPPER), 1: (1, 10, FULL)}


def each_block(packed, which):
    part, base, places_of = BLOCKS[which]
    for index, (i, j) in enumerate(places_of):
        value = packed[part][pl.ds((base + index) * LANES, LANES), :]
        yield i * LANES, j * LANES, value
        if places_of is UPPER and i != j:
            yield j * LANES, i * LANES, value.T


def pack(mats, packed, which):
    part, base, places_of = BLOCKS[which]
    for index, (i, j) in enumerate(places_of):
        packed[part][pl.ds((base + index) * LANES, LANES), :] = mats[
            which, pl.ds(i * LANES, LANES), pl.ds(j * LANES, LANES)
        ]


def fill(prior, which, pair):
    if isinstance(prior, tuple):
        for i, j, value in each_block(prior, which):
            put(pair, value, i, j)
    else:
        put(pair, prior[which])


def increase(mats, which, prior):
    if isinstance(prior, tuple):
        for i, j, value in each_block(prior, which):
            rows, columns = pl.ds(i, LANES), pl.ds(j, LANES)
            mats[which, rows, columns] = mats[which, rows, columns] + value
    else:
        mats[which] = mats[which] + prior[which]


def couple(own, own_vec, prior, inverse, tools):
    size = tools.size
    one, two, three, four, five, six = tools.pairs
    put(one, own[2])
    put(one, spread(row_of(own_vec, 4)), size)
    fill(prior, 0, two)
    coupling = tools.times(one, two)
    pulled = coupling[size : size + 1]
    coupling = coupling[:size]
    upper = 2.0 + one_norm(coupling)
    put(four, eye(size) + coupling)
    return Newton(tools, upper, 1.0, inverse, four, five), pulled


def combine_cov(own, prior, inverse, new, tools):
    times = tools.times
    one, two, three, four, five, six = tools.pairs
    fill(prior, 0, two)
    put(four, own[1])
    put(five, times(two, inverse))
    put(six, times(five, four, rows=tools.size))
    new[0] = times(four, six, TN) + own[0]


def combine_rest(own, own_vec, prior, prior_vec, inverse, pulled_row, new, new_vec, tools):
    size, times = tools.size, tools.times
    one, two, three, four, five, six = tools.pairs
    prior_mean, prior_pull = row_of(prior_vec, 0), row_of(prior_vec, 4)
    mean, pull = row_of(own_vec, 0), row_of(own_vec, 4)
    fill(prior, 1, five)
    put(five, spread(prior_mean + pulled_row), size)
    gained = times(five, inverse)
    put(two, gained[:size])
    put(six, gained)
    moved = times(six, four)
    new[1] = moved[:size]
    set_row(new_vec, 0, moved[size : size + 1] + mean)
    put(three, own[2])
    put(five, spread(prior_mean), size)
    pulled = times(five, three)
    put(six, pulled[:size])
    put(six, spread(pull - pulled[size : size + 1]), size)
    informed = times(six, two, NT)
    new[2] = informed[:size]
    increase(new, 2, prior)
    set_row(new_vec, 4, informed[size : size + 1] + prior_pull)


def unpack(slabs, mats, vecs):
    piece = mats.shape[1] // 16
    for y in range(4):
        total = None
        for x in range(4):
            rows = pl.ds((4 * y + x) * piece, piece)
            for index in range(10):
                which = 1 if index < 4 else 0 if index < 7 else 2
                group = index if index < 4 else (y + (index - 4) % 3) % 4
                mats[which, rows, pl.ds(group * LANES, LANES)] = slabs[y, x, pl.ds(index * piece, piece), :]
            tile = slabs[y, x, pl.ds(10 * piece, 8), :]
            total = tile if total is None else total + tile
        vecs[y : y + 1, :] = total[0:1, :]
        vecs[4 + y : 5 + y, :] = total[1:2, :]
    mats[1] = mats[1].T
    for which in (0, 2):
        for y in range(4):
            left, right = pl.ds(y * LANES, LANES), pl.ds((y + 3) % 4 * LANES, LANES)
            mats[which, left, right] = mats[which, right, left].T


def first_kernel(own_slabs, prior_slabs, own, own_vec, prior, prior_vec, inverse, pulled, *refs):
    odd = lax.axis_index("tm") % 2 == 1
    unpack(own_slabs, own, own_vec)

    @pl.when(odd)
    def _():
        unpack(prior_slabs, prior, prior_vec)
        newton, row = couple(own, own_vec, prior, inverse, Tools(refs))
        pulled[...] = spread(row)[:8]
        newton.whole()


def repair_kernel(own, own_vec, prior_cov, found, error, inverse, *refs, distance):
    @pl.when((lax.axis_index("tm") // distance) % 2 == 1)
    def _():
        @pl.when(jnp.logical_not(jnp.max(error[...]) < SMALL))
        def _():
            newton, _ = couple(own, own_vec, (prior_cov,), inverse, Tools(refs))
            newton.whole()


def gain_kernel(
    own, own_vec, prior_cov, prior_vec, dynamics, noise, gain, offset, cov_out, mean_out, new, mean_tile, *refs, distance
):
    tools = Tools(refs)
    size, times, thin = tools.size, tools.times, tools.thin
    time_pos, row_pos = lax.axis_index("tm"), lax.axis_index("row")
    present = (time_pos // distance) % 2 == 1
    one, two, three, four, five, six = tools.pairs

    @pl.when(present)
    def _():
        prior = (prior_cov,)
        newton, row = couple(own, own_vec, prior, three, tools)
        newton.whole()
        combine_cov(own, prior, three, new, tools)
        moved = thin(thin(spread(row_of(prior_vec, 0) + row), three), four)
        set_row(mean_tile, 0, moved[0:1] + row_of(own_vec, 0))

    @pl.when(jnp.logical_not(present))
    def _():
        new[0] = own[0]
        mean_tile[...] = own_vec[...]

    piece = cov_out.shape[0]
    cov_out[...] = new[0, pl.ds(pl.multiple_of(row_pos * piece, piece), piece), :]
    mean = row_of(mean_tile, 0)
    share(mean_out, mean, row_pos)

    @pl.when(time_pos == 15)
    def _():
        gain[...] = jnp.zeros_like(gain)
        offset[...] = jnp.broadcast_to(mean, offset.shape)

    @pl.when(time_pos < 15)
    def _():
        put(two, dynamics[...])
        put(three, new[0])
        put(one, times(two, three))
        put(one, spread(mean), size)
        projected = times(one, two, NT)
        predicted = projected[size:]
        innovation = projected[:size] + noise[...]
        upper = one_norm(innovation)
        put(four, innovation)
        Newton(tools, upper, upper * 0.004, three, four, two).whole()
        weights = times(three, one)
        gain[...] = weights
        put(six, weights)
        offset[...] = mean - thin(predicted, six)[:8]


def share(out, row, row_pos):
    piece = out.shape[1]
    for index in range(16):

        @pl.when(row_pos == index)
        def _():
            out[...] = row[0:1, index * piece : (index + 1) * piece]


def remote(src, dst, send, recv, tm, row):
    return pltpu.make_async_remote_copy(
        src_ref=src, dst_ref=dst, send_sem=send, recv_sem=recv, device_id=(tm, row), device_id_type=MESH
    )


def greet(barrier, tm, row):
    pl.semaphore_signal(barrier, inc=1, device_id=(tm, row), device_id_type=MESH)


def gather_kernel(rows, own, prior, send, recv, far_send, far_recv):
    z, core, y, x = places()
    time_pos, row_pos = lax.axis_index("tm"), lax.axis_index("row")
    piece = (rows.shape[0] - 8) // 3
    keep = (time_pos > 0).astype(F32)
    barrier = pltpu.get_barrier_semaphore()
    across = [y * 4 + (x + k) % 4 for k in (1, 2, 3)]
    along = [((y + k) % 4) * 4 + x for k in (1, 2, 3)]
    for peer in across + along:
        greet(barrier, time_pos, peer)

    @pl.when(core == 1)
    def _():
        greet(barrier, time_pos - 1, row_pos)

    for index in range(4):
        columns = pl.ds(index * LANES, LANES)
        own[y, x, pl.ds(index * piece, piece), :] = rows[pl.ds(0, piece), columns] * keep
    for index in range(3):
        columns = pl.ds(pl.multiple_of((y + index) % 4 * LANES, LANES), LANES)
        own[y, x, pl.ds((4 + index) * piece, piece), :] = rows[pl.ds(piece, piece), columns]
        own[y, x, pl.ds((7 + index) * piece, piece), :] = rows[pl.ds(2 * piece, piece), columns] * keep
    own[y, x, pl.ds(10 * piece, 8), :] = jnp.zeros((8, LANES), F32)
    for index in range(4):

        @pl.when(x == index)
        def _():
            lanes = pl.ds(index * piece, piece)
            own[y, x, pl.ds(10 * piece, 1), lanes] = rows[pl.ds(3 * piece, 1), :piece]
            own[y, x, pl.ds(10 * piece + 1, 1), lanes] = rows[pl.ds(3 * piece + 1, 1), :piece] * keep

    def gather(near, other, line):
        copies = []
        for k in range(3):
            copy = remote(own.at[y, x], own.at[y, x], send.at[k], recv.at[k], time_pos, near[k])
            copy.start()
            copies.append(copy)
        for copy in copies:
            copy.wait_recv()
        later = []
        for k in range(3):
            copy = remote(line, line, send.at[3 + k], recv.at[3 + k], time_pos, other[k])
            copy.start()
            later.append(copy)
        return copies, later

    @pl.when(core == 0)
    def _():
        pl.semaphore_wait(barrier, 7)
        copies, later = gather(across, along, own.at[y])
        passed = []
        for k in range(4):
            if k:
                later[k - 1].wait_recv()
            line = (y + 4 - k) % 4
            copy = remote(own.at[line], prior.at[line], far_send.at[k], far_recv.at[k], time_pos + 1, row_pos)
            copy.start()
            passed.append(copy)
        for copy in copies + later + passed:
            copy.wait_send()

    @pl.when(core == 1)
    def _():
        pl.semaphore_wait(barrier, 6)
        copies, later = gather(along, across, own.at[:, x])
        for copy in later:
            copy.wait_recv()
        for copy in copies + later:
            copy.wait_send()
        for k in range(4):
            line = (y + 4 - k) % 4
            remote(own.at[line], prior.at[line], far_send.at[k], far_recv.at[k], time_pos, row_pos).wait_recv()


def step_kernel(own, own_vec, *refs, count, distance, parts):
    prior_refs, refs = refs[:count], refs[count:]
    prior_vec, inverse, pulled, new, new_vec = refs[:5]
    got, got_vec, refs = refs[5 : 5 + parts], refs[5 + parts], refs[6 + parts :]
    if parts > 1:
        next_inverse, next_pulled, error, *refs = refs
    packed, refs = refs[:2], refs[2:]
    far_send, far_recv, send, recv, twin_send, twin_recv, vec_send, vec_recv = refs[:8]
    tools = Tools(refs[8:])
    prior = prior_refs[0] if count == 1 else prior_refs
    z, core, y, x = places()
    time_pos, row_pos = lax.axis_index("tm"), lax.axis_index("row")
    reach, relay = distance, distance == 2
    barrier = pltpu.get_barrier_semaphore()
    target = (z // reach) % 2 == 1
    source = ((z // reach) % 2 == 0) & (z % reach == reach - 1) & (core == 1)
    source_pos = ((z // reach) * reach) * 2 - 1
    outer_pos = (1 - core) * y + core * x
    hops = 1 if relay else reach
    onward = target & ((z % reach) < reach - 1) if relay else None
    present = (time_pos // distance) % 2 == 1
    twin = 2 * z + 1 - core

    def view(ref, side, line):
        rows = ref.shape[0] // 8
        return ref.at[pl.ds(pl.multiple_of((side * 4 + line) * rows, 8), rows)]

    def outer_row(k):
        place = (outer_pos + k) % 4
        return (1 - core) * (place * 4 + x) + core * (y * 4 + place)

    @pl.when(target)
    def _():
        if relay:
            greet(barrier, (z % reach == 0) * source_pos + (z % reach != 0) * (time_pos - 2), row_pos)
        else:
            greet(barrier, source_pos, row_pos)
        for k in (1, 2, 3):
            greet(barrier, time_pos, outer_row(k))
        greet(barrier, twin, row_pos)

    @pl.when(present)
    def _():
        combine_cov(own, prior, inverse, new, tools)

    def deliver(part):
        for step in reversed(range(hops)):
            for side in range(2):
                slot = 2 * step + side
                line = y if side == 0 else x
                yield remote(
                    view(packed[part], side, line),
                    view(got[part], side, line),
                    far_send.at[part * 8 + slot],
                    far_recv.at[part],
                    time_pos + 1 + slot,
                    row_pos,
                )

    def deliver_vec():
        for slot in reversed(range(2 * hops)):
            yield remote(new_vec, got_vec, vec_send.at[slot], vec_recv, time_pos + 1 + slot, row_pos)

    @pl.when(source)
    def _():
        pack(new, packed, 0)
        pl.semaphore_wait(barrier, 2 * hops)
        for copy in deliver(0):
            copy.start()

    @pl.when(present)
    def _():
        combine_rest(own, own_vec, prior, prior_vec, inverse, pulled[0:1, :], new, new_vec, tools)

    @pl.when(jnp.logical_not(present))
    def _():
        new[...] = own[...]
        new_vec[...] = own_vec[...]

    @pl.when(source)
    def _():
        for copy in deliver_vec():
            copy.start()
        if parts > 1:
            pack(new, packed, 2)
            pack(new, packed, 1)
            for copy in deliver(1):
                copy.start()
        for part in range(parts):
            for copy in deliver(part):
                copy.wait_send()
        for copy in deliver_vec():
            copy.wait_send()

    def onto(part):
        mine = view(got[part], core, outer_pos)
        return remote(mine, mine, far_send.at[part * 8], far_recv.at[part], time_pos + 2, row_pos)

    @pl.when(target)
    def _():
        if relay:

            @pl.when(onward)
            def _():
                pl.semaphore_wait(barrier, 5)

            @pl.when(jnp.logical_not(onward))
            def _():
                pl.semaphore_wait(barrier, 4)

        else:
            pl.semaphore_wait(barrier, 4)
        copies = []

        def over(k, part):
            mine = view(got[part], core, (outer_pos + 4 - k) % 4)
            slot = k * parts + part
            copy = remote(mine, mine, twin_send.at[slot], twin_recv.at[slot], twin, row_pos)
            copy.start()
            copies.append(copy)

        def pass_vec():
            arrived = remote(got_vec, got_vec, vec_send.at[0], vec_recv, time_pos + 2, row_pos)
            arrived.wait_recv()
            if relay:

                @pl.when(onward)
                def _():
                    arrived.start()

        def enter(part):
            onto(part).wait_recv()
            if relay:

                @pl.when(onward)
                def _():
                    onto(part).start()

            mine = view(got[part], core, outer_pos)
            for k in range(1, 4):
                slot = (k - 1) * parts + part
                copy = remote(mine, mine, send.at[slot], recv.at[slot], time_pos, outer_row(k))
                copy.start()
                copies.append(copy)
            over(0, part)

        def complete(part):
            for k in (1, 3, 2):
                line = view(got[part], core, (outer_pos + 4 - k) % 4)
                slot = (k - 1) * parts + part
                remote(line, line, send.at[slot], recv.at[slot], time_pos, outer_row(k)).wait_recv()
                over(k, part)
            for k in range(4):
                theirs = view(got[part], 1 - core, 0)
                slot = k * parts + part
                remote(theirs, theirs, twin_send.at[slot], twin_recv.at[slot], twin, row_pos).wait_recv()

        enter(0)
        complete(0)
        if parts > 1:
            newton, row = couple(new, new_vec, (got[0],), next_inverse, tools)
            next_pulled[...] = spread(row)[:8]
            enter(1)
            pass_vec()
            error[...] = jnp.zeros_like(error) + newton.fixed()
            complete(1)
        else:
            pass_vec()
        for copy in copies:
            copy.wait_send()
        if relay:

            @pl.when(onward)
            def _():
                remote(got_vec, got_vec, vec_send.at[0], vec_recv, time_pos + 2, row_pos).wait_send()
                for part in range(parts):
                    onto(part).wait_send()


def chain_kernel(gain, offset, smooth, near_gain, near_offset, held, sent, state, *rest):
    refs, (send, recv) = rest[:-2], rest[-2:]
    product, one, two = refs
    z, core, _, _ = places()
    time_pos, row_pos = lax.axis_index("tm"), lax.axis_index("row")
    size = gain.shape[0]
    barrier = pltpu.get_barrier_semaphore()
    first, last = core == 0, z == 7

    @pl.when(first)
    def _():
        greet(barrier, time_pos + 1, row_pos)

    @pl.when(jnp.logical_not(last))
    def _():
        greet(barrier, 2 * z + 2, row_pos)

    put(two, gain[...])
    link = remote(gain, near_gain, send.at[0], recv.at[0], 2 * z, row_pos)
    small = remote(offset, near_offset, send.at[1], recv.at[1], 2 * z, row_pos)

    def apply(row8):
        high = row8.astype(BF16).astype(F32)
        both = jnp.concatenate([high, row8 - high], axis=0).astype(BF16)
        result = dot(both, two[0])
        return result[:8] + result[8:] + dot(both, two[1])[:8]

    @pl.when(core == 1)
    def _():
        pl.semaphore_wait(barrier, 1)
        small.start()

        @pl.when(jnp.logical_not(last))
        def _():
            link.start()

        state[...] = offset[...]

    @pl.when(first & (z > 0))
    def _():
        pl.semaphore_wait(barrier, 2)

    @pl.when(first & last)
    def _():
        small.wait_recv()
        state[...] = apply(near_offset[...]) + offset[...]

    @pl.when(first & jnp.logical_not(last))
    def _():
        small.wait_recv()
        state[...] = apply(near_offset[...]) + offset[...]
        link.wait_recv()
        put(one, near_gain[...])

        def part(index, carry):
            columns = pl.ds(pl.multiple_of(index * 256, 256), 256)
            high, low = two[0, :, columns], two[1, :, columns]
            product[:, columns] = dot(one[0], high) + dot(one[0], low) + dot(one[1], high)
            return carry

        lax.fori_loop(0, size // 256, part, 0)
        put(two, product[...])

    @pl.when(jnp.logical_not(last))
    def _():
        remote(held, held, send.at[2], recv.at[2], time_pos, row_pos).wait_recv()
        state[...] = state[...] + apply(held[...])

    @pl.when(first & (z > 0))
    def _():
        sent[...] = state[...]
        copies = [remote(sent, held, send.at[2 + k], recv.at[2], 2 * z - 2 + k, row_pos) for k in range(2)]
        for copy in copies:
            copy.start()
        for copy in copies:
            copy.wait_send()

    share(smooth, state[0:1, :], row_pos)

    @pl.when(core == 1)
    def _():
        small.wait_send()

        @pl.when(jnp.logical_not(last))
        def _():
            link.wait_send()


def body(trans, mean, cov, info, pull, dynamics, noise):
    piece, size = trans.shape[1:]
    shape = jax.ShapeDtypeStruct
    vmem = pl.BlockSpec(memory_space=pltpu.VMEM)
    dma = pltpu.SemaphoreType.DMA

    def params(mib, **more):
        return pltpu.CompilerParams(vmem_limit_bytes=mib * MIB, **more)

    slab = shape((4, 4, 10 * piece + 8, LANES), F32)
    mats_shape, vecs_shape = shape((3, size, size), F32), shape((8, LANES), F32)
    pair_shape, row_shape = shape((2, size, size), BF16), shape((8, size), F32)
    part_shapes = shape((10 * LANES, LANES), F32), shape((26 * LANES, LANES), F32)
    lines = jnp.pad(jnp.concatenate([mean, pull]), ((0, 6), (0, size - piece)))
    own_slabs, prior_slabs = pl.pallas_call(
        gather_kernel,
        out_shape=(slab, slab),
        in_specs=[vmem],
        out_specs=(vmem, vmem),
        scratch_shapes=[dma((6,)), dma((6,)), dma((4,)), dma((4,))],
        compiler_params=params(12, collective_id=0, has_side_effects=True),
    )(jnp.concatenate([trans[0], cov[0], info[0], lines]))

    mats, vecs, got, got_vec, inverse, pulled = pl.pallas_call(
        first_kernel,
        out_shape=(mats_shape, vecs_shape, mats_shape, vecs_shape, pair_shape, row_shape),
        in_specs=[vmem] * 2,
        out_specs=(vmem,) * 6,
        scratch_shapes=scratch_tools(size),
        compiler_params=params(28),
    )(own_slabs, prior_slabs)
    got = [got]

    for distance in (1, 2, 4):
        parts = 2 if distance < 4 else 1
        hops = 1 if distance < 4 else 4
        more = (pair_shape, row_shape, vecs_shape) if parts > 1 else ()
        mats, vecs, *rest = pl.pallas_call(
            functools.partial(step_kernel, count=len(got), distance=distance, parts=parts),
            out_shape=(mats_shape, vecs_shape, *part_shapes[:parts], vecs_shape, *more),
            in_specs=[vmem] * (5 + len(got)),
            out_specs=(vmem,) * (3 + parts + len(more)),
            scratch_shapes=[pltpu.VMEM(part.shape, F32) for part in part_shapes]
            + [dma((8 * parts,)), dma((parts,))]
            + [dma((3 * parts,))] * 2
            + [dma((4 * parts,))] * 2
            + [dma((2 * hops,)), dma]
            + scratch_tools(size),
            compiler_params=params(28, collective_id=1 + distance, has_side_effects=True),
        )(mats, vecs, *got, got_vec, inverse, pulled)
        got, got_vec = rest[:parts], rest[parts]
        if parts > 1:
            found, pulled, error = rest[parts + 1 :]
            inverse = pl.pallas_call(
                functools.partial(repair_kernel, distance=2 * distance),
                out_shape=pair_shape,
                in_specs=[vmem] * 5,
                out_specs=vmem,
                scratch_shapes=scratch_tools(size),
                input_output_aliases={3: 0},
                compiler_params=params(28),
            )(mats, vecs, got[0], found, error)

    gain, offset, cov_out, mean_out = pl.pallas_call(
        functools.partial(gain_kernel, distance=8),
        out_shape=(
            shape((size, size), F32),
            shape((8, size), F32),
            shape((piece, size), F32),
            shape((1, piece), F32),
        ),
        in_specs=[vmem] * 6,
        out_specs=(vmem,) * 4,
        scratch_shapes=[pltpu.VMEM((1, size, size), F32), pltpu.VMEM((8, LANES), F32)] + scratch_tools(size),
        compiler_params=params(28),
    )(mats, vecs, *got, got_vec, dynamics[0], noise[0])

    smooth = pl.pallas_call(
        chain_kernel,
        out_shape=shape((1, piece), F32),
        in_specs=[vmem] * 2,
        out_specs=vmem,
        scratch_shapes=[
            pltpu.VMEM((size, size), F32),
            pltpu.VMEM((8, size), F32),
            pltpu.VMEM((8, size), F32),
            pltpu.VMEM((8, size), F32),
            pltpu.VMEM((8, size), F32),
            pltpu.VMEM((size, size), F32),
            pltpu.VMEM((2, size, size), BF16),
            pltpu.VMEM((2, size, size), BF16),
            dma((4,)),
            dma((3,)),
        ],
        compiler_params=params(12, collective_id=1, has_side_effects=True),
    )(gain, offset)

    return smooth, mean_out, cov_out[None]


def solution(mesh):
    in_specs = (
        P("tm", "row", None),
        P("tm", "row"),
        P("tm", "row", None),
        P("tm", "row", None),
        P("tm", "row"),
        P("tm", None, None),
        P("tm", None, None),
    )
    out_specs = (P("tm", "row"), P("tm", "row"), P("tm", "row", None))
    return jax.shard_map(body, mesh=mesh, in_specs=in_specs, out_specs=out_specs, check_vma=False)
```

```python
import functools

import jax
import jax.numpy as jnp
from jax import lax
from jax.experimental import pallas as pl
from jax.experimental.pallas import tpu as pltpu
from jax.sharding import PartitionSpec as P

MESH = pl.DeviceIdType.MESH
F32, BF16 = jnp.float32, jnp.bfloat16
NN = (((1,), (0,)), ((), ()))
NT = (((1,), (1,)), ((), ()))
TN = (((0,), (0,)), ((), ()))
VROWS = 16
LANES = 128
REACH = 0.008
SMALL = 4e-3
STEPS = 4
MIB = 1024 * 1024


def places():
    time_pos, row_pos = lax.axis_index("tm"), lax.axis_index("row")
    return time_pos // 2, time_pos % 2, row_pos // 4, row_pos % 4


def dot(lhs, rhs, dims=NN):
    return lax.dot_general(lhs, rhs, dims, preferred_element_type=F32)


def put(pair, value, start=0, column=0):
    high = value.astype(BF16)
    rows, columns = pl.ds(start, value.shape[0]), pl.ds(column, value.shape[1])
    pair[0, rows, columns] = high
    pair[1, rows, columns] = (value - high.astype(F32)).astype(BF16)


def put_high(pair, value):
    pair[0, : value.shape[0], :] = value.astype(BF16)


class Tools:
    def __init__(self, refs):
        self.product, self.value, *self.pairs = refs
        self.size = self.value.shape[0]

    def times(self, lhs, rhs, dims=NN, rows=None):
        size = self.size
        rows = lhs.shape[1] if rows is None else rows
        high, low = rhs[0, :size, :], rhs[1, :size, :]
        left = lhs[0, :rows, :]
        return dot(left, high, dims) + dot(left, low, dims) + dot(lhs[1, :rows, :], high, dims)

    def thin(self, lhs, rhs):
        size = self.size
        high = lhs.astype(BF16)
        low = (lhs - high.astype(F32)).astype(BF16)
        return dot(high, rhs[0, :size, :]) + dot(high, rhs[1, :size, :]) + dot(low, rhs[0, :size, :])


def scratch_tools(size):
    tall = size + VROWS
    return [pltpu.VMEM((tall, size), F32), pltpu.VMEM((size, size), F32)] + [
        pltpu.VMEM((2, tall if index in (0, 4, 5) else size, size), BF16) for index in range(6)
    ]


def eye(size):
    rows = lax.broadcasted_iota(jnp.int32, (size, size), 0)
    return (rows == lax.broadcasted_iota(jnp.int32, (size, size), 1)).astype(F32)


class Newton:
    def __init__(self, tools, upper, lower, out, mat, work):
        self.tools, self.size, self.value, self.product = tools, tools.size, tools.value, tools.product
        self.out, self.mat, self.work = out, mat, work
        self.first = 2.0 / (upper + lower)
        self.opening = (upper - lower) / (upper + lower)

    @staticmethod
    def scale_of(bound):
        return 2.0 / (2.0 - bound * bound)

    def after(self, bound):
        return bound * bound * 0.5 * self.scale_of(bound)

    def start(self):
        whole = self.mat[0].astype(F32) + self.mat[1].astype(F32)
        new = (self.scale_of(self.opening) * self.first) * (2.0 * eye(self.size) - self.first * whole)
        self.value[...] = new
        put(self.out, new)
        return self.after(self.opening)

    def coarse(self, bound):
        size, out, work = self.size, self.out, self.work
        put_high(work, eye(size) - dot(self.mat[0], out[0]))
        new = self.scale_of(bound) * (self.value[...] + dot(out[0], work[0, :size, :]))
        self.value[...] = new
        put_high(out, new)
        return self.after(bound)

    def add(self, lhs, rhs, sign):
        size, product = self.size, self.product

        def one(index, carry):
            product[:size, :] += sign * dot(lhs[index // 2, :size, :], rhs[index % 2, :size, :])
            return carry

        lax.fori_loop(0, 3, one, 0)

    def careful(self, bound):
        size, product = self.size, self.product
        product[:size, :] = eye(size)
        self.add(self.mat, self.out, -1.0)
        put(self.work, product[:size, :])
        product[:size, :] = self.value[...]
        self.add(self.out, self.work, 1.0)
        self.settle(self.scale_of(bound) * product[:size, :])
        return self.after(bound)

    def settle(self, new):
        self.value[...] = new
        put(self.out, new)

    def check(self):
        residual = eye(self.size) - self.tools.times(self.mat, self.out)
        self.product[: self.size, :] = residual
        put_high(self.work, residual)
        return jnp.sum(residual * residual)

    def step(self):
        self.settle(self.value[...] + dot(self.out[0], self.work[0, : self.size, :]))

    def last_step(self):
        small = self.work[0, : self.size, :]
        put_high(self.work, self.product[: self.size, :] + dot(small, small))
        put(self.out, self.value[...] + dot(self.out[0], self.work[0, : self.size, :]))

    def whole(self):
        def plain(carry):
            count, _ = carry
            error = self.check()
            fail = (count == 0) & jnp.logical_not(error < 1.0)

            @pl.when(fail)
            def _():
                lax.while_loop(lambda bound: bound > REACH, self.careful, self.start())

            @pl.when(jnp.logical_not(fail) & (error > SMALL))
            def _():
                self.step()

            return count + 1, jnp.where(fail, 1.0, error)

        lax.while_loop(lambda bound: bound > REACH, self.coarse, self.start())
        put(self.out, self.value[...])
        lax.while_loop(lambda c: (c[0] < 60) & (c[1] > SMALL), plain, (jnp.int32(0), jnp.float32(1.0)))
        self.last_step()

    def fixed(self):
        lax.fori_loop(0, STEPS, lambda _, bound: self.coarse(bound), self.start())
        put(self.out, self.value[...])

        def plain(index, error):
            error = self.check()

            @pl.when(index == 0)
            def _():
                self.step()

            return error

        error = lax.fori_loop(0, 2, plain, jnp.float32(0.0))
        self.last_step()
        return error

    def compact(self):
        size = self.size
        lax.while_loop(lambda bound: bound > REACH, self.careful, self.start())

        def plain(carry):
            self.careful(0.0)
            residual = self.work[0, :size, :].astype(F32)
            return carry[0] + 1, jnp.sum(residual * residual)

        lax.while_loop(lambda c: (c[0] < 60) & (c[1] > SMALL), plain, (jnp.int32(0), jnp.float32(1.0)))
        self.careful(0.0)


def one_norm(matrix):
    return jnp.max(jnp.sum(jnp.abs(matrix), axis=0, keepdims=True))


def spread(row):
    return jnp.broadcast_to(row, (VROWS, row.shape[1]))


def row_of(tile, start):
    return jnp.concatenate([tile[start + i : start + i + 1, :] for i in range(4)], axis=1)


def set_row(tile, start, row):
    for i in range(4):
        tile[start + i : start + i + 1, :] = row[0:1, i * LANES : (i + 1) * LANES]


UPPER = [(i, j) for i in range(4) for j in range(i, 4)]
FULL = [(i, j) for i in range(4) for j in range(4)]
BLOCKS = {0: (0, UPPER), 1: (1, FULL), 2: (2, UPPER)}


def each_block(packed, which):
    part, places_of = BLOCKS[which]
    for index, (i, j) in enumerate(places_of):
        value = packed[part][pl.ds(index * LANES, LANES), :]
        yield i * LANES, j * LANES, value
        if places_of is UPPER and i != j:
            yield j * LANES, i * LANES, value.T


def pack(mats, packed, which):
    part, places_of = BLOCKS[which]
    for index, (i, j) in enumerate(places_of):
        packed[part][pl.ds(index * LANES, LANES), :] = mats[
            which, pl.ds(i * LANES, LANES), pl.ds(j * LANES, LANES)
        ]


def fill(prior, which, pair):
    if isinstance(prior, tuple):
        for i, j, value in each_block(prior, which):
            put(pair, value, i, j)
    else:
        put(pair, prior[which])


def increase(mats, which, prior):
    if isinstance(prior, tuple):
        for i, j, value in each_block(prior, which):
            rows, columns = pl.ds(i, LANES), pl.ds(j, LANES)
            mats[which, rows, columns] = mats[which, rows, columns] + value
    else:
        mats[which] = mats[which] + prior[which]


def couple(own, own_vec, prior, tools):
    size = tools.size
    one, two, three, four, five, six = tools.pairs
    put(one, own[2])
    put(one, spread(row_of(own_vec, 4)), size)
    fill(prior, 0, two)
    coupling = tools.times(one, two)
    pulled = coupling[size : size + 1]
    coupling = coupling[:size]
    put(four, eye(size) + coupling)
    return 2.0 + one_norm(coupling), pulled


def combine_cov(own, prior, inverse, new, tools):
    times = tools.times
    one, two, three, four, five, six = tools.pairs
    fill(prior, 0, two)
    put(four, own[1])
    put(five, times(two, inverse))
    put(six, times(five, four, rows=tools.size))
    new[0] = times(four, six, TN) + own[0]


def combine_trans(own_vec, prior, prior_vec, inverse, pulled_row, new, new_vec, tools):
    size, times = tools.size, tools.times
    one, two, three, four, five, six = tools.pairs
    prior_mean, mean = row_of(prior_vec, 0), row_of(own_vec, 0)
    fill(prior, 1, five)
    put(five, spread(prior_mean + pulled_row), size)
    gained = times(five, inverse)
    put(two, gained[:size])
    put(six, gained)
    moved = times(six, four)
    new[1] = moved[:size]
    set_row(new_vec, 0, moved[size : size + 1] + mean)


def combine_info(own, own_vec, prior, prior_vec, new, new_vec, tools):
    size, times = tools.size, tools.times
    one, two, three, four, five, six = tools.pairs
    prior_mean, prior_pull, pull = row_of(prior_vec, 0), row_of(prior_vec, 4), row_of(own_vec, 4)
    put(three, own[2])
    put(five, spread(prior_mean), size)
    pulled = times(five, three)
    put(six, pulled[:size])
    put(six, spread(pull - pulled[size : size + 1]), size)
    informed = times(six, two, NT)
    new[2] = informed[:size]
    increase(new, 2, prior)
    set_row(new_vec, 4, informed[size : size + 1] + prior_pull)


def unpack(slabs, mats, vecs):
    piece = mats.shape[1] // 16
    for y in range(4):
        total = None
        for x in range(4):
            rows = pl.ds((4 * y + x) * piece, piece)
            for index in range(10):
                which = 1 if index < 4 else 0 if index < 7 else 2
                group = index if index < 4 else (y + (index - 4) % 3) % 4
                mats[which, rows, pl.ds(group * LANES, LANES)] = slabs[y, x, pl.ds(index * piece, piece), :]
            tile = slabs[y, x, pl.ds(10 * piece, 8), :]
            total = tile if total is None else total + tile
        vecs[y : y + 1, :] = total[0:1, :]
        vecs[4 + y : 5 + y, :] = total[1:2, :]
    mats[1] = mats[1].T
    for which in (0, 2):
        for y in range(4):
            left, right = pl.ds(y * LANES, LANES), pl.ds((y + 3) % 4 * LANES, LANES)
            mats[which, left, right] = mats[which, right, left].T


def first_kernel(own_slabs, prior_slabs, own, own_vec, prior, prior_vec, inverse, pulled, *refs):
    odd = lax.axis_index("tm") % 2 == 1
    unpack(own_slabs, own, own_vec)

    @pl.when(odd)
    def _():
        unpack(prior_slabs, prior, prior_vec)
        tools = Tools(refs)
        upper, row = couple(own, own_vec, prior, tools)
        pulled[...] = spread(row)[:8]
        Newton(tools, upper, 1.0, inverse, tools.pairs[3], tools.pairs[4]).whole()


def repair_kernel(own, prior_cov, found, error, inverse, *refs, distance):
    @pl.when((lax.axis_index("tm") // distance) % 2 == 1)
    def _():
        @pl.when(jnp.logical_not(jnp.max(error[...]) < SMALL))
        def _():
            tools = Tools(refs)
            size, product = tools.size, tools.product
            one, two, three, four, five, six = tools.pairs
            put(one, own[2])
            fill((prior_cov,), 0, two)
            product[...] = jnp.zeros_like(product)
            Newton(tools, 2.0, 1.0, three, four, five).add(one, two, 1.0)
            coupling = product[:size, :]
            put(four, eye(size) + coupling)
            Newton(tools, 2.0 + one_norm(coupling), 1.0, inverse, four, five).compact()


def gain_kernel(
    own, own_vec, prior_cov, prior_vec, dynamics, noise, gain, offset, cov_out, mean_out, new, mean_tile, kept, *refs, distance
):
    tools = Tools(refs)
    size, times, thin = tools.size, tools.times, tools.thin
    time_pos, row_pos = lax.axis_index("tm"), lax.axis_index("row")
    present = (time_pos // distance) % 2 == 1
    one, two, three, four, five, six = tools.pairs

    @pl.when(jnp.logical_not(present))
    def _():
        new[0] = own[0]
        mean_tile[...] = own_vec[...]

    prior = (prior_cov,)

    def couple_last():
        upper, row = couple(own, own_vec, prior, tools)
        kept[0:1, :] = row
        return upper, jnp.float32(1.0)

    def couple_gain():
        put(two, dynamics[...])
        put(three, new[0])
        put(one, times(two, three))
        put(one, spread(row_of(mean_tile, 0)), size)
        projected = times(one, two, NT)
        put(five, projected[size:], size)
        innovation = projected[:size] + noise[...]
        put(four, innovation)
        upper = one_norm(innovation)
        return upper, upper * 0.004

    def stage(index, carry):
        upper, lower = lax.cond(index == 0, couple_last, couple_gain)
        Newton(tools, upper, lower, three, four, six).whole()

        @pl.when(index == 0)
        def _():
            combine_cov(own, prior, three, new, tools)
            moved = thin(thin(spread(row_of(prior_vec, 0) + kept[0:1, :]), three), four)
            set_row(mean_tile, 0, moved[0:1] + row_of(own_vec, 0))

        return carry

    lax.fori_loop(jnp.where(present, 0, 1), jnp.where(time_pos == 15, 1, 2), stage, 0)
    piece = cov_out.shape[0]
    cov_out[...] = new[0, pl.ds(pl.multiple_of(row_pos * piece, piece), piece), :]
    mean = row_of(mean_tile, 0)
    share(mean_out, mean, row_pos)

    @pl.when(time_pos == 15)
    def _():
        gain[...] = jnp.zeros_like(gain)
        offset[...] = jnp.broadcast_to(mean, offset.shape)

    @pl.when(time_pos < 15)
    def _():
        weights = times(three, one)
        gain[...] = weights
        put(six, weights)
        predicted = five[0, size:, :].astype(F32) + five[1, size:, :].astype(F32)
        offset[...] = mean - thin(predicted, six)[:8]


def share(out, row, row_pos):
    piece = out.shape[1]
    for index in range(16):

        @pl.when(row_pos == index)
        def _():
            out[...] = row[0:1, index * piece : (index + 1) * piece]


def remote(src, dst, send, recv, tm, row):
    return pltpu.make_async_remote_copy(
        src_ref=src, dst_ref=dst, send_sem=send, recv_sem=recv, device_id=(tm, row), device_id_type=MESH
    )


def greet(barrier, tm, row):
    pl.semaphore_signal(barrier, inc=1, device_id=(tm, row), device_id_type=MESH)


def gather_kernel(rows, own, prior, send, recv, far_send, far_recv):
    z, core, y, x = places()
    time_pos, row_pos = lax.axis_index("tm"), lax.axis_index("row")
    piece = (rows.shape[0] - 8) // 3
    keep = (time_pos > 0).astype(F32)
    barrier = pltpu.get_barrier_semaphore()
    across = [y * 4 + (x + k) % 4 for k in (1, 2, 3)]
    along = [((y + k) % 4) * 4 + x for k in (1, 2, 3)]
    for peer in across + along:
        greet(barrier, time_pos, peer)

    @pl.when(core == 1)
    def _():
        greet(barrier, time_pos - 1, row_pos)

    for index in range(4):
        columns = pl.ds(index * LANES, LANES)
        own[y, x, pl.ds(index * piece, piece), :] = rows[pl.ds(0, piece), columns] * keep
    for index in range(3):
        columns = pl.ds(pl.multiple_of((y + index) % 4 * LANES, LANES), LANES)
        own[y, x, pl.ds((4 + index) * piece, piece), :] = rows[pl.ds(piece, piece), columns]
        own[y, x, pl.ds((7 + index) * piece, piece), :] = rows[pl.ds(2 * piece, piece), columns] * keep
    own[y, x, pl.ds(10 * piece, 8), :] = jnp.zeros((8, LANES), F32)
    for index in range(4):

        @pl.when(x == index)
        def _():
            lanes = pl.ds(index * piece, piece)
            own[y, x, pl.ds(10 * piece, 1), lanes] = rows[pl.ds(3 * piece, 1), :piece]
            own[y, x, pl.ds(10 * piece + 1, 1), lanes] = rows[pl.ds(3 * piece + 1, 1), :piece] * keep

    def gather(near, other, line):
        copies = []
        for k in range(3):
            copy = remote(own.at[y, x], own.at[y, x], send.at[k], recv.at[k], time_pos, near[k])
            copy.start()
            copies.append(copy)
        for copy in copies:
            copy.wait_recv()
        later = []
        for k in range(3):
            copy = remote(line, line, send.at[3 + k], recv.at[3 + k], time_pos, other[k])
            copy.start()
            later.append(copy)
        return copies, later

    @pl.when(core == 0)
    def _():
        pl.semaphore_wait(barrier, 7)
        copies, later = gather(across, along, own.at[y])
        passed = []
        for k in range(4):
            if k:
                later[k - 1].wait_recv()
            line = (y + 4 - k) % 4
            copy = remote(own.at[line], prior.at[line], far_send.at[k], far_recv.at[k], time_pos + 1, row_pos)
            copy.start()
            passed.append(copy)
        for copy in copies + later + passed:
            copy.wait_send()

    @pl.when(core == 1)
    def _():
        pl.semaphore_wait(barrier, 6)
        copies, later = gather(along, across, own.at[:, x])
        for copy in later:
            copy.wait_recv()
        for copy in copies + later:
            copy.wait_send()
        for k in range(4):
            line = (y + 4 - k) % 4
            remote(own.at[line], prior.at[line], far_send.at[k], far_recv.at[k], time_pos, row_pos).wait_recv()


def step_kernel(own, own_vec, *refs, count, distance, parts):
    prior_refs, refs = refs[:count], refs[count:]
    prior_vec, inverse, pulled, new, new_vec = refs[:5]
    got, got_vec, refs = refs[5 : 5 + parts], refs[5 + parts], refs[6 + parts :]
    if parts > 1:
        next_inverse, next_pulled, error, *refs = refs
    packed, refs = refs[:3], refs[3:]
    far_send, far_recv, send, recv, twin_send, twin_recv, vec_send, vec_recv = refs[:8]
    tools = Tools(refs[8:])
    prior = prior_refs[0] if count == 1 else prior_refs
    z, core, y, x = places()
    time_pos, row_pos = lax.axis_index("tm"), lax.axis_index("row")
    reach, relay = distance, distance == 2
    barrier = pltpu.get_barrier_semaphore()
    target = (z // reach) % 2 == 1
    source = ((z // reach) % 2 == 0) & (z % reach == reach - 1) & (core == 1)
    source_pos = ((z // reach) * reach) * 2 - 1
    outer_pos = (1 - core) * y + core * x
    hops = 1 if relay else reach
    onward = target & ((z % reach) < reach - 1) if relay else None
    present = (time_pos // distance) % 2 == 1
    twin = 2 * z + 1 - core

    def view(ref, side, line):
        rows = ref.shape[0] // 8
        return ref.at[pl.ds(pl.multiple_of((side * 4 + line) * rows, 8), rows)]

    def outer_row(k):
        place = (outer_pos + k) % 4
        return (1 - core) * (place * 4 + x) + core * (y * 4 + place)

    @pl.when(target)
    def _():
        if relay:
            greet(barrier, (z % reach == 0) * source_pos + (z % reach != 0) * (time_pos - 2), row_pos)
        else:
            greet(barrier, source_pos, row_pos)
        for k in (1, 2, 3):
            greet(barrier, time_pos, outer_row(k))
        greet(barrier, twin, row_pos)

    @pl.when(present)
    def _():
        combine_cov(own, prior, inverse, new, tools)

    def deliver(part):
        for step in reversed(range(hops)):
            for side in range(2):
                slot = 2 * step + side
                line = y if side == 0 else x
                yield remote(
                    view(packed[part], side, line),
                    view(got[part], side, line),
                    far_send.at[part * 8 + slot],
                    far_recv.at[part],
                    time_pos + 1 + slot,
                    row_pos,
                )

    def deliver_vec():
        for slot in reversed(range(2 * hops)):
            yield remote(new_vec, got_vec, vec_send.at[slot], vec_recv, time_pos + 1 + slot, row_pos)

    @pl.when(source)
    def _():
        pack(new, packed, 0)
        pl.semaphore_wait(barrier, 2 * hops)
        for copy in deliver(0):
            copy.start()

    @pl.when(present)
    def _():
        combine_trans(own_vec, prior, prior_vec, inverse, pulled[0:1, :], new, new_vec, tools)

    if parts > 1:

        @pl.when(source)
        def _():
            pack(new, packed, 1)
            for copy in deliver(1):
                copy.start()

    @pl.when(present)
    def _():
        combine_info(own, own_vec, prior, prior_vec, new, new_vec, tools)

    @pl.when(jnp.logical_not(present))
    def _():
        new[...] = own[...]
        new_vec[...] = own_vec[...]

    @pl.when(source)
    def _():
        for copy in deliver_vec():
            copy.start()
        if parts > 1:
            pack(new, packed, 2)
            for copy in deliver(2):
                copy.start()
        for part in range(parts):
            for copy in deliver(part):
                copy.wait_send()
        for copy in deliver_vec():
            copy.wait_send()

    def onto(part):
        mine = view(got[part], core, outer_pos)
        return remote(mine, mine, far_send.at[part * 8], far_recv.at[part], time_pos + 2, row_pos)

    @pl.when(target)
    def _():
        if relay:

            @pl.when(onward)
            def _():
                pl.semaphore_wait(barrier, 5)

            @pl.when(jnp.logical_not(onward))
            def _():
                pl.semaphore_wait(barrier, 4)

        else:
            pl.semaphore_wait(barrier, 4)
        copies = []

        def over(k, part):
            mine = view(got[part], core, (outer_pos + 4 - k) % 4)
            slot = k * parts + part
            copy = remote(mine, mine, twin_send.at[slot], twin_recv.at[slot], twin, row_pos)
            copy.start()
            copies.append(copy)

        def pass_vec():
            arrived = remote(got_vec, got_vec, vec_send.at[0], vec_recv, time_pos + 2, row_pos)
            arrived.wait_recv()
            if relay:

                @pl.when(onward)
                def _():
                    arrived.start()

        def enter(part):
            onto(part).wait_recv()
            if relay:

                @pl.when(onward)
                def _():
                    onto(part).start()

            mine = view(got[part], core, outer_pos)
            for k in range(1, 4):
                slot = (k - 1) * parts + part
                copy = remote(mine, mine, send.at[slot], recv.at[slot], time_pos, outer_row(k))
                copy.start()
                copies.append(copy)
            over(0, part)

        def complete(part):
            for k in (1, 3, 2):
                line = view(got[part], core, (outer_pos + 4 - k) % 4)
                slot = (k - 1) * parts + part
                remote(line, line, send.at[slot], recv.at[slot], time_pos, outer_row(k)).wait_recv()
                over(k, part)
            for k in range(4):
                theirs = view(got[part], 1 - core, 0)
                slot = k * parts + part
                remote(theirs, theirs, twin_send.at[slot], twin_recv.at[slot], twin, row_pos).wait_recv()

        enter(0)
        complete(0)
        if parts > 1:
            upper, row = couple(new, new_vec, (got[0],), tools)
            next_pulled[...] = spread(row)[:8]
            newton = Newton(tools, upper, 1.0, next_inverse, tools.pairs[3], tools.pairs[4])
            enter(1)
            pass_vec()
            found = newton.fixed()
            error[...] = jnp.zeros_like(error) + found
            enter(2)
            complete(1)
            complete(2)
        else:
            pass_vec()
        for copy in copies:
            copy.wait_send()
        if relay:

            @pl.when(onward)
            def _():
                remote(got_vec, got_vec, vec_send.at[0], vec_recv, time_pos + 2, row_pos).wait_send()
                for part in range(parts):
                    onto(part).wait_send()


def chain_kernel(gain, offset, smooth, near_gain, near_offset, held, sent, state, *rest):
    refs, (send, recv) = rest[:-2], rest[-2:]
    product, one, two = refs
    z, core, _, _ = places()
    time_pos, row_pos = lax.axis_index("tm"), lax.axis_index("row")
    size = gain.shape[0]
    barrier = pltpu.get_barrier_semaphore()
    first, last = core == 0, z == 7

    @pl.when(first)
    def _():
        greet(barrier, time_pos + 1, row_pos)

    @pl.when(jnp.logical_not(last))
    def _():
        greet(barrier, 2 * z + 2, row_pos)

    put(two, gain[...])
    link = remote(gain, near_gain, send.at[0], recv.at[0], 2 * z, row_pos)
    small = remote(offset, near_offset, send.at[1], recv.at[1], 2 * z, row_pos)

    def apply(row8):
        high = row8.astype(BF16).astype(F32)
        both = jnp.concatenate([high, row8 - high], axis=0).astype(BF16)
        result = dot(both, two[0])
        return result[:8] + result[8:] + dot(both, two[1])[:8]

    @pl.when(core == 1)
    def _():
        pl.semaphore_wait(barrier, 1)
        small.start()

        @pl.when(jnp.logical_not(last))
        def _():
            link.start()

        state[...] = offset[...]

    @pl.when(first & (z > 0))
    def _():
        pl.semaphore_wait(barrier, 2)

    @pl.when(first & last)
    def _():
        small.wait_recv()
        state[...] = apply(near_offset[...]) + offset[...]

    @pl.when(first & jnp.logical_not(last))
    def _():
        small.wait_recv()
        state[...] = apply(near_offset[...]) + offset[...]
        link.wait_recv()
        put(one, near_gain[...])

        def part(index, carry):
            columns = pl.ds(pl.multiple_of(index * 256, 256), 256)
            high, low = two[0, :, columns], two[1, :, columns]
            product[:, columns] = dot(one[0], high) + dot(one[0], low) + dot(one[1], high)
            return carry

        lax.fori_loop(0, size // 256, part, 0)
        put(two, product[...])

    @pl.when(jnp.logical_not(last))
    def _():
        remote(held, held, send.at[2], recv.at[2], time_pos, row_pos).wait_recv()
        state[...] = state[...] + apply(held[...])

    @pl.when(first & (z > 0))
    def _():
        sent[...] = state[...]
        copies = [remote(sent, held, send.at[2 + k], recv.at[2], 2 * z - 2 + k, row_pos) for k in range(2)]
        for copy in copies:
            copy.start()
        for copy in copies:
            copy.wait_send()

    share(smooth, state[0:1, :], row_pos)

    @pl.when(core == 1)
    def _():
        small.wait_send()

        @pl.when(jnp.logical_not(last))
        def _():
            link.wait_send()


def body(trans, mean, cov, info, pull, dynamics, noise):
    piece, size = trans.shape[1:]
    shape = jax.ShapeDtypeStruct
    vmem = pl.BlockSpec(memory_space=pltpu.VMEM)
    dma = pltpu.SemaphoreType.DMA

    def params(mib, **more):
        return pltpu.CompilerParams(vmem_limit_bytes=mib * MIB, **more)

    slab = shape((4, 4, 10 * piece + 8, LANES), F32)
    mats_shape, vecs_shape = shape((3, size, size), F32), shape((8, LANES), F32)
    pair_shape, row_shape = shape((2, size, size), BF16), shape((8, size), F32)
    part_shapes = tuple(shape((count * LANES, LANES), F32) for count in (10, 16, 10))
    lines = jnp.pad(jnp.concatenate([mean, pull]), ((0, 6), (0, size - piece)))
    own_slabs, prior_slabs = pl.pallas_call(
        gather_kernel,
        out_shape=(slab, slab),
        in_specs=[vmem],
        out_specs=(vmem, vmem),
        scratch_shapes=[dma((6,)), dma((6,)), dma((4,)), dma((4,))],
        compiler_params=params(12, collective_id=0, has_side_effects=True),
    )(jnp.concatenate([trans[0], cov[0], info[0], lines]))

    mats, vecs, got, got_vec, inverse, pulled = pl.pallas_call(
        first_kernel,
        out_shape=(mats_shape, vecs_shape, mats_shape, vecs_shape, pair_shape, row_shape),
        in_specs=[vmem] * 2,
        out_specs=(vmem,) * 6,
        scratch_shapes=scratch_tools(size),
        compiler_params=params(28),
    )(own_slabs, prior_slabs)
    got = [got]

    for distance in (1, 2, 4):
        parts = 3 if distance < 4 else 1
        hops = 1 if distance < 4 else 4
        more = (pair_shape, row_shape, vecs_shape) if parts > 1 else ()
        mats, vecs, *rest = pl.pallas_call(
            functools.partial(step_kernel, count=len(got), distance=distance, parts=parts),
            out_shape=(mats_shape, vecs_shape, *part_shapes[:parts], vecs_shape, *more),
            in_specs=[vmem] * (5 + len(got)),
            out_specs=(vmem,) * (3 + parts + len(more)),
            scratch_shapes=[pltpu.VMEM(part.shape, F32) for part in part_shapes]
            + [dma((8 * parts,)), dma((parts,))]
            + [dma((3 * parts,))] * 2
            + [dma((4 * parts,))] * 2
            + [dma((2 * hops,)), dma]
            + scratch_tools(size),
            compiler_params=params(28, collective_id=1 + distance, has_side_effects=True),
        )(mats, vecs, *got, got_vec, inverse, pulled)
        got, got_vec = rest[:parts], rest[parts]
        if parts > 1:
            found, pulled, error = rest[parts + 1 :]
            inverse = pl.pallas_call(
                functools.partial(repair_kernel, distance=2 * distance),
                out_shape=pair_shape,
                in_specs=[vmem] * 4,
                out_specs=vmem,
                scratch_shapes=scratch_tools(size),
                input_output_aliases={2: 0},
                compiler_params=params(28),
            )(mats, got[0], found, error)

    gain, offset, cov_out, mean_out = pl.pallas_call(
        functools.partial(gain_kernel, distance=8),
        out_shape=(
            shape((size, size), F32),
            shape((8, size), F32),
            shape((piece, size), F32),
            shape((1, piece), F32),
        ),
        in_specs=[vmem] * 6,
        out_specs=(vmem,) * 4,
        scratch_shapes=[pltpu.VMEM((1, size, size), F32), pltpu.VMEM((8, LANES), F32), pltpu.VMEM((8, size), F32)]
        + scratch_tools(size),
        compiler_params=params(28),
    )(mats, vecs, *got, got_vec, dynamics[0], noise[0])

    smooth = pl.pallas_call(
        chain_kernel,
        out_shape=shape((1, piece), F32),
        in_specs=[vmem] * 2,
        out_specs=vmem,
        scratch_shapes=[
            pltpu.VMEM((size, size), F32),
            pltpu.VMEM((8, size), F32),
            pltpu.VMEM((8, size), F32),
            pltpu.VMEM((8, size), F32),
            pltpu.VMEM((8, size), F32),
            pltpu.VMEM((size, size), F32),
            pltpu.VMEM((2, size, size), BF16),
            pltpu.VMEM((2, size, size), BF16),
            dma((4,)),
            dma((3,)),
        ],
        compiler_params=params(12, collective_id=1, has_side_effects=True),
    )(gain, offset)

    return smooth, mean_out, cov_out[None]


def solution(mesh):
    in_specs = (
        P("tm", "row", None),
        P("tm", "row"),
        P("tm", "row", None),
        P("tm", "row", None),
        P("tm", "row"),
        P("tm", None, None),
        P("tm", None, None),
    )
    out_specs = (P("tm", "row"), P("tm", "row"), P("tm", "row", None))
    return jax.shard_map(body, mesh=mesh, in_specs=in_specs, out_specs=out_specs, check_vma=False)
```

```python
import functools

import jax
import jax.numpy as jnp
from jax import lax
from jax.experimental import pallas as pl
from jax.experimental.pallas import tpu as pltpu
from jax.sharding import PartitionSpec as P

MESH = pl.DeviceIdType.MESH
F32, BF16 = jnp.float32, jnp.bfloat16
NN = (((1,), (0,)), ((), ()))
NT = (((1,), (1,)), ((), ()))
TN = (((0,), (0,)), ((), ()))
VROWS = 16
LANES = 128
REACH = 0.008
SMALL = 4e-3
STEPS = 3
MIB = 1024 * 1024


def places():
    time_pos, row_pos = lax.axis_index("tm"), lax.axis_index("row")
    return time_pos // 2, time_pos % 2, row_pos // 4, row_pos % 4


def dot(lhs, rhs, dims=NN):
    return lax.dot_general(lhs, rhs, dims, preferred_element_type=F32)


def put(pair, value, start=0, column=0):
    high = value.astype(BF16)
    rows, columns = pl.ds(start, value.shape[0]), pl.ds(column, value.shape[1])
    pair[0, rows, columns] = high
    pair[1, rows, columns] = (value - high.astype(F32)).astype(BF16)


def put_high(pair, value):
    pair[0, : value.shape[0], :] = value.astype(BF16)


class Tools:
    def __init__(self, refs):
        self.product, self.value, *self.pairs = refs
        self.size = self.value.shape[0]

    def times(self, lhs, rhs, dims=NN, rows=None):
        size = self.size
        rows = lhs.shape[1] if rows is None else rows
        high, low = rhs[0, :size, :], rhs[1, :size, :]
        left = lhs[0, :rows, :]
        return dot(left, high, dims) + dot(left, low, dims) + dot(lhs[1, :rows, :], high, dims)

    def thin(self, lhs, rhs):
        size = self.size
        high = lhs.astype(BF16)
        low = (lhs - high.astype(F32)).astype(BF16)
        return dot(high, rhs[0, :size, :]) + dot(high, rhs[1, :size, :]) + dot(low, rhs[0, :size, :])


def scratch_tools(size):
    tall = size + VROWS
    return [pltpu.VMEM((tall, size), F32), pltpu.VMEM((size, size), F32)] + [
        pltpu.VMEM((2, tall if index in (0, 4, 5) else size, size), BF16) for index in range(6)
    ]


def eye(size):
    rows = lax.broadcasted_iota(jnp.int32, (size, size), 0)
    return (rows == lax.broadcasted_iota(jnp.int32, (size, size), 1)).astype(F32)


class Newton:
    def __init__(self, tools, upper, lower, out, mat, work):
        self.tools, self.size, self.value, self.product = tools, tools.size, tools.value, tools.product
        self.out, self.mat, self.work = out, mat, work
        self.first = 2.0 / (upper + lower)
        self.opening = (upper - lower) / (upper + lower)

    @staticmethod
    def scale_of(bound):
        return 2.0 / (2.0 - bound * bound)

    def after(self, bound):
        return bound * bound * 0.5 * self.scale_of(bound)

    def start(self):
        whole = self.mat[0].astype(F32) + self.mat[1].astype(F32)
        new = (self.scale_of(self.opening) * self.first) * (2.0 * eye(self.size) - self.first * whole)
        self.value[...] = new
        put(self.out, new)
        return self.after(self.opening)

    def coarse(self, bound):
        size, out, work = self.size, self.out, self.work
        put_high(work, eye(size) - dot(self.mat[0], out[0]))
        new = self.scale_of(bound) * (self.value[...] + dot(out[0], work[0, :size, :]))
        self.value[...] = new
        put_high(out, new)
        return self.after(bound)

    def add(self, lhs, rhs, sign):
        size, product = self.size, self.product

        def one(index, carry):
            product[:size, :] += sign * dot(lhs[index // 2, :size, :], rhs[index % 2, :size, :])
            return carry

        lax.fori_loop(0, 3, one, 0)

    def careful(self, bound):
        size, product = self.size, self.product
        product[:size, :] = eye(size)
        self.add(self.mat, self.out, -1.0)
        put(self.work, product[:size, :])
        product[:size, :] = self.value[...]
        self.add(self.out, self.work, 1.0)
        self.settle(self.scale_of(bound) * product[:size, :])
        return self.after(bound)

    def settle(self, new):
        self.value[...] = new
        put(self.out, new)

    def check(self):
        residual = eye(self.size) - self.tools.times(self.mat, self.out)
        self.product[: self.size, :] = residual
        put_high(self.work, residual)
        return jnp.sum(residual * residual)

    def step(self):
        self.settle(self.value[...] + dot(self.out[0], self.work[0, : self.size, :]))

    def last_step(self):
        small = self.work[0, : self.size, :]
        put_high(self.work, self.product[: self.size, :] + dot(small, small))
        self.step()

    def whole(self):
        def plain(carry):
            count, _ = carry
            error = self.check()
            fail = (count == 0) & jnp.logical_not(error < 1.0)

            @pl.when(fail)
            def _():
                lax.while_loop(lambda bound: bound > REACH, self.careful, self.start())

            @pl.when(jnp.logical_not(fail) & (error > SMALL))
            def _():
                self.step()

            return count + 1, jnp.where(fail, 1.0, error)

        lax.while_loop(lambda bound: bound > REACH, self.coarse, self.start())
        put(self.out, self.value[...])
        lax.while_loop(lambda c: (c[0] < 60) & (c[1] > SMALL), plain, (jnp.int32(0), jnp.float32(1.0)))
        self.last_step()

    def fixed(self, between):
        lax.fori_loop(0, STEPS, lambda _, bound: self.coarse(bound), self.start())
        put(self.out, self.value[...])
        between()

        def plain(index, error):
            error = self.check()

            @pl.when(index == 0)
            def _():
                self.step()

            return error

        error = lax.fori_loop(0, 2, plain, jnp.float32(0.0))
        self.last_step()
        return error


def one_norm(matrix):
    return jnp.max(jnp.sum(jnp.abs(matrix), axis=0, keepdims=True))


def spread(row):
    return jnp.broadcast_to(row, (VROWS, row.shape[1]))


def row_of(tile, start):
    return jnp.concatenate([tile[start + i : start + i + 1, :] for i in range(4)], axis=1)


def set_row(tile, start, row):
    for i in range(4):
        tile[start + i : start + i + 1, :] = row[0:1, i * LANES : (i + 1) * LANES]


UPPER = [(i, j) for i in range(4) for j in range(i, 4)]
FULL = [(i, j) for i in range(4) for j in range(4)]
BLOCKS = {0: (0, UPPER), 1: (1, FULL), 2: (2, UPPER)}


def each_block(packed, which):
    part, places_of = BLOCKS[which]
    for index, (i, j) in enumerate(places_of):
        value = packed[part][pl.ds(index * LANES, LANES), :]
        yield i * LANES, j * LANES, value
        if places_of is UPPER and i != j:
            yield j * LANES, i * LANES, value.T


def pack(mats, packed, which):
    part, places_of = BLOCKS[which]
    for index, (i, j) in enumerate(places_of):
        packed[part][pl.ds(index * LANES, LANES), :] = mats[
            which, pl.ds(i * LANES, LANES), pl.ds(j * LANES, LANES)
        ]


def fill(prior, which, pair):
    if isinstance(prior, tuple):
        for i, j, value in each_block(prior, which):
            put(pair, value, i, j)
    else:
        put(pair, prior[which])


def increase(mats, which, prior):
    if isinstance(prior, tuple):
        for i, j, value in each_block(prior, which):
            rows, columns = pl.ds(i, LANES), pl.ds(j, LANES)
            mats[which, rows, columns] = mats[which, rows, columns] + value
    else:
        mats[which] = mats[which] + prior[which]


def couple(own, own_vec, prior, tools):
    size = tools.size
    one, two, three, four, five, six = tools.pairs
    put(one, own[2])
    put(one, spread(row_of(own_vec, 4)), size)
    fill(prior, 0, two)
    coupling = tools.times(one, two)
    pulled = coupling[size : size + 1]
    coupling = coupling[:size]
    put(four, eye(size) + coupling)
    return 2.0 + one_norm(coupling), pulled


def combine_cov(own, prior, inverse, new, tools):
    times = tools.times
    one, two, three, four, five, six = tools.pairs
    fill(prior, 0, two)
    put(four, own[1])
    put(five, times(two, inverse))
    put(six, times(five, four, rows=tools.size))
    new[0] = times(four, six, TN) + own[0]


def combine_trans(own_vec, prior, prior_vec, inverse, pulled_row, new, new_vec, tools):
    size, times = tools.size, tools.times
    one, two, three, four, five, six = tools.pairs
    prior_mean, mean = row_of(prior_vec, 0), row_of(own_vec, 0)
    fill(prior, 1, five)
    put(five, spread(prior_mean + pulled_row), size)
    gained = times(five, inverse)
    put(two, gained[:size])
    put(six, gained)
    moved = times(six, four)
    new[1] = moved[:size]
    set_row(new_vec, 0, moved[size : size + 1] + mean)


def combine_info(own, own_vec, prior, prior_vec, new, new_vec, tools):
    size, times = tools.size, tools.times
    one, two, three, four, five, six = tools.pairs
    prior_mean, prior_pull, pull = row_of(prior_vec, 0), row_of(prior_vec, 4), row_of(own_vec, 4)
    put(three, own[2])
    put(five, spread(prior_mean), size)
    pulled = times(five, three)
    put(six, pulled[:size])
    put(six, spread(pull - pulled[size : size + 1]), size)
    informed = times(six, two, NT)
    new[2] = informed[:size]
    increase(new, 2, prior)
    set_row(new_vec, 4, informed[size : size + 1] + prior_pull)


def unpack(slabs, mats, vecs):
    piece = mats.shape[1] // 16
    for y in range(4):
        total = None
        for x in range(4):
            rows = pl.ds((4 * y + x) * piece, piece)
            for index in range(10):
                which = 1 if index < 4 else 0 if index < 7 else 2
                group = index if index < 4 else (y + (index - 4) % 3) % 4
                mats[which, rows, pl.ds(group * LANES, LANES)] = slabs[y, x, pl.ds(index * piece, piece), :]
            tile = slabs[y, x, pl.ds(10 * piece, 8), :]
            total = tile if total is None else total + tile
        vecs[y : y + 1, :] = total[0:1, :]
        vecs[4 + y : 5 + y, :] = total[1:2, :]
    mats[1] = mats[1].T
    for which in (0, 2):
        for y in range(4):
            left, right = pl.ds(y * LANES, LANES), pl.ds((y + 3) % 4 * LANES, LANES)
            mats[which, left, right] = mats[which, right, left].T


def first_kernel(own_slabs, prior_slabs, own, own_vec, prior, prior_vec, inverse, pulled, *refs):
    odd = lax.axis_index("tm") % 2 == 1
    unpack(own_slabs, own, own_vec)

    @pl.when(odd)
    def _():
        unpack(prior_slabs, prior, prior_vec)
        tools = Tools(refs)
        upper, row = couple(own, own_vec, prior, tools)
        pulled[...] = spread(row)[:8]
        Newton(tools, upper, 1.0, inverse, tools.pairs[3], tools.pairs[4]).whole()


def repair_kernel(own, own_vec, prior_cov, found, error, inverse, *refs, distance):
    @pl.when((lax.axis_index("tm") // distance) % 2 == 1)
    def _():
        @pl.when(jnp.logical_not(jnp.max(error[...]) < SMALL))
        def _():
            tools = Tools(refs)
            upper, _ = couple(own, own_vec, (prior_cov,), tools)
            newton = Newton(tools, upper, 1.0, inverse, tools.pairs[3], tools.pairs[4])
            newton.whole()
            newton.check()
            newton.step()


def gain_kernel(
    own, own_vec, prior_cov, prior_vec, dynamics, noise, gain, offset, cov_out, mean_out, new, mean_tile, kept, *refs, distance
):
    tools = Tools(refs)
    size, times, thin = tools.size, tools.times, tools.thin
    time_pos, row_pos = lax.axis_index("tm"), lax.axis_index("row")
    present = (time_pos // distance) % 2 == 1
    one, two, three, four, five, six = tools.pairs

    @pl.when(jnp.logical_not(present))
    def _():
        new[0] = own[0]
        mean_tile[...] = own_vec[...]

    prior = (prior_cov,)

    def couple_last():
        upper, row = couple(own, own_vec, prior, tools)
        kept[0:1, :] = row
        return upper, jnp.float32(1.0)

    def couple_gain():
        put(two, dynamics[...])
        put(three, new[0])
        put(one, times(two, three))
        put(one, spread(row_of(mean_tile, 0)), size)
        projected = times(one, two, NT)
        put(five, projected[size:], size)
        innovation = projected[:size] + noise[...]
        put(four, innovation)
        upper = one_norm(innovation)
        return upper, upper * 0.004

    def stage(index, carry):
        upper, lower = lax.cond(index == 0, couple_last, couple_gain)
        Newton(tools, upper, lower, three, four, six).whole()

        @pl.when(index == 0)
        def _():
            combine_cov(own, prior, three, new, tools)
            moved = thin(thin(spread(row_of(prior_vec, 0) + kept[0:1, :]), three), four)
            set_row(mean_tile, 0, moved[0:1] + row_of(own_vec, 0))

        return carry

    lax.fori_loop(jnp.where(present, 0, 1), jnp.where(time_pos == 15, 1, 2), stage, 0)
    piece = cov_out.shape[0]
    cov_out[...] = new[0, pl.ds(pl.multiple_of(row_pos * piece, piece), piece), :]
    mean = row_of(mean_tile, 0)
    share(mean_out, mean, row_pos)

    @pl.when(time_pos == 15)
    def _():
        gain[...] = jnp.zeros_like(gain)
        offset[...] = jnp.broadcast_to(mean, offset.shape)

    @pl.when(time_pos < 15)
    def _():
        weights = times(three, one)
        gain[...] = weights
        put(six, weights)
        predicted = five[0, size:, :].astype(F32) + five[1, size:, :].astype(F32)
        offset[...] = mean - thin(predicted, six)[:8]


def share(out, row, row_pos):
    piece = out.shape[1]
    for index in range(16):

        @pl.when(row_pos == index)
        def _():
            out[...] = row[0:1, index * piece : (index + 1) * piece]


def remote(src, dst, send, recv, tm, row):
    return pltpu.make_async_remote_copy(
        src_ref=src, dst_ref=dst, send_sem=send, recv_sem=recv, device_id=(tm, row), device_id_type=MESH
    )


def greet(barrier, tm, row):
    pl.semaphore_signal(barrier, inc=1, device_id=(tm, row), device_id_type=MESH)


def gather_kernel(rows, own, prior, send, recv, far_send, far_recv):
    z, core, y, x = places()
    time_pos, row_pos = lax.axis_index("tm"), lax.axis_index("row")
    piece = (rows.shape[0] - 8) // 3
    keep = (time_pos > 0).astype(F32)
    barrier = pltpu.get_barrier_semaphore()
    across = [y * 4 + (x + k) % 4 for k in (1, 2, 3)]
    along = [((y + k) % 4) * 4 + x for k in (1, 2, 3)]
    for peer in across + along:
        greet(barrier, time_pos, peer)

    @pl.when(core == 1)
    def _():
        greet(barrier, time_pos - 1, row_pos)

    for index in range(4):
        columns = pl.ds(index * LANES, LANES)
        own[y, x, pl.ds(index * piece, piece), :] = rows[pl.ds(0, piece), columns] * keep
    for index in range(3):
        columns = pl.ds(pl.multiple_of((y + index) % 4 * LANES, LANES), LANES)
        own[y, x, pl.ds((4 + index) * piece, piece), :] = rows[pl.ds(piece, piece), columns]
        own[y, x, pl.ds((7 + index) * piece, piece), :] = rows[pl.ds(2 * piece, piece), columns] * keep
    own[y, x, pl.ds(10 * piece, 8), :] = jnp.zeros((8, LANES), F32)
    for index in range(4):

        @pl.when(x == index)
        def _():
            lanes = pl.ds(index * piece, piece)
            own[y, x, pl.ds(10 * piece, 1), lanes] = rows[pl.ds(3 * piece, 1), :piece]
            own[y, x, pl.ds(10 * piece + 1, 1), lanes] = rows[pl.ds(3 * piece + 1, 1), :piece] * keep

    def gather(near, other, line):
        copies = []
        for k in range(3):
            copy = remote(own.at[y, x], own.at[y, x], send.at[k], recv.at[k], time_pos, near[k])
            copy.start()
            copies.append(copy)
        for copy in copies:
            copy.wait_recv()
        later = []
        for k in range(3):
            copy = remote(line, line, send.at[3 + k], recv.at[3 + k], time_pos, other[k])
            copy.start()
            later.append(copy)
        return copies, later

    @pl.when(core == 0)
    def _():
        pl.semaphore_wait(barrier, 7)
        copies, later = gather(across, along, own.at[y])
        passed = []
        for k in range(4):
            if k:
                later[k - 1].wait_recv()
            line = (y + 4 - k) % 4
            copy = remote(own.at[line], prior.at[line], far_send.at[k], far_recv.at[k], time_pos + 1, row_pos)
            copy.start()
            passed.append(copy)
        for copy in copies + later + passed:
            copy.wait_send()

    @pl.when(core == 1)
    def _():
        pl.semaphore_wait(barrier, 6)
        copies, later = gather(along, across, own.at[:, x])
        for copy in later:
            copy.wait_recv()
        for copy in copies + later:
            copy.wait_send()
        for k in range(4):
            line = (y + 4 - k) % 4
            remote(own.at[line], prior.at[line], far_send.at[k], far_recv.at[k], time_pos, row_pos).wait_recv()


def step_kernel(own, own_vec, *refs, count, distance, parts):
    prior_refs, refs = refs[:count], refs[count:]
    prior_vec, inverse, pulled, new, new_vec = refs[:5]
    got, got_vec, refs = refs[5 : 5 + parts], refs[5 + parts], refs[6 + parts :]
    if parts > 1:
        next_inverse, next_pulled, error, *refs = refs
    packed, refs = refs[:3], refs[3:]
    far_send, far_recv, send, recv, twin_send, twin_recv, vec_send, vec_recv = refs[:8]
    tools = Tools(refs[8:])
    prior = prior_refs[0] if count == 1 else prior_refs
    z, core, y, x = places()
    time_pos, row_pos = lax.axis_index("tm"), lax.axis_index("row")
    reach, relay = distance, distance == 2
    barrier = pltpu.get_barrier_semaphore()
    target = (z // reach) % 2 == 1
    source = ((z // reach) % 2 == 0) & (z % reach == reach - 1) & (core == 1)
    source_pos = ((z // reach) * reach) * 2 - 1
    outer_pos = (1 - core) * y + core * x
    hops = 1 if relay else reach
    onward = target & ((z % reach) < reach - 1) if relay else None
    present = (time_pos // distance) % 2 == 1
    twin = 2 * z + 1 - core

    def view(ref, side, line):
        rows = ref.shape[0] // 8
        return ref.at[pl.ds(pl.multiple_of((side * 4 + line) * rows, 8), rows)]

    def outer_row(k):
        place = (outer_pos + k) % 4
        return (1 - core) * (place * 4 + x) + core * (y * 4 + place)

    @pl.when(target)
    def _():
        if relay:
            greet(barrier, (z % reach == 0) * source_pos + (z % reach != 0) * (time_pos - 2), row_pos)
        else:
            greet(barrier, source_pos, row_pos)
        for k in (1, 2, 3):
            greet(barrier, time_pos, outer_row(k))
        greet(barrier, twin, row_pos)

    @pl.when(present)
    def _():
        combine_cov(own, prior, inverse, new, tools)

    def deliver(part):
        for step in reversed(range(hops)):
            for side in range(2):
                slot = 2 * step + side
                line = y if side == 0 else x
                yield remote(
                    view(packed[part], side, line),
                    view(got[part], side, line),
                    far_send.at[part * 8 + slot],
                    far_recv.at[part],
                    time_pos + 1 + slot,
                    row_pos,
                )

    def deliver_vec():
        for slot in reversed(range(2 * hops)):
            yield remote(new_vec, got_vec, vec_send.at[slot], vec_recv, time_pos + 1 + slot, row_pos)

    @pl.when(source)
    def _():
        pack(new, packed, 0)
        pl.semaphore_wait(barrier, 2 * hops)
        for copy in deliver(0):
            copy.start()

    @pl.when(present)
    def _():
        combine_trans(own_vec, prior, prior_vec, inverse, pulled[0:1, :], new, new_vec, tools)

    if parts > 1:

        @pl.when(source)
        def _():
            pack(new, packed, 1)
            for copy in deliver(1):
                copy.start()

    @pl.when(present)
    def _():
        combine_info(own, own_vec, prior, prior_vec, new, new_vec, tools)

    @pl.when(jnp.logical_not(present))
    def _():
        new[...] = own[...]
        new_vec[...] = own_vec[...]

    @pl.when(source)
    def _():
        for copy in deliver_vec():
            copy.start()
        if parts > 1:
            pack(new, packed, 2)
            for copy in deliver(2):
                copy.start()
        for part in range(parts):
            for copy in deliver(part):
                copy.wait_send()
        for copy in deliver_vec():
            copy.wait_send()

    def onto(part):
        mine = view(got[part], core, outer_pos)
        return remote(mine, mine, far_send.at[part * 8], far_recv.at[part], time_pos + 2, row_pos)

    @pl.when(target)
    def _():
        if relay:

            @pl.when(onward)
            def _():
                pl.semaphore_wait(barrier, 5)

            @pl.when(jnp.logical_not(onward))
            def _():
                pl.semaphore_wait(barrier, 4)

        else:
            pl.semaphore_wait(barrier, 4)
        copies = []

        def over(k, part):
            mine = view(got[part], core, (outer_pos + 4 - k) % 4)
            slot = k * parts + part
            copy = remote(mine, mine, twin_send.at[slot], twin_recv.at[slot], twin, row_pos)
            copy.start()
            copies.append(copy)

        def pass_vec():
            arrived = remote(got_vec, got_vec, vec_send.at[0], vec_recv, time_pos + 2, row_pos)
            arrived.wait_recv()
            if relay:

                @pl.when(onward)
                def _():
                    arrived.start()

        def enter(part):
            onto(part).wait_recv()
            if relay:

                @pl.when(onward)
                def _():
                    onto(part).start()

            mine = view(got[part], core, outer_pos)
            for k in range(1, 4):
                slot = (k - 1) * parts + part
                copy = remote(mine, mine, send.at[slot], recv.at[slot], time_pos, outer_row(k))
                copy.start()
                copies.append(copy)
            over(0, part)

        def complete(part):
            for k in (1, 3, 2):
                line = view(got[part], core, (outer_pos + 4 - k) % 4)
                slot = (k - 1) * parts + part
                remote(line, line, send.at[slot], recv.at[slot], time_pos, outer_row(k)).wait_recv()
                over(k, part)
            for k in range(4):
                theirs = view(got[part], 1 - core, 0)
                slot = k * parts + part
                remote(theirs, theirs, twin_send.at[slot], twin_recv.at[slot], twin, row_pos).wait_recv()

        enter(0)
        complete(0)
        if parts > 1:
            upper, row = couple(new, new_vec, (got[0],), tools)
            next_pulled[...] = spread(row)[:8]
            newton = Newton(tools, upper, 1.0, next_inverse, tools.pairs[3], tools.pairs[4])
            enter(1)
            pass_vec()
            found = newton.fixed(lambda: enter(2))
            error[...] = jnp.zeros_like(error) + found
            complete(1)
            complete(2)
        else:
            pass_vec()
        for copy in copies:
            copy.wait_send()
        if relay:

            @pl.when(onward)
            def _():
                remote(got_vec, got_vec, vec_send.at[0], vec_recv, time_pos + 2, row_pos).wait_send()
                for part in range(parts):
                    onto(part).wait_send()


def chain_kernel(gain, offset, smooth, near_gain, near_offset, held, sent, state, *rest):
    refs, (send, recv) = rest[:-2], rest[-2:]
    product, one, two = refs
    z, core, _, _ = places()
    time_pos, row_pos = lax.axis_index("tm"), lax.axis_index("row")
    size = gain.shape[0]
    barrier = pltpu.get_barrier_semaphore()
    first, last = core == 0, z == 7

    @pl.when(first)
    def _():
        greet(barrier, time_pos + 1, row_pos)

    @pl.when(jnp.logical_not(last))
    def _():
        greet(barrier, 2 * z + 2, row_pos)

    put(two, gain[...])
    link = remote(gain, near_gain, send.at[0], recv.at[0], 2 * z, row_pos)
    small = remote(offset, near_offset, send.at[1], recv.at[1], 2 * z, row_pos)

    def apply(row8):
        high = row8.astype(BF16).astype(F32)
        both = jnp.concatenate([high, row8 - high], axis=0).astype(BF16)
        result = dot(both, two[0])
        return result[:8] + result[8:] + dot(both, two[1])[:8]

    @pl.when(core == 1)
    def _():
        pl.semaphore_wait(barrier, 1)
        small.start()

        @pl.when(jnp.logical_not(last))
        def _():
            link.start()

        state[...] = offset[...]

    @pl.when(first & (z > 0))
    def _():
        pl.semaphore_wait(barrier, 2)

    @pl.when(first & last)
    def _():
        small.wait_recv()
        state[...] = apply(near_offset[...]) + offset[...]

    @pl.when(first & jnp.logical_not(last))
    def _():
        small.wait_recv()
        state[...] = apply(near_offset[...]) + offset[...]
        link.wait_recv()
        put(one, near_gain[...])

        def part(index, carry):
            columns = pl.ds(pl.multiple_of(index * 256, 256), 256)
            high, low = two[0, :, columns], two[1, :, columns]
            product[:, columns] = dot(one[0], high) + dot(one[0], low) + dot(one[1], high)
            return carry

        lax.fori_loop(0, size // 256, part, 0)
        put(two, product[...])

    @pl.when(jnp.logical_not(last))
    def _():
        remote(held, held, send.at[2], recv.at[2], time_pos, row_pos).wait_recv()
        state[...] = state[...] + apply(held[...])

    @pl.when(first & (z > 0))
    def _():
        sent[...] = state[...]
        copies = [remote(sent, held, send.at[2 + k], recv.at[2], 2 * z - 2 + k, row_pos) for k in range(2)]
        for copy in copies:
            copy.start()
        for copy in copies:
            copy.wait_send()

    share(smooth, state[0:1, :], row_pos)

    @pl.when(core == 1)
    def _():
        small.wait_send()

        @pl.when(jnp.logical_not(last))
        def _():
            link.wait_send()


def body(trans, mean, cov, info, pull, dynamics, noise):
    piece, size = trans.shape[1:]
    shape = jax.ShapeDtypeStruct
    vmem = pl.BlockSpec(memory_space=pltpu.VMEM)
    dma = pltpu.SemaphoreType.DMA

    def params(mib, **more):
        return pltpu.CompilerParams(vmem_limit_bytes=mib * MIB, **more)

    slab = shape((4, 4, 10 * piece + 8, LANES), F32)
    mats_shape, vecs_shape = shape((3, size, size), F32), shape((8, LANES), F32)
    pair_shape, row_shape = shape((2, size, size), BF16), shape((8, size), F32)
    part_shapes = tuple(shape((count * LANES, LANES), F32) for count in (10, 16, 10))
    lines = jnp.pad(jnp.concatenate([mean, pull]), ((0, 6), (0, size - piece)))
    own_slabs, prior_slabs = pl.pallas_call(
        gather_kernel,
        out_shape=(slab, slab),
        in_specs=[vmem],
        out_specs=(vmem, vmem),
        scratch_shapes=[dma((6,)), dma((6,)), dma((4,)), dma((4,))],
        compiler_params=params(12, collective_id=0, has_side_effects=True),
    )(jnp.concatenate([trans[0], cov[0], info[0], lines]))

    mats, vecs, got, got_vec, inverse, pulled = pl.pallas_call(
        first_kernel,
        out_shape=(mats_shape, vecs_shape, mats_shape, vecs_shape, pair_shape, row_shape),
        in_specs=[vmem] * 2,
        out_specs=(vmem,) * 6,
        scratch_shapes=scratch_tools(size),
        compiler_params=params(28),
    )(own_slabs, prior_slabs)
    got = [got]

    for distance in (1, 2, 4):
        parts = 3 if distance < 4 else 1
        hops = 1 if distance < 4 else 4
        more = (pair_shape, row_shape, vecs_shape) if parts > 1 else ()
        mats, vecs, *rest = pl.pallas_call(
            functools.partial(step_kernel, count=len(got), distance=distance, parts=parts),
            out_shape=(mats_shape, vecs_shape, *part_shapes[:parts], vecs_shape, *more),
            in_specs=[vmem] * (5 + len(got)),
            out_specs=(vmem,) * (3 + parts + len(more)),
            scratch_shapes=[pltpu.VMEM(part.shape, F32) for part in part_shapes]
            + [dma((8 * parts,)), dma((parts,))]
            + [dma((3 * parts,))] * 2
            + [dma((4 * parts,))] * 2
            + [dma((2 * hops,)), dma]
            + scratch_tools(size),
            compiler_params=params(28, collective_id=1 + distance, has_side_effects=True),
        )(mats, vecs, *got, got_vec, inverse, pulled)
        got, got_vec = rest[:parts], rest[parts]
        if parts > 1:
            found, pulled, error = rest[parts + 1 :]
            inverse = pl.pallas_call(
                functools.partial(repair_kernel, distance=2 * distance),
                out_shape=pair_shape,
                in_specs=[vmem] * 5,
                out_specs=vmem,
                scratch_shapes=scratch_tools(size),
                input_output_aliases={3: 0},
                compiler_params=params(28),
            )(mats, vecs, got[0], found, error)

    gain, offset, cov_out, mean_out = pl.pallas_call(
        functools.partial(gain_kernel, distance=8),
        out_shape=(
            shape((size, size), F32),
            shape((8, size), F32),
            shape((piece, size), F32),
            shape((1, piece), F32),
        ),
        in_specs=[vmem] * 6,
        out_specs=(vmem,) * 4,
        scratch_shapes=[pltpu.VMEM((1, size, size), F32), pltpu.VMEM((8, LANES), F32), pltpu.VMEM((8, size), F32)]
        + scratch_tools(size),
        compiler_params=params(28),
    )(mats, vecs, *got, got_vec, dynamics[0], noise[0])

    smooth = pl.pallas_call(
        chain_kernel,
        out_shape=shape((1, piece), F32),
        in_specs=[vmem] * 2,
        out_specs=vmem,
        scratch_shapes=[
            pltpu.VMEM((size, size), F32),
            pltpu.VMEM((8, size), F32),
            pltpu.VMEM((8, size), F32),
            pltpu.VMEM((8, size), F32),
            pltpu.VMEM((8, size), F32),
            pltpu.VMEM((size, size), F32),
            pltpu.VMEM((2, size, size), BF16),
            pltpu.VMEM((2, size, size), BF16),
            dma((4,)),
            dma((3,)),
        ],
        compiler_params=params(12, collective_id=1, has_side_effects=True),
    )(gain, offset)

    return smooth, mean_out, cov_out[None]


def solution(mesh):
    in_specs = (
        P("tm", "row", None),
        P("tm", "row"),
        P("tm", "row", None),
        P("tm", "row", None),
        P("tm", "row"),
        P("tm", None, None),
        P("tm", None, None),
    )
    out_specs = (P("tm", "row"), P("tm", "row"), P("tm", "row", None))
    return jax.shard_map(body, mesh=mesh, in_specs=in_specs, out_specs=out_specs, check_vma=False)
```

```python
import functools

import jax
import jax.numpy as jnp
from jax import lax
from jax.experimental import pallas as pl
from jax.experimental.pallas import tpu as pltpu
from jax.sharding import PartitionSpec as P

MESH = pl.DeviceIdType.MESH
F32, BF16 = jnp.float32, jnp.bfloat16
NN = (((1,), (0,)), ((), ()))
NT = (((1,), (1,)), ((), ()))
TN = (((0,), (0,)), ((), ()))
VROWS = 16
LANES = 128
REACH = 0.008
SMALL = 4e-3
STEPS = 3
MIB = 1024 * 1024


def places():
    time_pos, row_pos = lax.axis_index("tm"), lax.axis_index("row")
    return time_pos // 2, time_pos % 2, row_pos // 4, row_pos % 4


def dot(lhs, rhs, dims=NN):
    return lax.dot_general(lhs, rhs, dims, preferred_element_type=F32)


def put(pair, value, start=0, column=0):
    high = value.astype(BF16)
    rows, columns = pl.ds(start, value.shape[0]), pl.ds(column, value.shape[1])
    pair[0, rows, columns] = high
    pair[1, rows, columns] = (value - high.astype(F32)).astype(BF16)


def put_high(pair, value):
    pair[0, : value.shape[0], :] = value.astype(BF16)


class Tools:
    def __init__(self, refs):
        self.product, self.value, *self.pairs = refs
        self.size = self.value.shape[0]

    def times(self, lhs, rhs, dims=NN, rows=None):
        size = self.size
        rows = lhs.shape[1] if rows is None else rows
        high, low = rhs[0, :size, :], rhs[1, :size, :]
        left = lhs[0, :rows, :]
        return dot(left, high, dims) + dot(left, low, dims) + dot(lhs[1, :rows, :], high, dims)

    def thin(self, lhs, rhs):
        size = self.size
        high = lhs.astype(BF16)
        low = (lhs - high.astype(F32)).astype(BF16)
        return dot(high, rhs[0, :size, :]) + dot(high, rhs[1, :size, :]) + dot(low, rhs[0, :size, :])


def scratch_tools(size):
    tall = size + VROWS
    return [pltpu.VMEM((tall, size), F32), pltpu.VMEM((size, size), F32)] + [
        pltpu.VMEM((2, tall if index in (0, 4, 5) else size, size), BF16) for index in range(6)
    ]


def eye(size):
    rows = lax.broadcasted_iota(jnp.int32, (size, size), 0)
    return (rows == lax.broadcasted_iota(jnp.int32, (size, size), 1)).astype(F32)


class Newton:
    def __init__(self, tools, upper, lower, out, mat, work):
        self.tools, self.size, self.value, self.product = tools, tools.size, tools.value, tools.product
        self.out, self.mat, self.work = out, mat, work
        self.first = 2.0 / (upper + lower)
        self.opening = (upper - lower) / (upper + lower)

    @staticmethod
    def scale_of(bound):
        return 2.0 / (2.0 - bound * bound)

    def after(self, bound):
        return bound * bound * 0.5 * self.scale_of(bound)

    def start(self):
        whole = self.mat[0].astype(F32) + self.mat[1].astype(F32)
        new = (self.scale_of(self.opening) * self.first) * (2.0 * eye(self.size) - self.first * whole)
        self.value[...] = new
        put(self.out, new)
        return self.after(self.opening)

    def coarse(self, bound):
        size, out, work = self.size, self.out, self.work
        put_high(work, eye(size) - dot(self.mat[0], out[0]))
        new = self.scale_of(bound) * (self.value[...] + dot(out[0], work[0, :size, :]))
        self.value[...] = new
        put_high(out, new)
        return self.after(bound)

    def add(self, lhs, rhs, sign):
        size, product = self.size, self.product

        def one(index, carry):
            product[:size, :] += sign * dot(lhs[index // 2, :size, :], rhs[index % 2, :size, :])
            return carry

        lax.fori_loop(0, 3, one, 0)

    def careful(self, bound):
        size, product = self.size, self.product
        product[:size, :] = eye(size)
        self.add(self.mat, self.out, -1.0)
        put(self.work, product[:size, :])
        product[:size, :] = self.value[...]
        self.add(self.out, self.work, 1.0)
        self.settle(self.scale_of(bound) * product[:size, :])
        return self.after(bound)

    def settle(self, new):
        self.value[...] = new
        put(self.out, new)

    def check(self):
        residual = eye(self.size) - self.tools.times(self.mat, self.out)
        self.product[: self.size, :] = residual
        put_high(self.work, residual)
        return jnp.sum(residual * residual)

    def step(self):
        self.settle(self.value[...] + dot(self.out[0], self.work[0, : self.size, :]))

    def last_step(self):
        small = self.work[0, : self.size, :]
        put_high(self.work, self.product[: self.size, :] + dot(small, small))
        put(self.out, self.value[...] + dot(self.out[0], self.work[0, : self.size, :]))

    def whole(self):
        def from_start(error):
            lax.while_loop(lambda bound: bound > REACH, self.careful, self.start())
            return self.check()

        def again(carry):
            self.step()
            return carry[0] + 1, self.check()

        lax.while_loop(lambda bound: bound > REACH, self.coarse, self.start())
        put(self.out, self.value[...])
        error = self.check()
        error = lax.cond(error < 1.0, lambda e: e, from_start, error)
        lax.while_loop(lambda c: (c[0] < 60) & (c[1] > SMALL), again, (jnp.int32(0), error))
        self.last_step()

    def fixed(self):
        lax.fori_loop(0, STEPS, lambda _, bound: self.coarse(bound), self.start())
        put(self.out, self.value[...])

        def plain(index, error):
            error = self.check()

            @pl.when(index == 0)
            def _():
                self.step()

            return error

        error = lax.fori_loop(0, 2, plain, jnp.float32(0.0))
        self.last_step()
        return error


def one_norm(matrix):
    return jnp.max(jnp.sum(jnp.abs(matrix), axis=0, keepdims=True))


def spread(row):
    return jnp.broadcast_to(row, (VROWS, row.shape[1]))


def row_of(tile, start):
    return jnp.concatenate([tile[start + i : start + i + 1, :] for i in range(4)], axis=1)


def set_row(tile, start, row):
    for i in range(4):
        tile[start + i : start + i + 1, :] = row[0:1, i * LANES : (i + 1) * LANES]


UPPER = [(i, j) for i in range(4) for j in range(i, 4)]
FULL = [(i, j) for i in range(4) for j in range(4)]
BLOCKS = {0: (0, 0, UPPER), 2: (1, 0, UPPER), 1: (1, 10, FULL)}


def each_block(packed, which):
    part, base, places_of = BLOCKS[which]
    for index, (i, j) in enumerate(places_of):
        value = packed[part][pl.ds((base + index) * LANES, LANES), :]
        yield i * LANES, j * LANES, value
        if places_of is UPPER and i != j:
            yield j * LANES, i * LANES, value.T


def pack(mats, packed, which):
    part, base, places_of = BLOCKS[which]
    for index, (i, j) in enumerate(places_of):
        packed[part][pl.ds((base + index) * LANES, LANES), :] = mats[
            which, pl.ds(i * LANES, LANES), pl.ds(j * LANES, LANES)
        ]


def fill(prior, which, pair):
    if isinstance(prior, tuple):
        for i, j, value in each_block(prior, which):
            put(pair, value, i, j)
    else:
        put(pair, prior[which])


def increase(mats, which, prior):
    if isinstance(prior, tuple):
        for i, j, value in each_block(prior, which):
            rows, columns = pl.ds(i, LANES), pl.ds(j, LANES)
            mats[which, rows, columns] = mats[which, rows, columns] + value
    else:
        mats[which] = mats[which] + prior[which]


def couple(own, own_vec, prior, inverse, tools):
    size = tools.size
    one, two, three, four, five, six = tools.pairs
    put(one, own[2])
    put(one, spread(row_of(own_vec, 4)), size)
    fill(prior, 0, two)
    coupling = tools.times(one, two)
    pulled = coupling[size : size + 1]
    coupling = coupling[:size]
    upper = 2.0 + one_norm(coupling)
    put(four, eye(size) + coupling)
    return Newton(tools, upper, 1.0, inverse, four, five), pulled


def combine_cov(own, prior, inverse, new, tools):
    times = tools.times
    one, two, three, four, five, six = tools.pairs
    fill(prior, 0, two)
    put(four, own[1])
    put(five, times(two, inverse))
    put(six, times(five, four, rows=tools.size))
    new[0] = times(four, six, TN) + own[0]


def combine_rest(own, own_vec, prior, prior_vec, inverse, pulled_row, new, new_vec, tools):
    size, times = tools.size, tools.times
    one, two, three, four, five, six = tools.pairs
    prior_mean, prior_pull = row_of(prior_vec, 0), row_of(prior_vec, 4)
    mean, pull = row_of(own_vec, 0), row_of(own_vec, 4)
    fill(prior, 1, five)
    put(five, spread(prior_mean + pulled_row), size)
    gained = times(five, inverse)
    put(two, gained[:size])
    put(six, gained)
    moved = times(six, four)
    new[1] = moved[:size]
    set_row(new_vec, 0, moved[size : size + 1] + mean)
    put(three, own[2])
    put(five, spread(prior_mean), size)
    pulled = times(five, three)
    put(six, pulled[:size])
    put(six, spread(pull - pulled[size : size + 1]), size)
    informed = times(six, two, NT)
    new[2] = informed[:size]
    increase(new, 2, prior)
    set_row(new_vec, 4, informed[size : size + 1] + prior_pull)


def unpack(slabs, mats, vecs):
    piece = mats.shape[1] // 16
    for y in range(4):
        total = None
        for x in range(4):
            rows = pl.ds((4 * y + x) * piece, piece)
            for index in range(10):
                which = 1 if index < 4 else 0 if index < 7 else 2
                group = index if index < 4 else (y + (index - 4) % 3) % 4
                mats[which, rows, pl.ds(group * LANES, LANES)] = slabs[y, x, pl.ds(index * piece, piece), :]
            tile = slabs[y, x, pl.ds(10 * piece, 8), :]
            total = tile if total is None else total + tile
        vecs[y : y + 1, :] = total[0:1, :]
        vecs[4 + y : 5 + y, :] = total[1:2, :]
    mats[1] = mats[1].T
    for which in (0, 2):
        for y in range(4):
            left, right = pl.ds(y * LANES, LANES), pl.ds((y + 3) % 4 * LANES, LANES)
            mats[which, left, right] = mats[which, right, left].T


def first_kernel(own_slabs, prior_slabs, own, own_vec, prior, prior_vec, inverse, pulled, *refs):
    odd = lax.axis_index("tm") % 2 == 1
    unpack(own_slabs, own, own_vec)

    @pl.when(odd)
    def _():
        unpack(prior_slabs, prior, prior_vec)
        newton, row = couple(own, own_vec, prior, inverse, Tools(refs))
        pulled[...] = spread(row)[:8]
        newton.whole()


def repair_kernel(own, own_vec, prior_cov, found, error, inverse, *refs, distance):
    @pl.when((lax.axis_index("tm") // distance) % 2 == 1)
    def _():
        @pl.when(jnp.logical_not(jnp.max(error[...]) < SMALL))
        def _():
            newton, _ = couple(own, own_vec, (prior_cov,), inverse, Tools(refs))
            newton.whole()


def gain_kernel(
    own, own_vec, prior_cov, prior_vec, dynamics, noise, gain, offset, cov_out, mean_out, new, mean_tile, *refs, distance
):
    tools = Tools(refs)
    size, times, thin = tools.size, tools.times, tools.thin
    time_pos, row_pos = lax.axis_index("tm"), lax.axis_index("row")
    present = (time_pos // distance) % 2 == 1
    one, two, three, four, five, six = tools.pairs

    @pl.when(present)
    def _():
        prior = (prior_cov,)
        newton, row = couple(own, own_vec, prior, three, tools)
        newton.whole()
        combine_cov(own, prior, three, new, tools)
        moved = thin(thin(spread(row_of(prior_vec, 0) + row), three), four)
        set_row(mean_tile, 0, moved[0:1] + row_of(own_vec, 0))

    @pl.when(jnp.logical_not(present))
    def _():
        new[0] = own[0]
        mean_tile[...] = own_vec[...]

    piece = cov_out.shape[0]
    cov_out[...] = new[0, pl.ds(pl.multiple_of(row_pos * piece, piece), piece), :]
    mean = row_of(mean_tile, 0)
    share(mean_out, mean, row_pos)

    @pl.when(time_pos == 15)
    def _():
        gain[...] = jnp.zeros_like(gain)
        offset[...] = jnp.broadcast_to(mean, offset.shape)

    @pl.when(time_pos < 15)
    def _():
        put(two, dynamics[...])
        put(three, new[0])
        put(one, times(two, three))
        put(one, spread(mean), size)
        projected = times(one, two, NT)
        predicted = projected[size:]
        innovation = projected[:size] + noise[...]
        upper = one_norm(innovation)
        put(four, innovation)
        Newton(tools, upper, upper * 0.004, three, four, two).whole()
        weights = times(three, one)
        gain[...] = weights
        put(six, weights)
        offset[...] = mean - thin(predicted, six)[:8]


def share(out, row, row_pos):
    piece = out.shape[1]
    for index in range(16):

        @pl.when(row_pos == index)
        def _():
            out[...] = row[0:1, index * piece : (index + 1) * piece]


def remote(src, dst, send, recv, tm, row):
    return pltpu.make_async_remote_copy(
        src_ref=src, dst_ref=dst, send_sem=send, recv_sem=recv, device_id=(tm, row), device_id_type=MESH
    )


def greet(barrier, tm, row):
    pl.semaphore_signal(barrier, inc=1, device_id=(tm, row), device_id_type=MESH)


def gather_kernel(rows, own, prior, send, recv, far_send, far_recv):
    z, core, y, x = places()
    time_pos, row_pos = lax.axis_index("tm"), lax.axis_index("row")
    piece = (rows.shape[0] - 8) // 3
    keep = (time_pos > 0).astype(F32)
    barrier = pltpu.get_barrier_semaphore()
    across = [y * 4 + (x + k) % 4 for k in (1, 2, 3)]
    along = [((y + k) % 4) * 4 + x for k in (1, 2, 3)]
    for peer in across + along:
        greet(barrier, time_pos, peer)

    @pl.when(core == 1)
    def _():
        greet(barrier, time_pos - 1, row_pos)

    for index in range(4):
        columns = pl.ds(index * LANES, LANES)
        own[y, x, pl.ds(index * piece, piece), :] = rows[pl.ds(0, piece), columns] * keep
    for index in range(3):
        columns = pl.ds(pl.multiple_of((y + index) % 4 * LANES, LANES), LANES)
        own[y, x, pl.ds((4 + index) * piece, piece), :] = rows[pl.ds(piece, piece), columns]
        own[y, x, pl.ds((7 + index) * piece, piece), :] = rows[pl.ds(2 * piece, piece), columns] * keep
    own[y, x, pl.ds(10 * piece, 8), :] = jnp.zeros((8, LANES), F32)
    for index in range(4):

        @pl.when(x == index)
        def _():
            lanes = pl.ds(index * piece, piece)
            own[y, x, pl.ds(10 * piece, 1), lanes] = rows[pl.ds(3 * piece, 1), :piece]
            own[y, x, pl.ds(10 * piece + 1, 1), lanes] = rows[pl.ds(3 * piece + 1, 1), :piece] * keep

    def gather(near, other, line):
        copies = []
        for k in range(3):
            copy = remote(own.at[y, x], own.at[y, x], send.at[k], recv.at[k], time_pos, near[k])
            copy.start()
            copies.append(copy)
        for copy in copies:
            copy.wait_recv()
        later = []
        for k in range(3):
            copy = remote(line, line, send.at[3 + k], recv.at[3 + k], time_pos, other[k])
            copy.start()
            later.append(copy)
        return copies, later

    @pl.when(core == 0)
    def _():
        pl.semaphore_wait(barrier, 7)
        copies, later = gather(across, along, own.at[y])
        passed = []
        for k in range(4):
            if k:
                later[k - 1].wait_recv()
            line = (y + 4 - k) % 4
            copy = remote(own.at[line], prior.at[line], far_send.at[k], far_recv.at[k], time_pos + 1, row_pos)
            copy.start()
            passed.append(copy)
        for copy in copies + later + passed:
            copy.wait_send()

    @pl.when(core == 1)
    def _():
        pl.semaphore_wait(barrier, 6)
        copies, later = gather(along, across, own.at[:, x])
        for copy in later:
            copy.wait_recv()
        for copy in copies + later:
            copy.wait_send()
        for k in range(4):
            line = (y + 4 - k) % 4
            remote(own.at[line], prior.at[line], far_send.at[k], far_recv.at[k], time_pos, row_pos).wait_recv()


def step_kernel(own, own_vec, *refs, count, distance, parts):
    prior_refs, refs = refs[:count], refs[count:]
    prior_vec, inverse, pulled, new, new_vec = refs[:5]
    got, got_vec, refs = refs[5 : 5 + parts], refs[5 + parts], refs[6 + parts :]
    if parts > 1:
        next_inverse, next_pulled, error, *refs = refs
    packed, refs = refs[:2], refs[2:]
    far_send, far_recv, send, recv, twin_send, twin_recv, vec_send, vec_recv = refs[:8]
    tools = Tools(refs[8:])
    prior = prior_refs[0] if count == 1 else prior_refs
    z, core, y, x = places()
    time_pos, row_pos = lax.axis_index("tm"), lax.axis_index("row")
    reach, relay = distance, distance == 2
    barrier = pltpu.get_barrier_semaphore()
    target = (z // reach) % 2 == 1
    source = ((z // reach) % 2 == 0) & (z % reach == reach - 1) & (core == 1)
    source_pos = ((z // reach) * reach) * 2 - 1
    outer_pos = (1 - core) * y + core * x
    hops = 1 if relay else reach
    onward = target & ((z % reach) < reach - 1) if relay else None
    present = (time_pos // distance) % 2 == 1
    twin = 2 * z + 1 - core

    def view(ref, side, line):
        rows = ref.shape[0] // 8
        return ref.at[pl.ds(pl.multiple_of((side * 4 + line) * rows, 8), rows)]

    def outer_row(k):
        place = (outer_pos + k) % 4
        return (1 - core) * (place * 4 + x) + core * (y * 4 + place)

    @pl.when(target)
    def _():
        if relay:
            greet(barrier, (z % reach == 0) * source_pos + (z % reach != 0) * (time_pos - 2), row_pos)
        else:
            greet(barrier, source_pos, row_pos)
        for k in (1, 2, 3):
            greet(barrier, time_pos, outer_row(k))
        greet(barrier, twin, row_pos)

    @pl.when(present)
    def _():
        combine_cov(own, prior, inverse, new, tools)

    def deliver(part):
        for step in reversed(range(hops)):
            for side in range(2):
                slot = 2 * step + side
                line = y if side == 0 else x
                yield remote(
                    view(packed[part], side, line),
                    view(got[part], side, line),
                    far_send.at[part * 8 + slot],
                    far_recv.at[part],
                    time_pos + 1 + slot,
                    row_pos,
                )

    def deliver_vec():
        for slot in reversed(range(2 * hops)):
            yield remote(new_vec, got_vec, vec_send.at[slot], vec_recv, time_pos + 1 + slot, row_pos)

    @pl.when(source)
    def _():
        pack(new, packed, 0)
        pl.semaphore_wait(barrier, 2 * hops)
        for copy in deliver(0):
            copy.start()

    @pl.when(present)
    def _():
        combine_rest(own, own_vec, prior, prior_vec, inverse, pulled[0:1, :], new, new_vec, tools)

    @pl.when(jnp.logical_not(present))
    def _():
        new[...] = own[...]
        new_vec[...] = own_vec[...]

    @pl.when(source)
    def _():
        for copy in deliver_vec():
            copy.start()
        if parts > 1:
            pack(new, packed, 2)
            pack(new, packed, 1)
            for copy in deliver(1):
                copy.start()
        for part in range(parts):
            for copy in deliver(part):
                copy.wait_send()
        for copy in deliver_vec():
            copy.wait_send()

    def onto(part):
        mine = view(got[part], core, outer_pos)
        return remote(mine, mine, far_send.at[part * 8], far_recv.at[part], time_pos + 2, row_pos)

    @pl.when(target)
    def _():
        if relay:

            @pl.when(onward)
            def _():
                pl.semaphore_wait(barrier, 5)

            @pl.when(jnp.logical_not(onward))
            def _():
                pl.semaphore_wait(barrier, 4)

        else:
            pl.semaphore_wait(barrier, 4)
        copies = []

        def over(k, part):
            mine = view(got[part], core, (outer_pos + 4 - k) % 4)
            slot = k * parts + part
            copy = remote(mine, mine, twin_send.at[slot], twin_recv.at[slot], twin, row_pos)
            copy.start()
            copies.append(copy)

        def pass_vec():
            arrived = remote(got_vec, got_vec, vec_send.at[0], vec_recv, time_pos + 2, row_pos)
            arrived.wait_recv()
            if relay:

                @pl.when(onward)
                def _():
                    arrived.start()

        def enter(part):
            onto(part).wait_recv()
            if relay:

                @pl.when(onward)
                def _():
                    onto(part).start()

            mine = view(got[part], core, outer_pos)
            for k in range(1, 4):
                slot = (k - 1) * parts + part
                copy = remote(mine, mine, send.at[slot], recv.at[slot], time_pos, outer_row(k))
                copy.start()
                copies.append(copy)
            over(0, part)

        def complete(part):
            for k in (1, 3, 2):
                line = view(got[part], core, (outer_pos + 4 - k) % 4)
                slot = (k - 1) * parts + part
                remote(line, line, send.at[slot], recv.at[slot], time_pos, outer_row(k)).wait_recv()
                over(k, part)
            for k in range(4):
                theirs = view(got[part], 1 - core, 0)
                slot = k * parts + part
                remote(theirs, theirs, twin_send.at[slot], twin_recv.at[slot], twin, row_pos).wait_recv()

        enter(0)
        complete(0)
        if parts > 1:
            newton, row = couple(new, new_vec, (got[0],), next_inverse, tools)
            next_pulled[...] = spread(row)[:8]
            enter(1)
            pass_vec()
            error[...] = jnp.zeros_like(error) + newton.fixed()
            complete(1)
        else:
            pass_vec()
        for copy in copies:
            copy.wait_send()
        if relay:

            @pl.when(onward)
            def _():
                remote(got_vec, got_vec, vec_send.at[0], vec_recv, time_pos + 2, row_pos).wait_send()
                for part in range(parts):
                    onto(part).wait_send()


def chain_kernel(gain, offset, smooth, near_gain, near_offset, held, sent, state, *rest):
    refs, (send, recv) = rest[:-2], rest[-2:]
    product, one, two = refs
    z, core, _, _ = places()
    time_pos, row_pos = lax.axis_index("tm"), lax.axis_index("row")
    size = gain.shape[0]
    barrier = pltpu.get_barrier_semaphore()
    first, last = core == 0, z == 7

    @pl.when(first)
    def _():
        greet(barrier, time_pos + 1, row_pos)

    @pl.when(jnp.logical_not(last))
    def _():
        greet(barrier, 2 * z + 2, row_pos)

    put(two, gain[...])
    link = remote(gain, near_gain, send.at[0], recv.at[0], 2 * z, row_pos)
    small = remote(offset, near_offset, send.at[1], recv.at[1], 2 * z, row_pos)

    def apply(row8):
        high = row8.astype(BF16).astype(F32)
        both = jnp.concatenate([high, row8 - high], axis=0).astype(BF16)
        result = dot(both, two[0])
        return result[:8] + result[8:] + dot(both, two[1])[:8]

    @pl.when(core == 1)
    def _():
        pl.semaphore_wait(barrier, 1)
        small.start()

        @pl.when(jnp.logical_not(last))
        def _():
            link.start()

        state[...] = offset[...]

    @pl.when(first & (z > 0))
    def _():
        pl.semaphore_wait(barrier, 2)

    @pl.when(first & last)
    def _():
        small.wait_recv()
        state[...] = apply(near_offset[...]) + offset[...]

    @pl.when(first & jnp.logical_not(last))
    def _():
        small.wait_recv()
        state[...] = apply(near_offset[...]) + offset[...]
        link.wait_recv()
        put(one, near_gain[...])

        def part(index, carry):
            columns = pl.ds(pl.multiple_of(index * 256, 256), 256)
            high, low = two[0, :, columns], two[1, :, columns]
            product[:, columns] = dot(one[0], high) + dot(one[0], low) + dot(one[1], high)
            return carry

        lax.fori_loop(0, size // 256, part, 0)
        put(two, product[...])

    @pl.when(jnp.logical_not(last))
    def _():
        remote(held, held, send.at[2], recv.at[2], time_pos, row_pos).wait_recv()
        state[...] = state[...] + apply(held[...])

    @pl.when(first & (z > 0))
    def _():
        sent[...] = state[...]
        copies = [remote(sent, held, send.at[2 + k], recv.at[2], 2 * z - 2 + k, row_pos) for k in range(2)]
        for copy in copies:
            copy.start()
        for copy in copies:
            copy.wait_send()

    share(smooth, state[0:1, :], row_pos)

    @pl.when(core == 1)
    def _():
        small.wait_send()

        @pl.when(jnp.logical_not(last))
        def _():
            link.wait_send()


def body(trans, mean, cov, info, pull, dynamics, noise):
    piece, size = trans.shape[1:]
    shape = jax.ShapeDtypeStruct
    vmem = pl.BlockSpec(memory_space=pltpu.VMEM)
    dma = pltpu.SemaphoreType.DMA

    def params(mib, **more):
        return pltpu.CompilerParams(vmem_limit_bytes=mib * MIB, **more)

    slab = shape((4, 4, 10 * piece + 8, LANES), F32)
    mats_shape, vecs_shape = shape((3, size, size), F32), shape((8, LANES), F32)
    pair_shape, row_shape = shape((2, size, size), BF16), shape((8, size), F32)
    part_shapes = shape((10 * LANES, LANES), F32), shape((26 * LANES, LANES), F32)
    lines = jnp.pad(jnp.concatenate([mean, pull]), ((0, 6), (0, size - piece)))
    own_slabs, prior_slabs = pl.pallas_call(
        gather_kernel,
        out_shape=(slab, slab),
        in_specs=[vmem],
        out_specs=(vmem, vmem),
        scratch_shapes=[dma((6,)), dma((6,)), dma((4,)), dma((4,))],
        compiler_params=params(12, collective_id=0, has_side_effects=True),
    )(jnp.concatenate([trans[0], cov[0], info[0], lines]))

    mats, vecs, got, got_vec, inverse, pulled = pl.pallas_call(
        first_kernel,
        out_shape=(mats_shape, vecs_shape, mats_shape, vecs_shape, pair_shape, row_shape),
        in_specs=[vmem] * 2,
        out_specs=(vmem,) * 6,
        scratch_shapes=scratch_tools(size),
        compiler_params=params(28),
    )(own_slabs, prior_slabs)
    got = [got]

    for distance in (1, 2, 4):
        parts = 2 if distance < 4 else 1
        hops = 1 if distance < 4 else 4
        more = (pair_shape, row_shape, vecs_shape) if parts > 1 else ()
        mats, vecs, *rest = pl.pallas_call(
            functools.partial(step_kernel, count=len(got), distance=distance, parts=parts),
            out_shape=(mats_shape, vecs_shape, *part_shapes[:parts], vecs_shape, *more),
            in_specs=[vmem] * (5 + len(got)),
            out_specs=(vmem,) * (3 + parts + len(more)),
            scratch_shapes=[pltpu.VMEM(part.shape, F32) for part in part_shapes]
            + [dma((8 * parts,)), dma((parts,))]
            + [dma((3 * parts,))] * 2
            + [dma((4 * parts,))] * 2
            + [dma((2 * hops,)), dma]
            + scratch_tools(size),
            compiler_params=params(28, collective_id=1 + distance, has_side_effects=True),
        )(mats, vecs, *got, got_vec, inverse, pulled)
        got, got_vec = rest[:parts], rest[parts]
        if parts > 1:
            found, pulled, error = rest[parts + 1 :]
            inverse = pl.pallas_call(
                functools.partial(repair_kernel, distance=2 * distance),
                out_shape=pair_shape,
                in_specs=[vmem] * 5,
                out_specs=vmem,
                scratch_shapes=scratch_tools(size),
                input_output_aliases={3: 0},
                compiler_params=params(28),
            )(mats, vecs, got[0], found, error)

    gain, offset, cov_out, mean_out = pl.pallas_call(
        functools.partial(gain_kernel, distance=8),
        out_shape=(
            shape((size, size), F32),
            shape((8, size), F32),
            shape((piece, size), F32),
            shape((1, piece), F32),
        ),
        in_specs=[vmem] * 6,
        out_specs=(vmem,) * 4,
        scratch_shapes=[pltpu.VMEM((1, size, size), F32), pltpu.VMEM((8, LANES), F32)] + scratch_tools(size),
        compiler_params=params(28),
    )(mats, vecs, *got, got_vec, dynamics[0], noise[0])

    smooth = pl.pallas_call(
        chain_kernel,
        out_shape=shape((1, piece), F32),
        in_specs=[vmem] * 2,
        out_specs=vmem,
        scratch_shapes=[
            pltpu.VMEM((size, size), F32),
            pltpu.VMEM((8, size), F32),
            pltpu.VMEM((8, size), F32),
            pltpu.VMEM((8, size), F32),
            pltpu.VMEM((8, size), F32),
            pltpu.VMEM((size, size), F32),
            pltpu.VMEM((2, size, size), BF16),
            pltpu.VMEM((2, size, size), BF16),
            dma((4,)),
            dma((3,)),
        ],
        compiler_params=params(12, collective_id=1, has_side_effects=True),
    )(gain, offset)

    return smooth, mean_out, cov_out[None]


def solution(mesh):
    in_specs = (
        P("tm", "row", None),
        P("tm", "row"),
        P("tm", "row", None),
        P("tm", "row", None),
        P("tm", "row"),
        P("tm", None, None),
        P("tm", None, None),
    )
    out_specs = (P("tm", "row"), P("tm", "row"), P("tm", "row", None))
    return jax.shard_map(body, mesh=mesh, in_specs=in_specs, out_specs=out_specs, check_vma=False)
```

```python
import functools

import jax
import jax.numpy as jnp
from jax import lax
from jax.experimental import pallas as pl
from jax.experimental.pallas import tpu as pltpu
from jax.sharding import PartitionSpec as P

MESH = pl.DeviceIdType.MESH
F32, BF16 = jnp.float32, jnp.bfloat16
NN = (((1,), (0,)), ((), ()))
NT = (((1,), (1,)), ((), ()))
TN = (((0,), (0,)), ((), ()))
VROWS = 16
LANES = 128
REACH = 0.008
SMALL = 4e-3
STEPS = 3
MIB = 1024 * 1024


def places():
    time_pos, row_pos = lax.axis_index("tm"), lax.axis_index("row")
    return time_pos // 2, time_pos % 2, row_pos // 4, row_pos % 4


def dot(lhs, rhs, dims=NN):
    return lax.dot_general(lhs, rhs, dims, preferred_element_type=F32)


def put(pair, value, start=0, column=0):
    high = value.astype(BF16)
    rows, columns = pl.ds(start, value.shape[0]), pl.ds(column, value.shape[1])
    pair[0, rows, columns] = high
    pair[1, rows, columns] = (value - high.astype(F32)).astype(BF16)


def put_high(pair, value):
    pair[0, : value.shape[0], :] = value.astype(BF16)


class Tools:
    def __init__(self, refs):
        self.product, self.value, *self.pairs = refs
        self.size = self.value.shape[0]

    def times(self, lhs, rhs, dims=NN, rows=None):
        size = self.size
        rows = lhs.shape[1] if rows is None else rows
        high, low = rhs[0, :size, :], rhs[1, :size, :]
        left = lhs[0, :rows, :]
        return dot(left, high, dims) + dot(left, low, dims) + dot(lhs[1, :rows, :], high, dims)

    def thin(self, lhs, rhs):
        size = self.size
        high = lhs.astype(BF16)
        low = (lhs - high.astype(F32)).astype(BF16)
        return dot(high, rhs[0, :size, :]) + dot(high, rhs[1, :size, :]) + dot(low, rhs[0, :size, :])


def scratch_tools(size):
    tall = size + VROWS
    return [pltpu.VMEM((tall, size), F32), pltpu.VMEM((size, size), F32)] + [
        pltpu.VMEM((2, tall if index in (0, 4, 5) else size, size), BF16) for index in range(6)
    ]


def eye(size):
    rows = lax.broadcasted_iota(jnp.int32, (size, size), 0)
    return (rows == lax.broadcasted_iota(jnp.int32, (size, size), 1)).astype(F32)


class Newton:
    def __init__(self, tools, upper, lower, out, mat, work):
        self.tools, self.size, self.value, self.product = tools, tools.size, tools.value, tools.product
        self.out, self.mat, self.work = out, mat, work
        self.upper = upper
        self.first = 2.0 / (upper + lower)
        self.opening = (upper - lower) / (upper + lower)

    @staticmethod
    def scale_of(bound):
        return 2.0 / (2.0 - bound * bound)

    def after(self, bound):
        return bound * bound * 0.5 * self.scale_of(bound)

    def start(self):
        whole = self.mat[0].astype(F32) + self.mat[1].astype(F32)
        new = (self.scale_of(self.opening) * self.first) * (2.0 * eye(self.size) - self.first * whole)
        self.value[...] = new
        put(self.out, new)
        return self.after(self.opening)

    def coarse(self, bound):
        size, out, work = self.size, self.out, self.work
        put_high(work, eye(size) - dot(self.mat[0], out[0]))
        new = self.scale_of(bound) * (self.value[...] + dot(out[0], work[0, :size, :]))
        self.value[...] = new
        put_high(out, new)
        return self.after(bound)

    def add(self, lhs, rhs, sign):
        size, product = self.size, self.product

        def one(index, carry):
            product[:size, :] += sign * dot(lhs[index // 2, :size, :], rhs[index % 2, :size, :])
            return carry

        lax.fori_loop(0, 3, one, 0)

    def careful(self, bound):
        size, product = self.size, self.product
        product[:size, :] = eye(size)
        self.add(self.mat, self.out, -1.0)
        put(self.work, product[:size, :])
        product[:size, :] = self.value[...]
        self.add(self.out, self.work, 1.0)
        self.settle(self.scale_of(bound) * product[:size, :])
        return self.after(bound)

    def settle(self, new):
        self.value[...] = new
        put(self.out, new)

    def check(self):
        residual = eye(self.size) - self.tools.times(self.mat, self.out)
        self.product[: self.size, :] = residual
        put_high(self.work, residual)
        return jnp.sum(residual * residual)

    def step(self):
        self.settle(self.value[...] + dot(self.out[0], self.work[0, : self.size, :]))

    def last_step(self):
        small = self.work[0, : self.size, :]
        put_high(self.work, self.product[: self.size, :] + dot(small, small))
        put(self.out, self.value[...] + dot(self.out[0], self.work[0, : self.size, :]))

    def whole(self):
        def from_start(error):
            lax.while_loop(lambda bound: bound > REACH, self.careful, self.start())
            return self.check()

        def again(carry):
            self.step()
            return carry[0] + 1, self.check()

        lax.while_loop(lambda bound: bound > REACH, self.coarse, self.start())
        put(self.out, self.value[...])
        error = self.check()
        error = lax.cond(error < 1.0, lambda e: e, from_start, error)
        lax.while_loop(lambda c: (c[0] < 60) & (c[1] > SMALL), again, (jnp.int32(0), error))
        self.last_step()

    def fixed(self):
        lax.fori_loop(0, STEPS, lambda _, bound: self.coarse(bound), self.start())
        put(self.out, self.value[...])

        def plain(index, error):
            error = self.check()

            @pl.when(index == 0)
            def _():
                self.step()

            return error

        error = lax.fori_loop(0, 2, plain, jnp.float32(0.0))
        self.last_step()
        return error


def one_norm(matrix):
    return jnp.max(jnp.sum(jnp.abs(matrix), axis=0, keepdims=True))


def spread(row):
    return jnp.broadcast_to(row, (VROWS, row.shape[1]))


def row_of(tile, start):
    return jnp.concatenate([tile[start + i : start + i + 1, :] for i in range(4)], axis=1)


def set_row(tile, start, row):
    for i in range(4):
        tile[start + i : start + i + 1, :] = row[0:1, i * LANES : (i + 1) * LANES]


UPPER = [(i, j) for i in range(4) for j in range(i, 4)]
FULL = [(i, j) for i in range(4) for j in range(4)]
BLOCKS = {0: (0, 0, UPPER), 2: (1, 0, UPPER), 1: (1, 10, FULL)}


def each_block(packed, which):
    part, base, places_of = BLOCKS[which]
    for index, (i, j) in enumerate(places_of):
        value = packed[part][pl.ds((base + index) * LANES, LANES), :]
        yield i * LANES, j * LANES, value
        if places_of is UPPER and i != j:
            yield j * LANES, i * LANES, value.T


def pack(mats, packed, which):
    part, base, places_of = BLOCKS[which]
    for index, (i, j) in enumerate(places_of):
        packed[part][pl.ds((base + index) * LANES, LANES), :] = mats[
            which, pl.ds(i * LANES, LANES), pl.ds(j * LANES, LANES)
        ]


def fill(prior, which, pair):
    if isinstance(prior, tuple):
        for i, j, value in each_block(prior, which):
            put(pair, value, i, j)
    else:
        put(pair, prior[which])


def increase(mats, which, prior):
    if isinstance(prior, tuple):
        for i, j, value in each_block(prior, which):
            rows, columns = pl.ds(i, LANES), pl.ds(j, LANES)
            mats[which, rows, columns] = mats[which, rows, columns] + value
    else:
        mats[which] = mats[which] + prior[which]


def couple(own, own_vec, prior, inverse, tools):
    size = tools.size
    one, two, three, four, five, six = tools.pairs
    put(one, own[2])
    put(one, spread(row_of(own_vec, 4)), size)
    fill(prior, 0, two)
    coupling = tools.times(one, two)
    pulled = coupling[size : size + 1]
    coupling = coupling[:size]
    upper = 2.0 + one_norm(coupling)
    put(four, eye(size) + coupling)
    return Newton(tools, upper, 1.0, inverse, four, five), pulled


def combine_cov(own, prior, inverse, new, tools):
    times = tools.times
    one, two, three, four, five, six = tools.pairs
    fill(prior, 0, two)
    put(four, own[1])
    put(five, times(two, inverse))
    put(six, times(five, four, rows=tools.size))
    new[0] = times(four, six, TN) + own[0]


def combine_rest(own, own_vec, prior, prior_vec, inverse, pulled_row, new, new_vec, tools):
    size, times = tools.size, tools.times
    one, two, three, four, five, six = tools.pairs
    prior_mean, prior_pull = row_of(prior_vec, 0), row_of(prior_vec, 4)
    mean, pull = row_of(own_vec, 0), row_of(own_vec, 4)
    fill(prior, 1, five)
    put(five, spread(prior_mean + pulled_row), size)
    gained = times(five, inverse)
    put(two, gained[:size])
    put(six, gained)
    moved = times(six, four)
    new[1] = moved[:size]
    set_row(new_vec, 0, moved[size : size + 1] + mean)
    put(three, own[2])
    put(five, spread(prior_mean), size)
    pulled = times(five, three)
    put(six, pulled[:size])
    put(six, spread(pull - pulled[size : size + 1]), size)
    informed = times(six, two, NT)
    new[2] = informed[:size]
    increase(new, 2, prior)
    set_row(new_vec, 4, informed[size : size + 1] + prior_pull)


def unpack(slabs, mats, vecs):
    piece = mats.shape[1] // 16
    for y in range(4):
        total = None
        for x in range(4):
            rows = pl.ds((4 * y + x) * piece, piece)
            for index in range(10):
                which = 1 if index < 4 else 0 if index < 7 else 2
                group = index if index < 4 else (y + (index - 4) % 3) % 4
                mats[which, rows, pl.ds(group * LANES, LANES)] = slabs[y, x, pl.ds(index * piece, piece), :]
            tile = slabs[y, x, pl.ds(10 * piece, 8), :]
            total = tile if total is None else total + tile
        vecs[y : y + 1, :] = total[0:1, :]
        vecs[4 + y : 5 + y, :] = total[1:2, :]
    mats[1] = mats[1].T
    for which in (0, 2):
        for y in range(4):
            left, right = pl.ds(y * LANES, LANES), pl.ds((y + 3) % 4 * LANES, LANES)
            mats[which, left, right] = mats[which, right, left].T


def first_kernel(own_slabs, prior_slabs, own, own_vec, prior, prior_vec, inverse, pulled, *refs):
    odd = lax.axis_index("tm") % 2 == 1
    unpack(own_slabs, own, own_vec)

    @pl.when(odd)
    def _():
        unpack(prior_slabs, prior, prior_vec)
        newton, row = couple(own, own_vec, prior, inverse, Tools(refs))
        pulled[...] = spread(row)[:8]
        newton.whole()


def repair_kernel(own, own_vec, prior_cov, found, error, inverse, *refs, distance):
    @pl.when((lax.axis_index("tm") // distance) % 2 == 1)
    def _():
        @pl.when(jnp.logical_not(jnp.max(error[...]) < SMALL))
        def _():
            newton, _ = couple(own, own_vec, (prior_cov,), inverse, Tools(refs))
            newton.whole()


def gain_kernel(
    own, own_vec, prior_cov, prior_vec, dynamics, noise, gain, offset, cov_out, mean_out, new, mean_tile, kept, *refs, distance
):
    tools = Tools(refs)
    size, times, thin = tools.size, tools.times, tools.thin
    time_pos, row_pos = lax.axis_index("tm"), lax.axis_index("row")
    present = (time_pos // distance) % 2 == 1
    one, two, three, four, five, six = tools.pairs

    @pl.when(jnp.logical_not(present))
    def _():
        new[0] = own[0]
        mean_tile[...] = own_vec[...]

    prior = (prior_cov,)

    def couple_last():
        newton, row = couple(own, own_vec, prior, three, tools)
        kept[0:1, :] = row
        return newton.upper, jnp.float32(1.0)

    def couple_gain():
        put(two, dynamics[...])
        put(three, new[0])
        put(one, times(two, three))
        put(one, spread(row_of(mean_tile, 0)), size)
        projected = times(one, two, NT)
        put(five, projected[size:], size)
        innovation = projected[:size] + noise[...]
        put(four, innovation)
        upper = one_norm(innovation)
        return upper, upper * 0.004

    def stage(index, carry):
        upper, lower = lax.cond(index == 0, couple_last, couple_gain)
        Newton(tools, upper, lower, three, four, six).whole()

        @pl.when(index == 0)
        def _():
            combine_cov(own, prior, three, new, tools)
            moved = thin(thin(spread(row_of(prior_vec, 0) + kept[0:1, :]), three), four)
            set_row(mean_tile, 0, moved[0:1] + row_of(own_vec, 0))

        return carry

    lax.fori_loop(jnp.where(present, 0, 1), jnp.where(time_pos == 15, 1, 2), stage, 0)
    piece = cov_out.shape[0]
    cov_out[...] = new[0, pl.ds(pl.multiple_of(row_pos * piece, piece), piece), :]
    mean = row_of(mean_tile, 0)
    share(mean_out, mean, row_pos)

    @pl.when(time_pos == 15)
    def _():
        gain[...] = jnp.zeros_like(gain)
        offset[...] = jnp.broadcast_to(mean, offset.shape)

    @pl.when(time_pos < 15)
    def _():
        weights = times(three, one)
        gain[...] = weights
        put(six, weights)
        predicted = five[0, size:, :].astype(F32) + five[1, size:, :].astype(F32)
        offset[...] = mean - thin(predicted, six)[:8]


def share(out, row, row_pos):
    piece = out.shape[1]
    for index in range(16):

        @pl.when(row_pos == index)
        def _():
            out[...] = row[0:1, index * piece : (index + 1) * piece]


def remote(src, dst, send, recv, tm, row):
    return pltpu.make_async_remote_copy(
        src_ref=src, dst_ref=dst, send_sem=send, recv_sem=recv, device_id=(tm, row), device_id_type=MESH
    )


def greet(barrier, tm, row):
    pl.semaphore_signal(barrier, inc=1, device_id=(tm, row), device_id_type=MESH)


def gather_kernel(rows, own, prior, send, recv, far_send, far_recv):
    z, core, y, x = places()
    time_pos, row_pos = lax.axis_index("tm"), lax.axis_index("row")
    piece = (rows.shape[0] - 8) // 3
    keep = (time_pos > 0).astype(F32)
    barrier = pltpu.get_barrier_semaphore()
    across = [y * 4 + (x + k) % 4 for k in (1, 2, 3)]
    along = [((y + k) % 4) * 4 + x for k in (1, 2, 3)]
    for peer in across + along:
        greet(barrier, time_pos, peer)

    @pl.when(core == 1)
    def _():
        greet(barrier, time_pos - 1, row_pos)

    for index in range(4):
        columns = pl.ds(index * LANES, LANES)
        own[y, x, pl.ds(index * piece, piece), :] = rows[pl.ds(0, piece), columns] * keep
    for index in range(3):
        columns = pl.ds(pl.multiple_of((y + index) % 4 * LANES, LANES), LANES)
        own[y, x, pl.ds((4 + index) * piece, piece), :] = rows[pl.ds(piece, piece), columns]
        own[y, x, pl.ds((7 + index) * piece, piece), :] = rows[pl.ds(2 * piece, piece), columns] * keep
    own[y, x, pl.ds(10 * piece, 8), :] = jnp.zeros((8, LANES), F32)
    for index in range(4):

        @pl.when(x == index)
        def _():
            lanes = pl.ds(index * piece, piece)
            own[y, x, pl.ds(10 * piece, 1), lanes] = rows[pl.ds(3 * piece, 1), :piece]
            own[y, x, pl.ds(10 * piece + 1, 1), lanes] = rows[pl.ds(3 * piece + 1, 1), :piece] * keep

    def gather(near, other, slab):
        copies = []

        def send_to(view, slot, peer):
            copy = remote(view, view, send.at[slot], recv.at[slot], time_pos, peer)
            copy.start()
            copies.append(copy)

        for k in (1, 3, 2):
            send_to(slab(0, 0), k - 1, near[k - 1])
        for k in (1, 3, 2):
            send_to(slab(0, 0), 4 * k - 1, other[k - 1])
        for j in (1, 3, 2):
            view = slab(j, 0)
            remote(view, view, send.at[j - 1], recv.at[j - 1], time_pos, near[j - 1]).wait_recv()
            for k in (1, 3, 2):
                send_to(view, 4 * k - 1 + j, other[k - 1])
        return copies

    def arrive(k, other, slab):
        for j in range(4):
            view, slot = slab(j, k), 4 * k - 1 + j
            remote(view, view, send.at[slot], recv.at[slot], time_pos, other[k - 1]).wait_recv()

    @pl.when(core == 0)
    def _():
        def slab(j, k):
            return own.at[(y + 4 - k) % 4, (x + 4 - j) % 4]

        pl.semaphore_wait(barrier, 7)
        copies = gather(across, along, slab)
        for k in (0, 1, 3, 2):
            if k:
                arrive(k, along, slab)
            line = (y + 4 - k) % 4
            copy = remote(own.at[line], prior.at[line], far_send.at[k], far_recv.at[k], time_pos + 1, row_pos)
            copy.start()
            copies.append(copy)
        for copy in copies:
            copy.wait_send()

    @pl.when(core == 1)
    def _():
        def slab(j, k):
            return own.at[(y + 4 - j) % 4, (x + 4 - k) % 4]

        pl.semaphore_wait(barrier, 6)
        copies = gather(along, across, slab)
        for k in (1, 3, 2):
            arrive(k, across, slab)
        for copy in copies:
            copy.wait_send()
        for k in range(4):
            line = (y + 4 - k) % 4
            remote(own.at[line], prior.at[line], far_send.at[k], far_recv.at[k], time_pos, row_pos).wait_recv()


def step_kernel(own, own_vec, *refs, count, distance, parts):
    prior_refs, refs = refs[:count], refs[count:]
    prior_vec, inverse, pulled, new, new_vec = refs[:5]
    got, got_vec, refs = refs[5 : 5 + parts], refs[5 + parts], refs[6 + parts :]
    if parts > 1:
        next_inverse, next_pulled, error, *refs = refs
    packed, refs = refs[:2], refs[2:]
    far_send, far_recv, send, recv, twin_send, twin_recv, vec_send, vec_recv = refs[:8]
    tools = Tools(refs[8:])
    prior = prior_refs[0] if count == 1 else prior_refs
    z, core, y, x = places()
    time_pos, row_pos = lax.axis_index("tm"), lax.axis_index("row")
    reach, relay = distance, distance == 2
    barrier = pltpu.get_barrier_semaphore()
    target = (z // reach) % 2 == 1
    source = ((z // reach) % 2 == 0) & (z % reach == reach - 1) & (core == 1)
    source_pos = ((z // reach) * reach) * 2 - 1
    outer_pos = (1 - core) * y + core * x
    hops = 1 if relay else reach
    onward = target & ((z % reach) < reach - 1) if relay else None
    present = (time_pos // distance) % 2 == 1
    twin = 2 * z + 1 - core

    def view(ref, side, line):
        rows = ref.shape[0] // 8
        return ref.at[pl.ds(pl.multiple_of((side * 4 + line) * rows, 8), rows)]

    def outer_row(k):
        place = (outer_pos + k) % 4
        return (1 - core) * (place * 4 + x) + core * (y * 4 + place)

    @pl.when(target)
    def _():
        if relay:
            greet(barrier, (z % reach == 0) * source_pos + (z % reach != 0) * (time_pos - 2), row_pos)
        else:
            greet(barrier, source_pos, row_pos)
        for k in (1, 2, 3):
            greet(barrier, time_pos, outer_row(k))
        greet(barrier, twin, row_pos)

    @pl.when(present)
    def _():
        combine_cov(own, prior, inverse, new, tools)

    def deliver(part):
        for step in reversed(range(hops)):
            for side in range(2):
                slot = 2 * step + side
                line = y if side == 0 else x
                yield remote(
                    view(packed[part], side, line),
                    view(got[part], side, line),
                    far_send.at[part * 8 + slot],
                    far_recv.at[part],
                    time_pos + 1 + slot,
                    row_pos,
                )

    def deliver_vec():
        for slot in reversed(range(2 * hops)):
            yield remote(new_vec, got_vec, vec_send.at[slot], vec_recv, time_pos + 1 + slot, row_pos)

    @pl.when(source)
    def _():
        pack(new, packed, 0)
        pl.semaphore_wait(barrier, 2 * hops)
        for copy in deliver(0):
            copy.start()

    @pl.when(present)
    def _():
        combine_rest(own, own_vec, prior, prior_vec, inverse, pulled[0:1, :], new, new_vec, tools)

    @pl.when(jnp.logical_not(present))
    def _():
        new[...] = own[...]
        new_vec[...] = own_vec[...]

    @pl.when(source)
    def _():
        for copy in deliver_vec():
            copy.start()
        if parts > 1:
            pack(new, packed, 2)
            pack(new, packed, 1)
            for copy in deliver(1):
                copy.start()
        for part in range(parts):
            for copy in deliver(part):
                copy.wait_send()
        for copy in deliver_vec():
            copy.wait_send()

    def onto(part):
        mine = view(got[part], core, outer_pos)
        return remote(mine, mine, far_send.at[part * 8], far_recv.at[part], time_pos + 2, row_pos)

    @pl.when(target)
    def _():
        if relay:

            @pl.when(onward)
            def _():
                pl.semaphore_wait(barrier, 5)

            @pl.when(jnp.logical_not(onward))
            def _():
                pl.semaphore_wait(barrier, 4)

        else:
            pl.semaphore_wait(barrier, 4)
        copies = []

        def over(k, part):
            mine = view(got[part], core, (outer_pos + 4 - k) % 4)
            slot = k * parts + part
            copy = remote(mine, mine, twin_send.at[slot], twin_recv.at[slot], twin, row_pos)
            copy.start()
            copies.append(copy)

        def pass_vec():
            arrived = remote(got_vec, got_vec, vec_send.at[0], vec_recv, time_pos + 2, row_pos)
            arrived.wait_recv()
            if relay:

                @pl.when(onward)
                def _():
                    arrived.start()

        def enter(part):
            onto(part).wait_recv()
            if relay:

                @pl.when(onward)
                def _():
                    onto(part).start()

            mine = view(got[part], core, outer_pos)
            for k in range(1, 4):
                slot = (k - 1) * parts + part
                copy = remote(mine, mine, send.at[slot], recv.at[slot], time_pos, outer_row(k))
                copy.start()
                copies.append(copy)
            over(0, part)

        def complete(part):
            for k in (1, 3, 2):
                line = view(got[part], core, (outer_pos + 4 - k) % 4)
                slot = (k - 1) * parts + part
                remote(line, line, send.at[slot], recv.at[slot], time_pos, outer_row(k)).wait_recv()
                over(k, part)
            for k in range(4):
                theirs = view(got[part], 1 - core, 0)
                slot = k * parts + part
                remote(theirs, theirs, twin_send.at[slot], twin_recv.at[slot], twin, row_pos).wait_recv()

        enter(0)
        complete(0)
        if parts > 1:
            newton, row = couple(new, new_vec, (got[0],), next_inverse, tools)
            next_pulled[...] = spread(row)[:8]
            enter(1)
            pass_vec()
            error[...] = jnp.zeros_like(error) + newton.fixed()
            complete(1)
        else:
            pass_vec()
        for copy in copies:
            copy.wait_send()
        if relay:

            @pl.when(onward)
            def _():
                remote(got_vec, got_vec, vec_send.at[0], vec_recv, time_pos + 2, row_pos).wait_send()
                for part in range(parts):
                    onto(part).wait_send()


def chain_kernel(gain, offset, smooth, near_gain, near_offset, held, sent, state, *rest):
    refs, (send, recv) = rest[:-2], rest[-2:]
    product, one, two = refs
    z, core, _, _ = places()
    time_pos, row_pos = lax.axis_index("tm"), lax.axis_index("row")
    size = gain.shape[0]
    barrier = pltpu.get_barrier_semaphore()
    first, last = core == 0, z == 7

    @pl.when(first)
    def _():
        greet(barrier, time_pos + 1, row_pos)

    @pl.when(jnp.logical_not(last))
    def _():
        greet(barrier, 2 * z + 2, row_pos)

    put(two, gain[...])
    link = remote(gain, near_gain, send.at[0], recv.at[0], 2 * z, row_pos)
    small = remote(offset, near_offset, send.at[1], recv.at[1], 2 * z, row_pos)

    def apply(row8):
        high = row8.astype(BF16).astype(F32)
        both = jnp.concatenate([high, row8 - high], axis=0).astype(BF16)
        result = dot(both, two[0])
        return result[:8] + result[8:] + dot(both, two[1])[:8]

    @pl.when(core == 1)
    def _():
        pl.semaphore_wait(barrier, 1)
        small.start()

        @pl.when(jnp.logical_not(last))
        def _():
            link.start()

        state[...] = offset[...]

    @pl.when(first & (z > 0))
    def _():
        pl.semaphore_wait(barrier, 2)

    @pl.when(first & last)
    def _():
        small.wait_recv()
        state[...] = apply(near_offset[...]) + offset[...]

    @pl.when(first & jnp.logical_not(last))
    def _():
        small.wait_recv()
        state[...] = apply(near_offset[...]) + offset[...]
        link.wait_recv()
        put(one, near_gain[...])

        def part(index, carry):
            columns = pl.ds(pl.multiple_of(index * 256, 256), 256)
            high, low = two[0, :, columns], two[1, :, columns]
            product[:, columns] = dot(one[0], high) + dot(one[0], low) + dot(one[1], high)
            return carry

        lax.fori_loop(0, size // 256, part, 0)
        put(two, product[...])

    @pl.when(jnp.logical_not(last))
    def _():
        remote(held, held, send.at[2], recv.at[2], time_pos, row_pos).wait_recv()
        state[...] = state[...] + apply(held[...])

    @pl.when(first & (z > 0))
    def _():
        sent[...] = state[...]
        copies = [remote(sent, held, send.at[2 + k], recv.at[2], 2 * z - 2 + k, row_pos) for k in range(2)]
        for copy in copies:
            copy.start()
        for copy in copies:
            copy.wait_send()

    share(smooth, state[0:1, :], row_pos)

    @pl.when(core == 1)
    def _():
        small.wait_send()

        @pl.when(jnp.logical_not(last))
        def _():
            link.wait_send()


def body(trans, mean, cov, info, pull, dynamics, noise):
    piece, size = trans.shape[1:]
    shape = jax.ShapeDtypeStruct
    vmem = pl.BlockSpec(memory_space=pltpu.VMEM)
    dma = pltpu.SemaphoreType.DMA

    def params(mib, **more):
        return pltpu.CompilerParams(vmem_limit_bytes=mib * MIB, **more)

    slab = shape((4, 4, 10 * piece + 8, LANES), F32)
    mats_shape, vecs_shape = shape((3, size, size), F32), shape((8, LANES), F32)
    pair_shape, row_shape = shape((2, size, size), BF16), shape((8, size), F32)
    part_shapes = shape((10 * LANES, LANES), F32), shape((26 * LANES, LANES), F32)
    lines = jnp.pad(jnp.concatenate([mean, pull]), ((0, 6), (0, size - piece)))
    own_slabs, prior_slabs = pl.pallas_call(
        gather_kernel,
        out_shape=(slab, slab),
        in_specs=[vmem],
        out_specs=(vmem, vmem),
        scratch_shapes=[dma((15,)), dma((15,)), dma((4,)), dma((4,))],
        compiler_params=params(12, collective_id=0, has_side_effects=True),
    )(jnp.concatenate([trans[0], cov[0], info[0], lines]))

    mats, vecs, got, got_vec, inverse, pulled = pl.pallas_call(
        first_kernel,
        out_shape=(mats_shape, vecs_shape, mats_shape, vecs_shape, pair_shape, row_shape),
        in_specs=[vmem] * 2,
        out_specs=(vmem,) * 6,
        scratch_shapes=scratch_tools(size),
        compiler_params=params(28),
    )(own_slabs, prior_slabs)
    got = [got]

    for distance in (1, 2, 4):
        parts = 2 if distance < 4 else 1
        hops = 1 if distance < 4 else 4
        more = (pair_shape, row_shape, vecs_shape) if parts > 1 else ()
        mats, vecs, *rest = pl.pallas_call(
            functools.partial(step_kernel, count=len(got), distance=distance, parts=parts),
            out_shape=(mats_shape, vecs_shape, *part_shapes[:parts], vecs_shape, *more),
            in_specs=[vmem] * (5 + len(got)),
            out_specs=(vmem,) * (3 + parts + len(more)),
            scratch_shapes=[pltpu.VMEM(part.shape, F32) for part in part_shapes]
            + [dma((8 * parts,)), dma((parts,))]
            + [dma((3 * parts,))] * 2
            + [dma((4 * parts,))] * 2
            + [dma((2 * hops,)), dma]
            + scratch_tools(size),
            compiler_params=params(28, collective_id=1 + distance, has_side_effects=True),
        )(mats, vecs, *got, got_vec, inverse, pulled)
        got, got_vec = rest[:parts], rest[parts]
        if parts > 1:
            found, pulled, error = rest[parts + 1 :]
            inverse = pl.pallas_call(
                functools.partial(repair_kernel, distance=2 * distance),
                out_shape=pair_shape,
                in_specs=[vmem] * 5,
                out_specs=vmem,
                scratch_shapes=scratch_tools(size),
                input_output_aliases={3: 0},
                compiler_params=params(28),
            )(mats, vecs, got[0], found, error)

    gain, offset, cov_out, mean_out = pl.pallas_call(
        functools.partial(gain_kernel, distance=8),
        out_shape=(
            shape((size, size), F32),
            shape((8, size), F32),
            shape((piece, size), F32),
            shape((1, piece), F32),
        ),
        in_specs=[vmem] * 6,
        out_specs=(vmem,) * 4,
        scratch_shapes=[pltpu.VMEM((1, size, size), F32), pltpu.VMEM((8, LANES), F32), pltpu.VMEM((8, size), F32)]
        + scratch_tools(size),
        compiler_params=params(28),
    )(mats, vecs, *got, got_vec, dynamics[0], noise[0])

    smooth = pl.pallas_call(
        chain_kernel,
        out_shape=shape((1, piece), F32),
        in_specs=[vmem] * 2,
        out_specs=vmem,
        scratch_shapes=[
            pltpu.VMEM((size, size), F32),
            pltpu.VMEM((8, size), F32),
            pltpu.VMEM((8, size), F32),
            pltpu.VMEM((8, size), F32),
            pltpu.VMEM((8, size), F32),
            pltpu.VMEM((size, size), F32),
            pltpu.VMEM((2, size, size), BF16),
            pltpu.VMEM((2, size, size), BF16),
            dma((4,)),
            dma((3,)),
        ],
        compiler_params=params(12, collective_id=1, has_side_effects=True),
    )(gain, offset)

    return smooth, mean_out, cov_out[None]


def solution(mesh):
    in_specs = (
        P("tm", "row", None),
        P("tm", "row"),
        P("tm", "row", None),
        P("tm", "row", None),
        P("tm", "row"),
        P("tm", None, None),
        P("tm", None, None),
    )
    out_specs = (P("tm", "row"), P("tm", "row"), P("tm", "row", None))
    return jax.shard_map(body, mesh=mesh, in_specs=in_specs, out_specs=out_specs, check_vma=False)
```

```python
import functools

import jax
import jax.numpy as jnp
from jax import lax
from jax.experimental import pallas as pl
from jax.experimental.pallas import tpu as pltpu
from jax.sharding import PartitionSpec as P

MESH = pl.DeviceIdType.MESH
F32, BF16 = jnp.float32, jnp.bfloat16
NN = (((1,), (0,)), ((), ()))
NT = (((1,), (1,)), ((), ()))
TN = (((0,), (0,)), ((), ()))
VROWS = 16
LANES = 128
REACH = 0.008
SMALL = 4e-3
STEPS = 3
MIB = 1024 * 1024


def places():
    time_pos, row_pos = lax.axis_index("tm"), lax.axis_index("row")
    return time_pos // 2, time_pos % 2, row_pos // 4, row_pos % 4


def dot(lhs, rhs, dims=NN):
    return lax.dot_general(lhs, rhs, dims, preferred_element_type=F32)


def put(pair, value, start=0, column=0):
    high = value.astype(BF16)
    rows, columns = pl.ds(start, value.shape[0]), pl.ds(column, value.shape[1])
    pair[0, rows, columns] = high
    pair[1, rows, columns] = (value - high.astype(F32)).astype(BF16)


def put_high(pair, value):
    pair[0, : value.shape[0], :] = value.astype(BF16)


class Tools:
    def __init__(self, refs):
        self.product, self.value, *self.pairs = refs
        self.size = self.value.shape[0]

    def times(self, lhs, rhs, dims=NN, rows=None):
        size = self.size
        rows = lhs.shape[1] if rows is None else rows
        high, low = rhs[0, :size, :], rhs[1, :size, :]
        left = lhs[0, :rows, :]
        return dot(left, high, dims) + dot(left, low, dims) + dot(lhs[1, :rows, :], high, dims)

    def thin(self, lhs, rhs):
        size = self.size
        high = lhs.astype(BF16)
        low = (lhs - high.astype(F32)).astype(BF16)
        return dot(high, rhs[0, :size, :]) + dot(high, rhs[1, :size, :]) + dot(low, rhs[0, :size, :])


def scratch_tools(size):
    tall = size + VROWS
    return [pltpu.VMEM((tall, size), F32), pltpu.VMEM((size, size), F32)] + [
        pltpu.VMEM((2, tall if index in (0, 4, 5) else size, size), BF16) for index in range(6)
    ]


def eye(size):
    rows = lax.broadcasted_iota(jnp.int32, (size, size), 0)
    return (rows == lax.broadcasted_iota(jnp.int32, (size, size), 1)).astype(F32)


class Newton:
    def __init__(self, tools, upper, lower, out, mat, work):
        self.tools, self.size, self.value, self.product = tools, tools.size, tools.value, tools.product
        self.out, self.mat, self.work = out, mat, work
        self.first = 2.0 / (upper + lower)
        self.opening = (upper - lower) / (upper + lower)

    @staticmethod
    def scale_of(bound):
        return 2.0 / (2.0 - bound * bound)

    def after(self, bound):
        return bound * bound * 0.5 * self.scale_of(bound)

    def start(self):
        whole = self.mat[0].astype(F32) + self.mat[1].astype(F32)
        new = (self.scale_of(self.opening) * self.first) * (2.0 * eye(self.size) - self.first * whole)
        self.value[...] = new
        put(self.out, new)
        return self.after(self.opening)

    def coarse(self, bound):
        size, out, work = self.size, self.out, self.work
        put_high(work, eye(size) - dot(self.mat[0], out[0]))
        new = self.scale_of(bound) * (self.value[...] + dot(out[0], work[0, :size, :]))
        self.value[...] = new
        put_high(out, new)
        return self.after(bound)

    def add(self, lhs, rhs, sign):
        size, product = self.size, self.product

        def one(index, carry):
            product[:size, :] += sign * dot(lhs[index // 2, :size, :], rhs[index % 2, :size, :])
            return carry

        lax.fori_loop(0, 3, one, 0)

    def careful(self, bound):
        size, product = self.size, self.product
        product[:size, :] = eye(size)
        self.add(self.mat, self.out, -1.0)
        put(self.work, product[:size, :])
        product[:size, :] = self.value[...]
        self.add(self.out, self.work, 1.0)
        self.settle(self.scale_of(bound) * product[:size, :])
        return self.after(bound)

    def settle(self, new):
        self.value[...] = new
        put(self.out, new)

    def check(self):
        residual = eye(self.size) - self.tools.times(self.mat, self.out)
        self.product[: self.size, :] = residual
        put_high(self.work, residual)
        return jnp.sum(residual * residual)

    def step(self):
        self.settle(self.value[...] + dot(self.out[0], self.work[0, : self.size, :]))

    def last_step(self):
        small = self.work[0, : self.size, :]
        put_high(self.work, self.product[: self.size, :] + dot(small, small))
        put(self.out, self.value[...] + dot(self.out[0], self.work[0, : self.size, :]))

    def whole(self):
        def from_start(error):
            lax.while_loop(lambda bound: bound > REACH, self.careful, self.start())
            return self.check()

        def again(carry):
            self.step()
            return carry[0] + 1, self.check()

        lax.while_loop(lambda bound: bound > REACH, self.coarse, self.start())
        put(self.out, self.value[...])
        error = self.check()
        error = lax.cond(error < 1.0, lambda e: e, from_start, error)
        lax.while_loop(lambda c: (c[0] < 60) & (c[1] > SMALL), again, (jnp.int32(0), error))
        self.last_step()

    def fixed(self):
        lax.fori_loop(0, STEPS, lambda _, bound: self.coarse(bound), self.start())
        put(self.out, self.value[...])

        def plain(index, error):
            error = self.check()

            @pl.when(index == 0)
            def _():
                self.step()

            return error

        error = lax.fori_loop(0, 2, plain, jnp.float32(0.0))
        self.last_step()
        return error


def one_norm(matrix):
    return jnp.max(jnp.sum(jnp.abs(matrix), axis=0, keepdims=True))


def spread(row):
    return jnp.broadcast_to(row, (VROWS, row.shape[1]))


def row_of(tile, start):
    return jnp.concatenate([tile[start + i : start + i + 1, :] for i in range(4)], axis=1)


def set_row(tile, start, row):
    for i in range(4):
        tile[start + i : start + i + 1, :] = row[0:1, i * LANES : (i + 1) * LANES]


UPPER = [(i, j) for i in range(4) for j in range(i, 4)]
FULL = [(i, j) for i in range(4) for j in range(4)]
BLOCKS = {0: (0, 0, UPPER), 2: (1, 0, UPPER), 1: (1, 10, FULL)}


def each_block(packed, which):
    part, base, places_of = BLOCKS[which]
    for index, (i, j) in enumerate(places_of):
        value = packed[part][pl.ds((base + index) * LANES, LANES), :]
        yield i * LANES, j * LANES, value
        if places_of is UPPER and i != j:
            yield j * LANES, i * LANES, value.T


def pack(mats, packed, which):
    part, base, places_of = BLOCKS[which]
    for index, (i, j) in enumerate(places_of):
        packed[part][pl.ds((base + index) * LANES, LANES), :] = mats[
            which, pl.ds(i * LANES, LANES), pl.ds(j * LANES, LANES)
        ]


def fill(prior, which, pair):
    if isinstance(prior, tuple):
        for i, j, value in each_block(prior, which):
            put(pair, value, i, j)
    else:
        put(pair, prior[which])


def increase(mats, which, prior):
    if isinstance(prior, tuple):
        for i, j, value in each_block(prior, which):
            rows, columns = pl.ds(i, LANES), pl.ds(j, LANES)
            mats[which, rows, columns] = mats[which, rows, columns] + value
    else:
        mats[which] = mats[which] + prior[which]


def couple(own, own_vec, prior, inverse, tools):
    size = tools.size
    one, two, three, four, five, six = tools.pairs
    put(one, own[2])
    put(one, spread(row_of(own_vec, 4)), size)
    fill(prior, 0, two)
    coupling = tools.times(one, two)
    pulled = coupling[size : size + 1]
    coupling = coupling[:size]
    upper = 2.0 + one_norm(coupling)
    put(four, eye(size) + coupling)
    return Newton(tools, upper, 1.0, inverse, four, five), pulled


def combine_cov(own, prior, inverse, new, tools):
    times = tools.times
    one, two, three, four, five, six = tools.pairs
    fill(prior, 0, two)
    put(four, own[1])
    put(five, times(two, inverse))
    put(six, times(five, four, rows=tools.size))
    new[0] = times(four, six, TN) + own[0]


def combine_rest(own, own_vec, prior, prior_vec, inverse, pulled_row, new, new_vec, tools):
    size, times = tools.size, tools.times
    one, two, three, four, five, six = tools.pairs
    prior_mean, prior_pull = row_of(prior_vec, 0), row_of(prior_vec, 4)
    mean, pull = row_of(own_vec, 0), row_of(own_vec, 4)
    fill(prior, 1, five)
    put(five, spread(prior_mean + pulled_row), size)
    gained = times(five, inverse)
    put(two, gained[:size])
    put(six, gained)
    moved = times(six, four)
    new[1] = moved[:size]
    set_row(new_vec, 0, moved[size : size + 1] + mean)
    put(three, own[2])
    put(five, spread(prior_mean), size)
    pulled = times(five, three)
    put(six, pulled[:size])
    put(six, spread(pull - pulled[size : size + 1]), size)
    informed = times(six, two, NT)
    new[2] = informed[:size]
    increase(new, 2, prior)
    set_row(new_vec, 4, informed[size : size + 1] + prior_pull)


def unpack(slabs, mats, vecs):
    piece = mats.shape[1] // 16
    for y in range(4):
        total = None
        for x in range(4):
            rows = pl.ds((4 * y + x) * piece, piece)
            for index in range(10):
                which = 1 if index < 4 else 0 if index < 7 else 2
                group = index if index < 4 else (y + (index - 4) % 3) % 4
                mats[which, rows, pl.ds(group * LANES, LANES)] = slabs[y, x, pl.ds(index * piece, piece), :]
            tile = slabs[y, x, pl.ds(10 * piece, 8), :]
            total = tile if total is None else total + tile
        vecs[y : y + 1, :] = total[0:1, :]
        vecs[4 + y : 5 + y, :] = total[1:2, :]
    mats[1] = mats[1].T
    for which in (0, 2):
        for y in range(4):
            left, right = pl.ds(y * LANES, LANES), pl.ds((y + 3) % 4 * LANES, LANES)
            mats[which, left, right] = mats[which, right, left].T


def first_kernel(own_slabs, prior_slabs, own, own_vec, prior, prior_vec, inverse, pulled, *refs):
    odd = lax.axis_index("tm") % 2 == 1
    unpack(own_slabs, own, own_vec)

    @pl.when(odd)
    def _():
        unpack(prior_slabs, prior, prior_vec)
        newton, row = couple(own, own_vec, prior, inverse, Tools(refs))
        pulled[...] = spread(row)[:8]
        newton.whole()


def repair_kernel(own, own_vec, prior_cov, found, error, inverse, *refs, distance):
    @pl.when((lax.axis_index("tm") // distance) % 2 == 1)
    def _():
        @pl.when(jnp.logical_not(jnp.max(error[...]) < SMALL))
        def _():
            newton, _ = couple(own, own_vec, (prior_cov,), inverse, Tools(refs))
            newton.whole()


def gain_kernel(
    own, own_vec, prior_cov, prior_vec, dynamics, noise, gain, offset, cov_out, mean_out, new, mean_tile, *refs, distance
):
    tools = Tools(refs)
    size, times, thin = tools.size, tools.times, tools.thin
    time_pos, row_pos = lax.axis_index("tm"), lax.axis_index("row")
    present = (time_pos // distance) % 2 == 1
    one, two, three, four, five, six = tools.pairs

    @pl.when(present)
    def _():
        prior = (prior_cov,)
        newton, row = couple(own, own_vec, prior, three, tools)
        newton.whole()
        combine_cov(own, prior, three, new, tools)
        moved = thin(thin(spread(row_of(prior_vec, 0) + row), three), four)
        set_row(mean_tile, 0, moved[0:1] + row_of(own_vec, 0))

    @pl.when(jnp.logical_not(present))
    def _():
        new[0] = own[0]
        mean_tile[...] = own_vec[...]

    piece = cov_out.shape[0]
    cov_out[...] = new[0, pl.ds(pl.multiple_of(row_pos * piece, piece), piece), :]
    mean = row_of(mean_tile, 0)
    share(mean_out, mean, row_pos)

    @pl.when(time_pos == 15)
    def _():
        gain[...] = jnp.zeros_like(gain)
        offset[...] = jnp.broadcast_to(mean, offset.shape)

    @pl.when(time_pos < 15)
    def _():
        put(two, dynamics[...])
        put(three, new[0])
        put(one, times(two, three))
        put(one, spread(mean), size)
        projected = times(one, two, NT)
        predicted = projected[size:]
        innovation = projected[:size] + noise[...]
        upper = one_norm(innovation)
        put(four, innovation)
        Newton(tools, upper, upper * 0.004, three, four, two).whole()
        weights = times(three, one)
        gain[...] = weights
        put(six, weights)
        offset[...] = mean - thin(predicted, six)[:8]


def share(out, row, row_pos):
    piece = out.shape[1]
    for index in range(16):

        @pl.when(row_pos == index)
        def _():
            out[...] = row[0:1, index * piece : (index + 1) * piece]


def remote(src, dst, send, recv, tm, row):
    return pltpu.make_async_remote_copy(
        src_ref=src, dst_ref=dst, send_sem=send, recv_sem=recv, device_id=(tm, row), device_id_type=MESH
    )


def greet(barrier, tm, row):
    pl.semaphore_signal(barrier, inc=1, device_id=(tm, row), device_id_type=MESH)


def gather_kernel(rows, own, prior, send, recv, far_send, far_recv):
    z, core, y, x = places()
    time_pos, row_pos = lax.axis_index("tm"), lax.axis_index("row")
    piece = (rows.shape[0] - 8) // 3
    keep = (time_pos > 0).astype(F32)
    barrier = pltpu.get_barrier_semaphore()
    across = [y * 4 + (x + k) % 4 for k in (1, 2, 3)]
    along = [((y + k) % 4) * 4 + x for k in (1, 2, 3)]
    for peer in across + along:
        greet(barrier, time_pos, peer)

    @pl.when(core == 1)
    def _():
        greet(barrier, time_pos - 1, row_pos)

    for index in range(4):
        columns = pl.ds(index * LANES, LANES)
        own[y, x, pl.ds(index * piece, piece), :] = rows[pl.ds(0, piece), columns] * keep
    for index in range(3):
        columns = pl.ds(pl.multiple_of((y + index) % 4 * LANES, LANES), LANES)
        own[y, x, pl.ds((4 + index) * piece, piece), :] = rows[pl.ds(piece, piece), columns]
        own[y, x, pl.ds((7 + index) * piece, piece), :] = rows[pl.ds(2 * piece, piece), columns] * keep
    own[y, x, pl.ds(10 * piece, 8), :] = jnp.zeros((8, LANES), F32)
    for index in range(4):

        @pl.when(x == index)
        def _():
            lanes = pl.ds(index * piece, piece)
            own[y, x, pl.ds(10 * piece, 1), lanes] = rows[pl.ds(3 * piece, 1), :piece]
            own[y, x, pl.ds(10 * piece + 1, 1), lanes] = rows[pl.ds(3 * piece + 1, 1), :piece] * keep

    def gather(near, other, slab):
        copies = []

        def send_to(view, slot, peer):
            copy = remote(view, view, send.at[slot], recv.at[slot], time_pos, peer)
            copy.start()
            copies.append(copy)

        for k in (1, 3, 2):
            send_to(slab(0, 0), k - 1, near[k - 1])
        for k in (1, 3, 2):
            send_to(slab(0, 0), 4 * k - 1, other[k - 1])
        for j in (1, 3, 2):
            view = slab(j, 0)
            remote(view, view, send.at[j - 1], recv.at[j - 1], time_pos, near[j - 1]).wait_recv()
            for k in (1, 3, 2):
                send_to(view, 4 * k - 1 + j, other[k - 1])
        return copies

    def arrive(k, other, slab):
        for j in range(4):
            view, slot = slab(j, k), 4 * k - 1 + j
            remote(view, view, send.at[slot], recv.at[slot], time_pos, other[k - 1]).wait_recv()

    @pl.when(core == 0)
    def _():
        def slab(j, k):
            return own.at[(y + 4 - k) % 4, (x + 4 - j) % 4]

        pl.semaphore_wait(barrier, 7)
        copies = gather(across, along, slab)
        for k in (0, 1, 3, 2):
            if k:
                arrive(k, along, slab)
            line = (y + 4 - k) % 4
            copy = remote(own.at[line], prior.at[line], far_send.at[k], far_recv.at[k], time_pos + 1, row_pos)
            copy.start()
            copies.append(copy)
        for copy in copies:
            copy.wait_send()

    @pl.when(core == 1)
    def _():
        def slab(j, k):
            return own.at[(y + 4 - j) % 4, (x + 4 - k) % 4]

        pl.semaphore_wait(barrier, 6)
        copies = gather(along, across, slab)
        for k in (1, 3, 2):
            arrive(k, across, slab)
        for copy in copies:
            copy.wait_send()
        for k in range(4):
            line = (y + 4 - k) % 4
            remote(own.at[line], prior.at[line], far_send.at[k], far_recv.at[k], time_pos, row_pos).wait_recv()


def step_kernel(own, own_vec, *refs, count, distance, parts):
    prior_refs, refs = refs[:count], refs[count:]
    prior_vec, inverse, pulled, new, new_vec = refs[:5]
    got, got_vec, refs = refs[5 : 5 + parts], refs[5 + parts], refs[6 + parts :]
    if parts > 1:
        next_inverse, next_pulled, error, *refs = refs
    packed, refs = refs[:2], refs[2:]
    far_send, far_recv, send, recv, twin_send, twin_recv, vec_send, vec_recv = refs[:8]
    tools = Tools(refs[8:])
    prior = prior_refs[0] if count == 1 else prior_refs
    z, core, y, x = places()
    time_pos, row_pos = lax.axis_index("tm"), lax.axis_index("row")
    reach, relay = distance, distance == 2
    barrier = pltpu.get_barrier_semaphore()
    target = (z // reach) % 2 == 1
    source = ((z // reach) % 2 == 0) & (z % reach == reach - 1) & (core == 1)
    source_pos = ((z // reach) * reach) * 2 - 1
    outer_pos = (1 - core) * y + core * x
    hops = 1 if relay else reach
    onward = target & ((z % reach) < reach - 1) if relay else None
    present = (time_pos // distance) % 2 == 1
    twin = 2 * z + 1 - core

    def view(ref, side, line):
        rows = ref.shape[0] // 8
        return ref.at[pl.ds(pl.multiple_of((side * 4 + line) * rows, 8), rows)]

    def outer_row(k):
        place = (outer_pos + k) % 4
        return (1 - core) * (place * 4 + x) + core * (y * 4 + place)

    @pl.when(target)
    def _():
        if relay:
            greet(barrier, (z % reach == 0) * source_pos + (z % reach != 0) * (time_pos - 2), row_pos)
        else:
            greet(barrier, source_pos, row_pos)
        for k in (1, 2, 3):
            greet(barrier, time_pos, outer_row(k))
        greet(barrier, twin, row_pos)

    @pl.when(present)
    def _():
        combine_cov(own, prior, inverse, new, tools)

    def deliver(part):
        for step in reversed(range(hops)):
            for side in range(2):
                slot = 2 * step + side
                line = y if side == 0 else x
                yield remote(
                    view(packed[part], side, line),
                    view(got[part], side, line),
                    far_send.at[part * 8 + slot],
                    far_recv.at[part],
                    time_pos + 1 + slot,
                    row_pos,
                )

    def deliver_vec():
        for slot in reversed(range(2 * hops)):
            yield remote(new_vec, got_vec, vec_send.at[slot], vec_recv, time_pos + 1 + slot, row_pos)

    @pl.when(source)
    def _():
        pack(new, packed, 0)
        pl.semaphore_wait(barrier, 2 * hops)
        for copy in deliver(0):
            copy.start()

    @pl.when(present)
    def _():
        combine_rest(own, own_vec, prior, prior_vec, inverse, pulled[0:1, :], new, new_vec, tools)

    @pl.when(jnp.logical_not(present))
    def _():
        new[...] = own[...]
        new_vec[...] = own_vec[...]

    @pl.when(source)
    def _():
        for copy in deliver_vec():
            copy.start()
        if parts > 1:
            pack(new, packed, 2)
            pack(new, packed, 1)
            for copy in deliver(1):
                copy.start()
        for part in range(parts):
            for copy in deliver(part):
                copy.wait_send()
        for copy in deliver_vec():
            copy.wait_send()

    def onto(part):
        mine = view(got[part], core, outer_pos)
        return remote(mine, mine, far_send.at[part * 8], far_recv.at[part], time_pos + 2, row_pos)

    @pl.when(target)
    def _():
        if relay:

            @pl.when(onward)
            def _():
                pl.semaphore_wait(barrier, 5)

            @pl.when(jnp.logical_not(onward))
            def _():
                pl.semaphore_wait(barrier, 4)

        else:
            pl.semaphore_wait(barrier, 4)
        copies = []

        def over(k, part):
            mine = view(got[part], core, (outer_pos + 4 - k) % 4)
            slot = k * parts + part
            copy = remote(mine, mine, twin_send.at[slot], twin_recv.at[slot], twin, row_pos)
            copy.start()
            copies.append(copy)

        def pass_vec():
            arrived = remote(got_vec, got_vec, vec_send.at[0], vec_recv, time_pos + 2, row_pos)
            arrived.wait_recv()
            if relay:

                @pl.when(onward)
                def _():
                    arrived.start()

        def enter(part):
            onto(part).wait_recv()
            if relay:

                @pl.when(onward)
                def _():
                    onto(part).start()

            mine = view(got[part], core, outer_pos)
            for k in range(1, 4):
                slot = (k - 1) * parts + part
                copy = remote(mine, mine, send.at[slot], recv.at[slot], time_pos, outer_row(k))
                copy.start()
                copies.append(copy)
            over(0, part)

        def complete(part):
            for k in (1, 3, 2):
                line = view(got[part], core, (outer_pos + 4 - k) % 4)
                slot = (k - 1) * parts + part
                remote(line, line, send.at[slot], recv.at[slot], time_pos, outer_row(k)).wait_recv()
                over(k, part)
            for k in range(4):
                theirs = view(got[part], 1 - core, 0)
                slot = k * parts + part
                remote(theirs, theirs, twin_send.at[slot], twin_recv.at[slot], twin, row_pos).wait_recv()

        enter(0)
        complete(0)
        if parts > 1:
            newton, row = couple(new, new_vec, (got[0],), next_inverse, tools)
            next_pulled[...] = spread(row)[:8]
            enter(1)
            pass_vec()
            error[...] = jnp.zeros_like(error) + newton.fixed()
            complete(1)
        else:
            pass_vec()
        for copy in copies:
            copy.wait_send()
        if relay:

            @pl.when(onward)
            def _():
                remote(got_vec, got_vec, vec_send.at[0], vec_recv, time_pos + 2, row_pos).wait_send()
                for part in range(parts):
                    onto(part).wait_send()


def chain_kernel(gain, offset, smooth, near_gain, near_offset, held, sent, state, *rest):
    refs, (send, recv) = rest[:-2], rest[-2:]
    product, one, two = refs
    z, core, _, _ = places()
    time_pos, row_pos = lax.axis_index("tm"), lax.axis_index("row")
    size = gain.shape[0]
    barrier = pltpu.get_barrier_semaphore()
    first, last = core == 0, z == 7

    @pl.when(first)
    def _():
        greet(barrier, time_pos + 1, row_pos)

    @pl.when(jnp.logical_not(last))
    def _():
        greet(barrier, 2 * z + 2, row_pos)

    put(two, gain[...])
    link = remote(gain, near_gain, send.at[0], recv.at[0], 2 * z, row_pos)
    small = remote(offset, near_offset, send.at[1], recv.at[1], 2 * z, row_pos)

    def apply(row8):
        high = row8.astype(BF16).astype(F32)
        both = jnp.concatenate([high, row8 - high], axis=0).astype(BF16)
        result = dot(both, two[0])
        return result[:8] + result[8:] + dot(both, two[1])[:8]

    @pl.when(core == 1)
    def _():
        pl.semaphore_wait(barrier, 1)
        small.start()

        @pl.when(jnp.logical_not(last))
        def _():
            link.start()

        state[...] = offset[...]

    @pl.when(first & (z > 0))
    def _():
        pl.semaphore_wait(barrier, 2)

    @pl.when(first & last)
    def _():
        small.wait_recv()
        state[...] = apply(near_offset[...]) + offset[...]

    @pl.when(first & jnp.logical_not(last))
    def _():
        small.wait_recv()
        state[...] = apply(near_offset[...]) + offset[...]
        link.wait_recv()
        put(one, near_gain[...])

        def part(index, carry):
            columns = pl.ds(pl.multiple_of(index * 256, 256), 256)
            high, low = two[0, :, columns], two[1, :, columns]
            product[:, columns] = dot(one[0], high) + dot(one[0], low) + dot(one[1], high)
            return carry

        lax.fori_loop(0, size // 256, part, 0)
        put(two, product[...])

    @pl.when(jnp.logical_not(last))
    def _():
        remote(held, held, send.at[2], recv.at[2], time_pos, row_pos).wait_recv()
        state[...] = state[...] + apply(held[...])

    @pl.when(first & (z > 0))
    def _():
        sent[...] = state[...]
        copies = [remote(sent, held, send.at[2 + k], recv.at[2], 2 * z - 2 + k, row_pos) for k in range(2)]
        for copy in copies:
            copy.start()
        for copy in copies:
            copy.wait_send()

    share(smooth, state[0:1, :], row_pos)

    @pl.when(core == 1)
    def _():
        small.wait_send()

        @pl.when(jnp.logical_not(last))
        def _():
            link.wait_send()


def body(trans, mean, cov, info, pull, dynamics, noise):
    piece, size = trans.shape[1:]
    shape = jax.ShapeDtypeStruct
    vmem = pl.BlockSpec(memory_space=pltpu.VMEM)
    dma = pltpu.SemaphoreType.DMA

    def params(mib, **more):
        return pltpu.CompilerParams(vmem_limit_bytes=mib * MIB, **more)

    slab = shape((4, 4, 10 * piece + 8, LANES), F32)
    mats_shape, vecs_shape = shape((3, size, size), F32), shape((8, LANES), F32)
    pair_shape, row_shape = shape((2, size, size), BF16), shape((8, size), F32)
    part_shapes = shape((10 * LANES, LANES), F32), shape((26 * LANES, LANES), F32)
    lines = jnp.pad(jnp.concatenate([mean, pull]), ((0, 6), (0, size - piece)))
    own_slabs, prior_slabs = pl.pallas_call(
        gather_kernel,
        out_shape=(slab, slab),
        in_specs=[vmem],
        out_specs=(vmem, vmem),
        scratch_shapes=[dma((15,)), dma((15,)), dma((4,)), dma((4,))],
        compiler_params=params(12, collective_id=0, has_side_effects=True),
    )(jnp.concatenate([trans[0], cov[0], info[0], lines]))

    mats, vecs, got, got_vec, inverse, pulled = pl.pallas_call(
        first_kernel,
        out_shape=(mats_shape, vecs_shape, mats_shape, vecs_shape, pair_shape, row_shape),
        in_specs=[vmem] * 2,
        out_specs=(vmem,) * 6,
        scratch_shapes=scratch_tools(size),
        compiler_params=params(28),
    )(own_slabs, prior_slabs)
    got = [got]

    for distance in (1, 2, 4):
        parts = 2 if distance < 4 else 1
        hops = 1 if distance < 4 else 4
        more = (pair_shape, row_shape, vecs_shape) if parts > 1 else ()
        mats, vecs, *rest = pl.pallas_call(
            functools.partial(step_kernel, count=len(got), distance=distance, parts=parts),
            out_shape=(mats_shape, vecs_shape, *part_shapes[:parts], vecs_shape, *more),
            in_specs=[vmem] * (5 + len(got)),
            out_specs=(vmem,) * (3 + parts + len(more)),
            scratch_shapes=[pltpu.VMEM(part.shape, F32) for part in part_shapes]
            + [dma((8 * parts,)), dma((parts,))]
            + [dma((3 * parts,))] * 2
            + [dma((4 * parts,))] * 2
            + [dma((2 * hops,)), dma]
            + scratch_tools(size),
            compiler_params=params(28, collective_id=1 + distance, has_side_effects=True),
        )(mats, vecs, *got, got_vec, inverse, pulled)
        got, got_vec = rest[:parts], rest[parts]
        if parts > 1:
            found, pulled, error = rest[parts + 1 :]
            inverse = pl.pallas_call(
                functools.partial(repair_kernel, distance=2 * distance),
                out_shape=pair_shape,
                in_specs=[vmem] * 5,
                out_specs=vmem,
                scratch_shapes=scratch_tools(size),
                input_output_aliases={3: 0},
                compiler_params=params(28),
            )(mats, vecs, got[0], found, error)

    gain, offset, cov_out, mean_out = pl.pallas_call(
        functools.partial(gain_kernel, distance=8),
        out_shape=(
            shape((size, size), F32),
            shape((8, size), F32),
            shape((piece, size), F32),
            shape((1, piece), F32),
        ),
        in_specs=[vmem] * 6,
        out_specs=(vmem,) * 4,
        scratch_shapes=[pltpu.VMEM((1, size, size), F32), pltpu.VMEM((8, LANES), F32)] + scratch_tools(size),
        compiler_params=params(28),
    )(mats, vecs, *got, got_vec, dynamics[0], noise[0])

    smooth = pl.pallas_call(
        chain_kernel,
        out_shape=shape((1, piece), F32),
        in_specs=[vmem] * 2,
        out_specs=vmem,
        scratch_shapes=[
            pltpu.VMEM((size, size), F32),
            pltpu.VMEM((8, size), F32),
            pltpu.VMEM((8, size), F32),
            pltpu.VMEM((8, size), F32),
            pltpu.VMEM((8, size), F32),
            pltpu.VMEM((size, size), F32),
            pltpu.VMEM((2, size, size), BF16),
            pltpu.VMEM((2, size, size), BF16),
            dma((4,)),
            dma((3,)),
        ],
        compiler_params=params(12, collective_id=1, has_side_effects=True),
    )(gain, offset)

    return smooth, mean_out, cov_out[None]


def solution(mesh):
    in_specs = (
        P("tm", "row", None),
        P("tm", "row"),
        P("tm", "row", None),
        P("tm", "row", None),
        P("tm", "row"),
        P("tm", None, None),
        P("tm", None, None),
    )
    out_specs = (P("tm", "row"), P("tm", "row"), P("tm", "row", None))
    return jax.shard_map(body, mesh=mesh, in_specs=in_specs, out_specs=out_specs, check_vma=False)
```
